128 devices in a mesh: dp: 4 (over y), group: 8 (over x, core), node: 4 (over z).
Axes of the slice: x: 4, y: 4, z: 4, core: 2. Of those that a mesh axis runs over, the one named last changes fastest.
Arguments:
- tokens: bfloat16 [32768, 1024], P(('dp', 'group', 'node')), may hold values from -24 to 24
- w_qkv: bfloat16 [1024, 3072], replicated, may hold values from -0.1875 to 0.1875
- w_proj: bfloat16 [1024, 1024], replicated, may hold values from -0.1875 to 0.1875
- rel_bias: float32 [32, 225], replicated, may hold values from -135 to 135
- gain_attn: float32 [1024], replicated, may hold values from 0.5 to 1.5
- shift_attn: float32 [1024], replicated, may hold values from -1.75 to 1.75
- w_router: float32 [1024, 32], replicated, may hold values from -0.1875 to 0.1875
- gain_moe: float32 [1024], replicated, may hold values from 0.5 to 1.5
- shift_moe: float32 [1024], replicated, may hold values from -1.75 to 1.75
- w_in: bfloat16 [32, 1024, 2048], P(('group', 'node')), may hold values from -0.1875 to 0.1875
- w_out: bfloat16 [32, 2048, 1024], P(('group', 'node')), may hold values from -0.125 to 0.125
- expert_ids: int32 [32768, 2], P(('dp', 'group', 'node')), may hold values from 0 to 31, all different within a row; in each aligned block of 256 rows (0 to 255, 256 to 511, ...) at most 20 rows name the same one
- cotangent: bfloat16 [32768, 1024], P(('dp', 'group', 'node')), may hold values from -6 to 6
Outputs:
- block_out: bfloat16 [32768, 1024], P(('dp', 'group', 'node'))
- d_tokens: bfloat16 [32768, 1024], P(('dp', 'group', 'node'))
- d_w_qkv: bfloat16 [1024, 3072], P(('dp', 'group', 'node'))
- d_w_proj: bfloat16 [1024, 1024], P(('dp', 'group', 'node'))
- d_router: float32 [1024, 32], P(('dp', 'group', 'node'))
- d_w_in: bfloat16 [32, 1024, 2048], P(('group', 'node'), 'dp')
- d_w_out: bfloat16 [32, 2048, 1024], P(('group', 'node'), 'dp')
The draws below stay inside these ranges and needn't reach their ends.
Inputs may be any that keep to these rules, and one draw needn't show every extreme that they name: `expert_ids`: within the 256 rows of one device no expert is named by more than 20 rows.
All inputs are finite; a program needn't handle non-finite values.
Results may differ from the reference program's by a relative error of at most 0.02.
Values may be sent and summed in bfloat16 or wider, within the bound.
A program may use at most 192 MiB of HBM per device.

```python
import math
import jax
import jax.numpy as jnp
import numpy as np
from jax import lax

D = 1024
FF = 2048
HEADS = 32
HEAD_DIM = 32
GRID = 16
WIN = 8
TOP = 2
SHIFT = 4
TOK_DEV = 256
TOKENS = 32768
EXPERTS = 32
CAP = 20
N_DP = 4
N_GROUP = 8
N_NODE = 4


def draw_rel_bias(key, part):
    key = jax.random.fold_in(key, 7)
    base_key = jax.random.fold_in(key, 0)
    base = jax.random.normal(base_key, (HEADS, (2 * WIN - 1) * (2 * WIN - 1)), jnp.float32)
    return jnp.clip(base, -4.0, 4.0)


def raised(drawn, own_key, source, target, blocks, factor):
    def block_of(dim):
        return (jnp.arange(drawn.shape[dim]) // (drawn.shape[dim] // blocks)).reshape((-1,) + (1,) * (drawn.ndim - 1 - dim))

    one_side = jax.random.permutation(own_key, blocks)[block_of(target)]
    other_side = (block_of(target) + blocks // 2) % blocks
    return jnp.where((block_of(source) == one_side) | (block_of(source) == other_side), factor * drawn, drawn)


def steps_of(rng, extent, cuts, smallest, high):
    factor_of = 1.0
    for axis_at, parts in cuts:
        heights = jax.random.uniform(jax.random.fold_in(jax.random.fold_in(rng, 6), axis_at), (parts,), jnp.float32, smallest / len(cuts), high / len(cuts))
        factor_of = factor_of * jnp.repeat(jnp.exp(heights), extent[axis_at] // parts).reshape((-1,) + (1,) * (len(extent) - 1 - axis_at))
    return factor_of


def shared_out(own_key, own, number, rows, count, top, bound, slope):
    ranking = jax.random.permutation(own_key, count)
    crowded, common = load_shares(count, rows * top, bound, slope, True), load_shares(count, rows * top, bound, slope, False)
    places = jnp.arange(count)

    def named(sizes, offset_by):
        used = int((sizes > 0).sum())
        fixed = max(1, used // 4)
        moved = fixed + (places - fixed + offset_by * (used - fixed)) % max(1, count - fixed)
        return jnp.zeros((count,), jnp.int32).at[ranking[jnp.where(places < fixed, places, moved)]].set(jnp.asarray(sizes, jnp.int32))

    sizes = jnp.where(number % 4 == 0, named(crowded, number // 4), named(common, number - number // 4 - 1))
    mixed = jax.random.permutation(jax.random.fold_in(own, 3), count)
    donor, receiver = mixed[0:count // 2 * 2:2], mixed[1:count // 2 * 2:2]
    room = jnp.minimum(sizes[donor] - 1, bound - sizes[receiver]) // 2
    room = jnp.where((donor == ranking[0]) | (receiver == ranking[0]) | (sizes[receiver] == 0), 0, jnp.maximum(room, 0))
    moved = jax.random.randint(jax.random.fold_in(own, 4), (count // 2,), 0, 1 << 20) % (room + 1)
    sizes = sizes.at[donor].add(-moved).at[receiver].add(moved)
    items = jnp.searchsorted(jnp.cumsum(sizes), jnp.arange(rows * top), side="right").astype(jnp.int32)
    listing = items.reshape(top, rows).T
    listing = listing[jax.random.permutation(jax.random.fold_in(own, 1), rows)]
    offset_by = jax.random.randint(jax.random.fold_in(own, 2), (rows, 1), 0, top)
    return jnp.take_along_axis(listing, (jnp.arange(top)[None, :] + offset_by) % top, axis=1)


def load_shares(amount, total, reach, lean, full):
    weights = [(1 << 20) // math.isqrt(standing ** lean) + 1 for standing in range(1, amount + 1)]
    largest = reach if full else min(reach, max(-(-total // amount), total * weights[0] // sum(weights)))
    least = 1 if total - largest >= amount - 1 else 0
    holding, spare = [largest] + [least] * (amount - 1), total - largest - least * (amount - 1)
    while spare > 0:
        free = [i for i in range(1, amount) if holding[i] < largest] or [i for i in range(1, amount) if holding[i] < reach]
        pool, budget = sum([weights[i] for i in free]), spare
        for i in free:
            extra = min(reach - holding[i], max(1, budget * weights[i] // pool), spare)
            holding[i] = holding[i] + extra
            spare = spare - extra
    return np.array(holding)


def scatter_about(rng, shape, scale, limit, pieces=(), kind=jnp.bfloat16):
    entries = jax.random.normal(rng, shape, jnp.float32) * scale
    if len(pieces) > 0:
        entries = steps_of(rng, shape, pieces, -0.22, 0.18) * entries
    return jnp.clip(entries, min=-limit, max=limit).astype(kind)


def gaussian_with(own_key, extent, spread, most, cuts, heavy, held_as=jnp.bfloat16):
    result = spread * jax.random.normal(own_key, extent, jnp.float32)
    if cuts:
        result = result * steps_of(own_key, extent, cuts, -0.22, 0.18)
    return jnp.clip(raised(result, jax.random.fold_in(own_key, 3), *heavy), -most, most).astype(held_as)


def setup_inputs(seed: int = 0) -> dict:
    keys = jax.random.split(jax.random.key(seed), 14)
    tokens = gaussian_with(keys[0], (TOKENS, D), 1.0, 24.0, ((0, 128),), (0, 1, 128, 5.5))
    w_qkv = scatter_about(keys[1], (D, 3 * D), D ** -0.5, 0.1875)
    w_proj = scatter_about(keys[2], (D, D), D ** -0.5, 0.1875)
    rel_bias = draw_rel_bias(jax.random.fold_in(keys[13], 71), 0)
    gain_attn = jnp.clip(1.0 + 0.1 * jax.random.normal(keys[4], (D,), jnp.float32), 0.5, 1.5)
    shift_attn = scatter_about(keys[5], (D,), 0.3, 1.75, (), jnp.float32)
    w_router = scatter_about(keys[6], (D, EXPERTS), D ** -0.5, 0.1875, (), jnp.float32)
    gain_moe = jnp.clip(1.0 + 0.1 * jax.random.normal(keys[7], (D,), jnp.float32), 0.5, 1.5)
    shift_moe = scatter_about(keys[8], (D,), 0.3, 1.75, (), jnp.float32)
    w_in = scatter_about(keys[9], (EXPERTS, D, FF), D ** -0.5, 0.1875, ((0, 32),))
    w_out = scatter_about(keys[10], (EXPERTS, FF, D), FF ** -0.5, 0.125, ((0, 32),))
    expert_ids_keys = jax.random.split(jax.random.fold_in(keys[11], 1), TOKENS // TOK_DEV)
    expert_ids_turns = jax.random.permutation(jax.random.fold_in(keys[11], 3), TOKENS // TOK_DEV)
    expert_ids = jax.vmap(lambda own, number: shared_out(jax.random.fold_in(keys[11], 2), own, number, TOK_DEV, EXPERTS, TOP, CAP, 2))(expert_ids_keys, expert_ids_turns).reshape((TOKENS, TOP))
    cotangent = scatter_about(keys[12], (TOKENS, D), 1.0, 6.0, ((0, 128),))
    return {"tokens": tokens, "w_qkv": w_qkv, "w_proj": w_proj, "rel_bias": rel_bias, "gain_attn": gain_attn, "shift_attn": shift_attn, "w_router": w_router, "gain_moe": gain_moe, "shift_moe": shift_moe, "w_in": w_in, "w_out": w_out, "expert_ids": expert_ids, "cotangent": cotangent}


EPS = 1e-05
NEG = -1e+30

def rel_index():
    coords = np.arange(WIN * WIN)
    rows_at = coords // WIN
    cols_at = coords % WIN
    return (rows_at[:, None] - rows_at[None, :] + WIN - 1) * (2 * WIN - 1) + (cols_at[:, None] - cols_at[None, :] + WIN - 1)

def region_same():
    labels = np.zeros((GRID, GRID), np.int32)
    bounds = [0, GRID - WIN, GRID - SHIFT, GRID]
    for row_part in range(3):
        for col_part in range(3):
            labels[bounds[row_part]:bounds[row_part + 1], bounds[col_part]:bounds[col_part + 1]] = 3 * row_part + col_part
    per_side = GRID // WIN
    tiled = labels.reshape(per_side, WIN, per_side, WIN).transpose(0, 2, 1, 3).reshape(per_side * per_side, WIN * WIN)
    return tiled[:, :, None] == tiled[:, None, :]

def to_windows(grid_rows, images):
    channels = grid_rows.shape[-1]
    per_side = GRID // WIN
    shaped = grid_rows.reshape(images, GRID, GRID, channels)
    rolled = jnp.roll(shaped, (-SHIFT, -SHIFT), axis=(1, 2))
    parted = rolled.reshape(images, per_side, WIN, per_side, WIN, channels).transpose(0, 1, 3, 2, 4, 5)
    return parted.reshape(images * per_side * per_side, WIN * WIN, channels)

def from_windows(windowed, images):
    channels = windowed.shape[-1]
    per_side = GRID // WIN
    parted = windowed.reshape(images, per_side, per_side, WIN, WIN, channels).transpose(0, 1, 3, 2, 4, 5)
    rolled = jnp.roll(parted.reshape(images, GRID, GRID, channels), (SHIFT, SHIFT), axis=(1, 2))
    return rolled.reshape(images * GRID * GRID, channels)

def window_core(qkv_rows, rel_bias):
    images = qkv_rows.shape[0] // (GRID * GRID)
    windowed = to_windows(qkv_rows, images).astype(jnp.float32)
    num_windows = windowed.shape[0]
    length = windowed.shape[1]
    queries = windowed[:, :, :D].reshape(num_windows, length, HEADS, HEAD_DIM)
    keys_all = windowed[:, :, D:2 * D].reshape(num_windows, length, HEADS, HEAD_DIM)
    values = windowed[:, :, 2 * D:].reshape(num_windows, length, HEADS, HEAD_DIM)
    bias_table = jnp.take(rel_bias, jnp.asarray(rel_index().reshape(-1), dtype=jnp.int32), axis=1).reshape(HEADS, length, length)
    same_region = jnp.asarray(np.tile(region_same(), (images, 1, 1)))
    scores = jnp.einsum('bqhd,bkhd->bhqk', queries, keys_all) * HEAD_DIM ** (-0.5) + bias_table[None]
    scores = jnp.where(same_region[:, None], scores, NEG)
    row_top = lax.optimization_barrier(jnp.max(scores, axis=-1, keepdims=True))
    weights = jnp.exp(scores - row_top)
    attn_probs = (weights / lax.optimization_barrier(jnp.sum(weights, axis=-1, keepdims=True))).astype(jnp.bfloat16)
    attn_probs = lax.optimization_barrier(attn_probs).astype(jnp.float32)
    context = jnp.einsum('bhqk,bkhd->bqhd', attn_probs, values).astype(jnp.bfloat16)
    return from_windows(context.reshape(num_windows, length, D), images)

def post_norm(values, gain, shift):
    row_mean = lax.optimization_barrier(jnp.mean(values, axis=-1, keepdims=True))
    centered = values - row_mean
    row_var = lax.optimization_barrier(jnp.mean(centered * centered, axis=-1, keepdims=True))
    return centered * lax.rsqrt(row_var + EPS) * gain + shift

def exact_gelu(values):
    return jax.nn.gelu(values, approximate=False)

def slot_positions(ids_dev, experts, capacity):
    flat_ids = ids_dev.reshape(-1)
    one_hot = (flat_ids[:, None] == jnp.arange(experts, dtype=jnp.int32)[None, :]).astype(jnp.int32)
    earlier = jnp.cumsum(one_hot, axis=0) - one_hot
    ranks = lax.optimization_barrier(jnp.sum(earlier * one_hot, axis=1))
    return (flat_ids * capacity + ranks).astype(jnp.int32)

def slot_tables(positions, slots):
    owners = jnp.zeros((slots,), jnp.int32).at[positions].set(jnp.arange(positions.shape[0], dtype=jnp.int32))
    slot_used = jnp.zeros((slots,), jnp.bool_).at[positions].set(True)
    return (owners, slot_used)

def reference(tokens, w_qkv, w_proj, rel_bias, gain_attn, shift_attn, w_router, gain_moe, shift_moe, w_in, w_out, expert_ids, cotangent):
    devices = N_DP * N_GROUP * N_NODE
    tok_dev = tokens.reshape(devices, TOK_DEV, D)
    ids_dev = expert_ids.reshape(devices, TOK_DEV, TOP)
    cot_dev = cotangent.reshape(devices, TOK_DEV, D)
    highest = lax.Precision.HIGHEST

    def attend(rows_in):
        qkv_rows = jnp.dot(rows_in, w_qkv, preferred_element_type=jnp.float32).astype(jnp.bfloat16)
        context, core_pull = jax.vjp(lambda packed: window_core(packed, rel_bias), qkv_rows)
        attn_out = jnp.dot(context, w_proj, preferred_element_type=jnp.float32)
        normed_attn, attn_pull = jax.vjp(lambda values: post_norm(values, gain_attn, shift_attn), attn_out)
        mid_rows = (rows_in.astype(jnp.float32) + normed_attn).astype(jnp.bfloat16)
        return (mid_rows, context, core_pull, attn_pull)

    def route_gates(mid_float, ids_in):
        logits = jnp.dot(mid_float, w_router, precision=highest)
        selection = (ids_in[:, :, None] == jnp.arange(EXPERTS, dtype=jnp.int32)[None, None, :]).astype(jnp.float32)
        chosen = jnp.einsum('te,tke->tk', logits, selection, precision=highest)
        return (jax.nn.sigmoid(chosen), selection)

    def front(pair):
        rows_in, ids_in = pair
        mid_rows = attend(rows_in)[0]
        gating = route_gates(mid_rows.astype(jnp.float32), ids_in)[0]
        positions = slot_positions(ids_in, EXPERTS, CAP)
        owners, slot_used = slot_tables(positions, EXPERTS * CAP)
        outbox = jnp.where(slot_used[:, None], mid_rows[owners // TOP], jnp.zeros((), jnp.bfloat16))
        return (mid_rows, outbox, gating, positions)
    mids, outboxes, gatings, positions_all = lax.map(front, (tok_dev, ids_dev))

    def to_experts(arr):
        return arr.reshape(N_DP, EXPERTS, EXPERTS, CAP, D).transpose(2, 0, 1, 3, 4).reshape(EXPERTS, N_DP * EXPERTS * CAP, D)

    def from_experts(arr):
        return arr.reshape(EXPERTS, N_DP, EXPERTS, CAP, D).transpose(1, 2, 0, 3, 4).reshape(devices, EXPERTS * CAP, D)

    def expert_forward(expert_item):
        rows, w_first, w_second = expert_item
        pre_act = jnp.dot(rows, w_first, preferred_element_type=jnp.float32)
        hidden_b = exact_gelu(pre_act).astype(jnp.bfloat16)
        return jnp.dot(hidden_b, w_second, preferred_element_type=jnp.float32).astype(jnp.bfloat16)
    returned = from_experts(lax.map(expert_forward, (to_experts(outboxes), w_in, w_out)))

    def middle(item_dev):
        mid_rows, returned_rows, gating, positions, cot_in = item_dev
        picked = returned_rows[positions].reshape(TOK_DEV, TOP, D).astype(jnp.float32)
        mixture = lax.optimization_barrier(jnp.sum(gating[:, :, None] * picked, axis=1))
        normed_moe, moe_pull = jax.vjp(lambda values: post_norm(values, gain_moe, shift_moe), mixture)
        block_rows = (mid_rows.astype(jnp.float32) + normed_moe).astype(jnp.bfloat16)
        d_mixture = moe_pull(cot_in.astype(jnp.float32))[0]
        d_gating = jnp.einsum('td,tkd->tk', d_mixture, picked, precision=highest)
        d_picked = (gating[:, :, None] * d_mixture[:, None, :]).astype(jnp.bfloat16).reshape(TOK_DEV * TOP, D)
        owners, slot_used = slot_tables(positions, EXPERTS * CAP)
        d_outbox = jnp.where(slot_used[:, None], d_picked[owners], jnp.zeros((), jnp.bfloat16))
        return (block_rows, d_outbox, d_gating)
    blocks, d_outboxes, d_gatings = lax.map(middle, (mids, returned, gatings, positions_all, cot_dev))

    def expert_backward(expert_item):
        rows, w_first, w_second, d_rows_out = expert_item

        def replica(rows_r, d_out_r):
            pre_act = jnp.dot(rows_r, w_first, preferred_element_type=jnp.float32)
            hidden_f, gelu_pull = jax.vjp(exact_gelu, pre_act)
            hidden_b = hidden_f.astype(jnp.bfloat16)
            d_hidden = jnp.dot(d_out_r, w_second.T, preferred_element_type=jnp.float32)
            d_pre = gelu_pull(d_hidden)[0].astype(jnp.bfloat16)
            grad_second = jnp.dot(hidden_b.T, d_out_r, preferred_element_type=jnp.float32)
            grad_first = jnp.dot(rows_r.T, d_pre, preferred_element_type=jnp.float32)
            d_rows_in = jnp.dot(d_pre, w_first.T, preferred_element_type=jnp.float32).astype(jnp.bfloat16)
            return (d_rows_in, grad_first, grad_second)
        rows_split = rows.reshape(N_DP, EXPERTS * CAP, D)
        d_split = d_rows_out.reshape(N_DP, EXPERTS * CAP, D)
        d_rows_in, grad_first, grad_second = jax.vmap(replica)(rows_split, d_split)
        first_sum = lax.optimization_barrier(jnp.sum(lax.optimization_barrier(grad_first.astype(jnp.bfloat16)).astype(jnp.float32), axis=0))
        second_sum = lax.optimization_barrier(jnp.sum(lax.optimization_barrier(grad_second.astype(jnp.bfloat16)).astype(jnp.float32), axis=0))
        return (d_rows_in.reshape(N_DP * EXPERTS * CAP, D), first_sum.astype(jnp.bfloat16), second_sum.astype(jnp.bfloat16))
    d_rows_all, d_w_in, d_w_out = lax.map(expert_backward, (to_experts(outboxes), w_in, w_out, to_experts(d_outboxes)))
    d_returned = from_experts(d_rows_all)

    def finish(carry, item_dev):
        rows_in, ids_in, cot_in, d_back_rows, d_gating, positions = item_dev
        mid_rows, context, core_pull, attn_pull = attend(rows_in)
        mid_float = mid_rows.astype(jnp.float32)
        gating, selection = route_gates(mid_float, ids_in)
        d_chosen = d_gating * gating * (1.0 - gating)
        d_logits = jnp.einsum('tk,tke->te', d_chosen, selection, precision=highest)
        d_mid = cot_in.astype(jnp.float32) + lax.optimization_barrier(jnp.sum(d_back_rows[positions].reshape(TOK_DEV, TOP, D).astype(jnp.float32), axis=1))
        d_mid = d_mid + jnp.dot(d_logits, w_router.T, precision=highest)
        d_mid_b = d_mid.astype(jnp.bfloat16)
        d_attn_b = attn_pull(d_mid_b.astype(jnp.float32))[0].astype(jnp.bfloat16)
        d_context = jnp.dot(d_attn_b, w_proj.T, preferred_element_type=jnp.float32).astype(jnp.bfloat16)
        d_qkv = core_pull(d_context)[0]
        d_tok = (d_mid_b.astype(jnp.float32) + jnp.dot(d_qkv, w_qkv.T, preferred_element_type=jnp.float32)).astype(jnp.bfloat16)
        sum_qkv = carry[0] + jnp.dot(rows_in.T, d_qkv, preferred_element_type=jnp.float32)
        sum_proj = carry[1] + jnp.dot(context.T, d_attn_b, preferred_element_type=jnp.float32)
        sum_router = carry[2] + jnp.dot(mid_float.T, d_logits, precision=highest)
        return ((sum_qkv, sum_proj, sum_router), d_tok)
    init = (jnp.zeros((D, 3 * D), jnp.float32), jnp.zeros((D, D), jnp.float32), jnp.zeros((D, EXPERTS), jnp.float32))
    sums, d_toks = lax.scan(finish, init, (tok_dev, ids_dev, cot_dev, d_returned, d_gatings, positions_all))
    return (blocks.reshape(TOKENS, D), d_toks.reshape(TOKENS, D), sums[0].astype(jnp.bfloat16), sums[1].astype(jnp.bfloat16), sums[2], d_w_in, d_w_out)
```

```python
import jax
import jax.numpy as jnp
import numpy as np
from jax import lax
from jax.experimental import pallas as pl
from jax.experimental.pallas import tpu as pltpu
from jax.sharding import PartitionSpec as P

MESH = pl.DeviceIdType.MESH
F32 = jnp.float32
BF16 = jnp.bfloat16
MIB = 1 << 20
WIDTH = 2176
COLS_X = 1152

D = 1024
HEADS = 32
HEAD_DIM = 32
GRID = 16
WIN = 8
TOP = 2
SHIFT = 4


EPS = 1e-05
NEG = -1e30


def rel_index():
    coords = np.arange(WIN * WIN)
    rows_at = coords // WIN
    cols_at = coords % WIN
    return (rows_at[:, None] - rows_at[None, :] + WIN - 1) * (2 * WIN - 1) + (
        cols_at[:, None] - cols_at[None, :] + WIN - 1
    )


def region_same():
    labels = np.zeros((GRID, GRID), np.int32)
    bounds = [0, GRID - WIN, GRID - SHIFT, GRID]
    for row_part in range(3):
        for col_part in range(3):
            labels[
                bounds[row_part] : bounds[row_part + 1], bounds[col_part] : bounds[col_part + 1]
            ] = (3 * row_part + col_part)
    per_side = GRID // WIN
    tiled = (
        labels.reshape(per_side, WIN, per_side, WIN)
        .transpose(0, 2, 1, 3)
        .reshape(per_side * per_side, WIN * WIN)
    )
    return tiled[:, :, None] == tiled[:, None, :]


def to_windows(grid_rows, images):
    channels = grid_rows.shape[-1]
    per_side = GRID // WIN
    shaped = grid_rows.reshape(images, GRID, GRID, channels)
    rolled = jnp.roll(shaped, (-SHIFT, -SHIFT), axis=(1, 2))
    parted = rolled.reshape(images, per_side, WIN, per_side, WIN, channels).transpose(
        0, 1, 3, 2, 4, 5
    )
    return parted.reshape(images * per_side * per_side, WIN * WIN, channels)


def from_windows(windowed, images):
    channels = windowed.shape[-1]
    per_side = GRID // WIN
    parted = windowed.reshape(images, per_side, per_side, WIN, WIN, channels).transpose(
        0, 1, 3, 2, 4, 5
    )
    rolled = jnp.roll(parted.reshape(images, GRID, GRID, channels), (SHIFT, SHIFT), axis=(1, 2))
    return rolled.reshape(images * GRID * GRID, channels)


def window_core(qkv_rows, rel_bias):
    images = qkv_rows.shape[0] // (GRID * GRID)
    windowed = to_windows(qkv_rows, images)
    num_windows = windowed.shape[0]
    length = windowed.shape[1]
    queries = windowed[:, :, :D].reshape(num_windows, length, HEADS, HEAD_DIM)
    keys_all = windowed[:, :, D : 2 * D].reshape(num_windows, length, HEADS, HEAD_DIM)
    values = windowed[:, :, 2 * D :].reshape(num_windows, length, HEADS, HEAD_DIM)
    bias_table = jnp.take(
        rel_bias, jnp.asarray(rel_index().reshape(-1), dtype=jnp.int32), axis=1
    ).reshape(HEADS, length, length)
    same_region = jnp.asarray(np.tile(region_same(), (images, 1, 1)))
    scores = (
        jnp.einsum("bqhd,bkhd->bhqk", queries, keys_all, preferred_element_type=jnp.float32)
        * HEAD_DIM ** (-0.5)
        + bias_table[None]
    )
    scores = jnp.where(same_region[:, None], scores, NEG)
    row_top = jnp.max(scores, axis=-1, keepdims=True)
    weights = jnp.exp(scores - row_top)
    attn_probs = (weights / jnp.sum(weights, axis=-1, keepdims=True)).astype(jnp.bfloat16)
    context = jnp.einsum(
        "bhqk,bkhd->bqhd", attn_probs, values, preferred_element_type=jnp.float32
    ).astype(jnp.bfloat16)
    return from_windows(context.reshape(num_windows, length, D), images)


def post_norm(values, gain, shift):
    row_mean = jnp.mean(values, axis=-1, keepdims=True)
    centered = values - row_mean
    row_var = jnp.mean(centered * centered, axis=-1, keepdims=True)
    return centered * lax.rsqrt(row_var + EPS) * gain + shift


def exact_gelu(values):
    return jax.nn.gelu(values, approximate=False)


def slot_positions(ids_dev, experts, capacity):
    flat_ids = ids_dev.reshape(-1)
    one_hot = (flat_ids[:, None] == jnp.arange(experts, dtype=jnp.int32)[None, :]).astype(jnp.int32)
    earlier = jnp.cumsum(one_hot, axis=0) - one_hot
    ranks = jnp.sum(earlier * one_hot, axis=1)
    return flat_ids * capacity + ranks


def slot_tables(positions, slots):
    owners = (
        jnp.zeros((slots,), jnp.int32)
        .at[positions]
        .set(jnp.arange(positions.shape[0], dtype=jnp.int32))
    )
    slot_used = jnp.zeros((slots,), jnp.bool_).at[positions].set(True)
    return (owners, slot_used)


def route(slot_block):
    moved = lax.all_to_all(slot_block, ("group", "node"), split_axis=0, concat_axis=0, tiled=True)
    return moved.reshape(slot_block.shape[0] * slot_block.shape[1], slot_block.shape[2])


def reduce_kernel(
    shared, first, second,
    out_shared, out_first, out_second,
    from_core, core_sum, x_recv, x_sum, z_recv, z_sum, x_recv2, x_sum2, z_recv2, y_recv,
    f_far, f_near, f_pass, f_done, s_far, s_near, s_pass, s_done,
    send_core, recv_core, send_a, recv_a, send_b, recv_b, send_c, recv_c, send_d, recv_d, send_y, recv_y,
    send_dp, recv_dp,
):
    y = lax.axis_index("dp")
    g = lax.axis_index("group")
    z = lax.axis_index("node")
    x = g // 2
    c = g % 2
    in_x = pl.ds(0, COLS_X)
    in_z = pl.ds(COLS_X, WIDTH - COLS_X)

    def at_x(j):
        return {"group": lax.rem(x + j, 4) * 2 + c}

    def at_y(j):
        return {"dp": lax.rem(y + j, 4)}

    def at_z(j):
        return {"node": lax.rem(z + j, 4)}

    other = {"group": x * 2 + (1 - c)}
    barrier = pltpu.get_barrier_semaphore()
    peers = [other] + [at(j) for at in (at_x, at_y, at_z) for j in (1, 2, 3)]
    for peer in peers:
        pl.semaphore_signal(barrier, inc=1, device_id=peer, device_id_type=MESH)
    pl.semaphore_wait(barrier, len(peers))

    def send(src, dst, s_sem, r_sem, peer):
        copy = pltpu.make_async_remote_copy(
            src_ref=src, dst_ref=dst, send_sem=s_sem, recv_sem=r_sem, device_id=peer, device_id_type=MESH
        )
        copy.start()
        return copy

    core_copies = [
        send(shared.at[:, k, 1 - c], from_core.at[:, k], send_core.at[k], recv_core.at[k], other) for k in range(4)
    ]

    right, left, far = lax.rem(y + 1, 4), lax.rem(y + 3, 4), lax.rem(y + 2, 4)
    halves = []
    for at, (grad, far_in, near_in, done_in) in enumerate(
        ((first, f_far, f_near, f_done), (second, s_far, s_near, s_done))
    ):
        half = grad.shape[1] // 2
        rows = (pl.ds(0, half), pl.ds(half, half))
        halves.append(rows)
    dp_sets = ((first, f_far, f_near, f_pass, f_done), (second, s_far, s_near, s_pass, s_done))
    far_copies, near_copies = [], []
    for at, (grad, far_in, near_in, passing, done_in) in enumerate(dp_sets):
        rows = halves[at]
        far_copies.append((
            send(grad.at[far, rows[0]], far_in.at[0], send_dp.at[at, 0, 0], recv_dp.at[at, 0, 0], at_y(1)),
            send(grad.at[far, rows[1]], far_in.at[1], send_dp.at[at, 0, 1], recv_dp.at[at, 0, 1], at_y(3)),
        ))
    for at, (grad, far_in, near_in, passing, done_in) in enumerate(dp_sets):
        rows = halves[at]
        near_copies.append((
            send(grad.at[right, rows[1]], near_in.at[1], send_dp.at[at, 1, 1], recv_dp.at[at, 1, 1], at_y(1)),
            send(grad.at[left, rows[0]], near_in.at[0], send_dp.at[at, 1, 0], recv_dp.at[at, 1, 0], at_y(3)),
        ))

    for k in range(4):
        core_copies[k].wait()

        @pl.loop(0, 16)
        def _(i):
            yy, zz = i // 4, i % 4
            core_sum[yy, k, zz] = (
                shared[yy, k, c, zz].astype(F32) + from_core[yy, k, zz].astype(F32)
            ).astype(BF16)

    a_copies = [
        send(core_sum.at[:, lax.rem(x + j, 4), :, :, in_x], x_recv.at[j - 1], send_a.at[j - 1], recv_a.at[j - 1], at_x(j))
        for j in (1, 2, 3)
    ]
    b_copies = [
        send(core_sum.at[:, :, lax.rem(z + j, 4), :, in_z], z_recv.at[j - 1], send_b.at[j - 1], recv_b.at[j - 1], at_z(j))
        for j in (1, 2, 3)
    ]
    for copy in a_copies:
        copy.wait()

    @pl.loop(0, 16)
    def _(i):
        yy, zz = i // 4, i % 4
        total = core_sum[yy, x, zz, :, in_x].astype(F32)
        for j in range(3):
            total = total + x_recv[j, yy, zz].astype(F32)
        x_sum[yy, zz] = total.astype(BF16)

    c_copies = [
        send(x_sum.at[:, lax.rem(z + j, 4)], x_recv2.at[j - 1], send_c.at[j - 1], recv_c.at[j - 1], at_z(j))
        for j in (1, 2, 3)
    ]
    for copy in b_copies:
        copy.wait()

    @pl.loop(0, 16)
    def _(i):
        yy, xx = i // 4, i % 4
        total = core_sum[yy, xx, z, :, in_z].astype(F32)
        for j in range(3):
            total = total + z_recv[j, yy, xx].astype(F32)
        z_sum[yy, xx] = total.astype(BF16)

    d_copies = [
        send(z_sum.at[:, lax.rem(x + j, 4)], z_recv2.at[j - 1], send_d.at[j - 1], recv_d.at[j - 1], at_x(j))
        for j in (1, 2, 3)
    ]

    pass_copies = []
    for at, (grad, far_in, near_in, passing, done_in) in enumerate(dp_sets):
        rows = halves[at]
        step = 64
        for side, (block, peer) in enumerate(((right, at_y(1)), (left, at_y(3)))):
            far_copies[at][side].wait()
            half = rows[side].size

            @pl.loop(0, half // step)
            def _(i):
                here = pl.ds(pl.multiple_of(i * step, step), step)
                mine = pl.ds(pl.multiple_of(side * half + i * step, step), step)
                passing[side, here] = (grad[block, mine].astype(F32) + far_in[side, here].astype(F32)).astype(BF16)

            pass_copies.append(
                send(passing.at[side], done_in.at[side], send_dp.at[at, 2, side], recv_dp.at[at, 2, side], peer)
            )

    for copy in c_copies + d_copies:
        copy.wait()

    @pl.loop(0, 4)
    def _(yy):
        total = x_sum[yy, z].astype(F32)
        other_total = z_sum[yy, x].astype(F32)
        for j in range(3):
            total = total + x_recv2[j, yy].astype(F32)
            other_total = other_total + z_recv2[j, yy].astype(F32)
        x_sum2[yy, :, in_x] = total.astype(BF16)
        x_sum2[yy, :, in_z] = other_total.astype(BF16)

    y_copies = [
        send(x_sum2.at[lax.rem(y + j, 4)], y_recv.at[j - 1], send_y.at[j - 1], recv_y.at[j - 1], at_y(j))
        for j in (1, 2, 3)
    ]

    for at, (grad, far_in, near_in, passing, done_in) in enumerate(dp_sets):
        out = (out_first, out_second)[at]
        half = halves[at][0].size
        step = 64
        for side in (0, 1):
            near_copies[at][1 - side].wait()
            pass_copies[2 * at + side].wait()

            @pl.loop(0, half // step)
            def _(i):
                here = pl.ds(pl.multiple_of(i * step, step), step)
                mine = pl.ds(pl.multiple_of(side * half + i * step, step), step)
                out[mine] = (
                    grad[y, mine].astype(F32) + near_in[side, here].astype(F32) + done_in[side, here].astype(F32)
                ).astype(BF16)

    for copy in y_copies:
        copy.wait()
    total = x_sum2[y].astype(F32)
    for j in range(3):
        total = total + y_recv[j].astype(F32)
    out_shared[...] = total


def reduce_all(shared, first, second):
    def both(rows, cols):
        return pltpu.VMEM((2, rows, cols), BF16)

    dma = pltpu.SemaphoreType.DMA
    rest = WIDTH - COLS_X
    f_rows, f_cols = first.shape[0] // 8, first.shape[1]
    s_rows, s_cols = second.shape[0] // 8, second.shape[1]
    vmem = pl.BlockSpec(memory_space=pltpu.VMEM)
    return pl.pallas_call(
        reduce_kernel,
        out_shape=(
            jax.ShapeDtypeStruct((16, WIDTH), F32),
            jax.ShapeDtypeStruct((2 * f_rows, f_cols), BF16),
            jax.ShapeDtypeStruct((2 * s_rows, s_cols), BF16),
        ),
        in_specs=[vmem] * 3,
        out_specs=[vmem] * 3,
        scratch_shapes=[
            pltpu.VMEM((4, 4, 4, 16, WIDTH), BF16),
            pltpu.VMEM((4, 4, 4, 16, WIDTH), BF16),
            pltpu.VMEM((3, 4, 4, 16, COLS_X), BF16),
            pltpu.VMEM((4, 4, 16, COLS_X), BF16),
            pltpu.VMEM((3, 4, 4, 16, rest), BF16),
            pltpu.VMEM((4, 4, 16, rest), BF16),
            pltpu.VMEM((3, 4, 16, COLS_X), BF16),
            pltpu.VMEM((4, 16, WIDTH), BF16),
            pltpu.VMEM((3, 4, 16, rest), BF16),
            pltpu.VMEM((3, 16, WIDTH), BF16),
            both(f_rows, f_cols), both(f_rows, f_cols), both(f_rows, f_cols), both(f_rows, f_cols),
            both(s_rows, s_cols), both(s_rows, s_cols), both(s_rows, s_cols), both(s_rows, s_cols),
            dma((4,)), dma((4,)),
            dma((3,)), dma((3,)), dma((3,)), dma((3,)), dma((3,)), dma((3,)), dma((3,)), dma((3,)), dma((3,)), dma((3,)),
            dma((2, 3, 2)), dma((2, 3, 2)),
        ],
        compiler_params=pltpu.CompilerParams(
            collective_id=0, has_side_effects=True, vmem_limit_bytes=58 * MIB
        ),
    )(
        shared.reshape(4, 4, 2, 4, 16, WIDTH),
        first.reshape(4, 2 * f_rows, f_cols),
        second.reshape(4, 2 * s_rows, s_cols),
    )


def fold_shared(grad_qkv, grad_proj, grad_router):
    wide = jnp.concatenate([grad_qkv, grad_proj], axis=1).reshape(128, 8, 4 * D)
    high = grad_router.astype(BF16).astype(F32)
    router = jnp.concatenate([high.reshape(128, 8, 32), (grad_router - high).reshape(128, 8, 32)], axis=1)
    router = jnp.pad(router, ((0, 0), (0, 0), (0, 96)))
    main = jnp.concatenate([wide[:, :, : 2 * D], wide[:, :, 2 * D :]], axis=1)
    return jnp.concatenate([main, router], axis=2).astype(BF16)


def unfold_shared(total):
    wide = jnp.concatenate([total[:8, : 2 * D], total[8:, : 2 * D]], axis=1)
    router = total[:8, 2 * D : 2 * D + 32] + total[8:, 2 * D : 2 * D + 32]
    return wide[:, : 3 * D].astype(BF16), wide[:, 3 * D :].astype(BF16), router


def per_device(
    tokens,
    w_qkv,
    w_proj,
    rel_bias,
    gain_attn,
    shift_attn,
    w_router,
    gain_moe,
    shift_moe,
    w_in,
    w_out,
    expert_ids,
    cotangent,
):
    highest = lax.Precision.HIGHEST
    experts = lax.axis_size("group") * lax.axis_size("node")
    tok_rows = tokens.shape[0]
    model_dim = tokens.shape[1]
    capacity = 5 * tok_rows * TOP // (4 * experts)
    qkv_rows = jnp.dot(tokens, w_qkv, preferred_element_type=jnp.float32).astype(jnp.bfloat16)
    context, core_pull = jax.vjp(lambda packed: window_core(packed, rel_bias), qkv_rows)
    attn_out = jnp.dot(context, w_proj, preferred_element_type=jnp.float32)
    normed_attn, attn_pull = jax.vjp(
        lambda values: post_norm(values, gain_attn, shift_attn), attn_out
    )
    mid_rows = (tokens.astype(jnp.float32) + normed_attn).astype(jnp.bfloat16)
    mid_float = mid_rows.astype(jnp.float32)
    logits = jnp.dot(mid_float, w_router, precision=highest)
    selection = (
        expert_ids[:, :, None] == jnp.arange(experts, dtype=jnp.int32)[None, None, :]
    ).astype(jnp.float32)
    chosen = jnp.einsum("te,tke->tk", logits, selection, precision=highest)
    gating = jax.nn.sigmoid(chosen)
    positions = slot_positions(expert_ids, experts, capacity)
    owners, slot_used = slot_tables(positions, experts * capacity)
    outbox = jnp.where(slot_used[:, None], mid_rows[owners // TOP], jnp.zeros((), jnp.bfloat16))
    inbox = route(outbox.reshape(experts, capacity, model_dim))
    w_first = w_in[0]
    w_second = w_out[0]
    pre_act = jnp.dot(inbox, w_first, preferred_element_type=jnp.float32)
    hidden_f, gelu_pull = jax.vjp(exact_gelu, pre_act)
    hidden_b = hidden_f.astype(jnp.bfloat16)
    expert_rows = jnp.dot(hidden_b, w_second, preferred_element_type=jnp.float32).astype(
        jnp.bfloat16
    )
    returned = route(expert_rows.reshape(experts, capacity, model_dim))
    picked = returned[positions].reshape(tok_rows, TOP, model_dim).astype(jnp.float32)
    mixture = jnp.sum(gating[:, :, None] * picked, axis=1)
    normed_moe, moe_pull = jax.vjp(lambda values: post_norm(values, gain_moe, shift_moe), mixture)
    block_out = (mid_float + normed_moe).astype(jnp.bfloat16)
    d_mixture = moe_pull(cotangent.astype(jnp.float32))[0]
    d_gating = jnp.einsum("td,tkd->tk", d_mixture, picked, precision=highest)
    d_picked = (
        (gating[:, :, None] * d_mixture[:, None, :])
        .astype(jnp.bfloat16)
        .reshape(tok_rows * TOP, model_dim)
    )
    d_outbox = jnp.where(slot_used[:, None], d_picked[owners], jnp.zeros((), jnp.bfloat16))
    d_inbox = route(d_outbox.reshape(experts, capacity, model_dim))
    d_hidden = jnp.dot(d_inbox, w_second.T, preferred_element_type=jnp.float32)
    d_pre = gelu_pull(d_hidden)[0].astype(jnp.bfloat16)
    grad_second = jnp.dot(hidden_b.T, d_inbox, preferred_element_type=jnp.float32)
    grad_first = jnp.dot(inbox.T, d_pre, preferred_element_type=jnp.float32)
    d_rows_in = jnp.dot(d_pre, w_first.T, preferred_element_type=jnp.float32).astype(jnp.bfloat16)
    d_returned = route(d_rows_in.reshape(experts, capacity, model_dim))
    d_chosen = d_gating * gating * (1.0 - gating)
    d_logits = jnp.einsum("tk,tke->te", d_chosen, selection, precision=highest)
    d_mid = cotangent.astype(jnp.float32) + jnp.sum(
        d_returned[positions].reshape(tok_rows, TOP, model_dim).astype(jnp.float32), axis=1
    )
    d_mid = d_mid + jnp.dot(d_logits, w_router.T, precision=highest)
    d_mid_b = d_mid.astype(jnp.bfloat16)
    d_attn_b = attn_pull(d_mid_b.astype(jnp.float32))[0].astype(jnp.bfloat16)
    d_context = jnp.dot(d_attn_b, w_proj.T, preferred_element_type=jnp.float32).astype(jnp.bfloat16)
    d_qkv = core_pull(d_context)[0]
    d_tokens = (
        d_mid_b.astype(jnp.float32) + jnp.dot(d_qkv, w_qkv.T, preferred_element_type=jnp.float32)
    ).astype(jnp.bfloat16)
    grad_qkv = jnp.dot(tokens.T, d_qkv, preferred_element_type=jnp.float32)
    grad_proj = jnp.dot(context.T, d_attn_b, preferred_element_type=jnp.float32)
    grad_router = jnp.dot(mid_float.T, d_logits, precision=highest)
    total, first_sum, second_sum = reduce_all(
        fold_shared(grad_qkv, grad_proj, grad_router), grad_first.astype(BF16), grad_second.astype(BF16)
    )
    sum_qkv, sum_proj, sum_router = unfold_shared(total)
    return (
        block_out,
        d_tokens,
        sum_qkv,
        sum_proj,
        sum_router,
        first_sum[None],
        second_sum[None],
    )


def solution(mesh):
    return jax.shard_map(
        per_device,
        mesh=mesh,
        in_specs=(
            P(("dp", "group", "node"), None),
            P(),
            P(),
            P(),
            P(),
            P(),
            P(),
            P(),
            P(),
            P(("group", "node"), None, None),
            P(("group", "node"), None, None),
            P(("dp", "group", "node"), None),
            P(("dp", "group", "node"), None),
        ),
        out_specs=(
            P(("dp", "group", "node"), None),
            P(("dp", "group", "node"), None),
            P(("dp", "group", "node"), None),
            P(("dp", "group", "node"), None),
            P(("dp", "group", "node"), None),
            P(("group", "node"), "dp", None),
            P(("group", "node"), "dp", None),
        ),
        check_vma=False,
    )
```

```python
import jax
import jax.numpy as jnp
from jax import lax
from jax.experimental import pallas as pl
from jax.experimental.pallas import tpu as pltpu
from jax.sharding import PartitionSpec as P

MESH = pl.DeviceIdType.MESH
F32 = jnp.float32
BF16 = jnp.bfloat16
MIB = 1 << 20
D = 1024
FF = 2048
HEADS = 32
HEAD_DIM = 32
WIN = 8
EXPERTS = 32
ROWS = 256
SLOTS = 20
EPS = 1e-05
NEG = -1e30
SCALE = HEAD_DIM ** (-0.5)
CHUNK = 1280
WIDTH = 2176
COLS_X = 1152
BATCH = 16


def dot(a, b):
    return lax.dot_general(a, b, (((1,), (0,)), ((), ())), preferred_element_type=F32)


def dot_nt(a, b):
    return lax.dot_general(a, b, (((1,), (1,)), ((), ())), preferred_element_type=F32)


def dot_tn(a, b):
    return lax.dot_general(a, b, (((0,), (0,)), ((), ())), preferred_element_type=F32)


def iota(shape, dim):
    return lax.broadcasted_iota(jnp.int32, shape, dim)


def flag(cond):
    return jnp.where(cond, 1.0, 0.0).astype(BF16)


def split3(values):
    high = values.astype(BF16)
    rest = values - high.astype(F32)
    mid = rest.astype(BF16)
    return high, mid, (rest - mid.astype(F32)).astype(BF16)


def token_of(place):
    window, inner = place >> 6, place & 63
    row = (((window >> 1) << 3) + (inner >> 3) + WIN // 2) & 15
    col = (((window & 1) << 3) + (inner & 7) + WIN // 2) & 15
    return (row << 4) + col


def to_windows():
    return flag(iota((ROWS, ROWS), 1) == token_of(iota((ROWS, ROWS), 0)))


def from_windows():
    return flag(iota((ROWS, ROWS), 0) == token_of(iota((ROWS, ROWS), 1)))


def normalise(values):
    mean = jnp.mean(values, axis=-1, keepdims=True)
    centered = values - mean
    rstd = lax.rsqrt(jnp.mean(centered * centered, axis=-1, keepdims=True) + EPS)
    return centered * rstd, rstd


def norm_pull(unit, rstd, slope):
    return rstd * (
        slope - jnp.mean(slope, axis=-1, keepdims=True) - unit * jnp.mean(slope * unit, axis=-1, keepdims=True)
    )


def head_mask():
    return flag((iota((256, 128), 0) >> 6) == (iota((256, 128), 1) >> 5))


def by_head(ref, pair, first, mask):
    parts = []
    for side in (0, 1):
        rows = ref[pair * 128 + side * 64 : pair * 128 + side * 64 + 64, pl.ds(first, 128)]
        parts.append(jnp.concatenate([rows] * 4, axis=0) * mask)
    return jnp.concatenate(parts, axis=1)


def by_window(ref, pair, first, upper):
    rows = ref[pair * 128 : pair * 128 + 128, pl.ds(first, 128)]
    return jnp.concatenate([rows * upper, rows * (1 - upper)], axis=1)


def attend_kernel(
    tokens, w_qkv, w_proj, rel_bias, gain, shift,
    tok_w, qkv, probs, context, attn_out, mid,
    bias,
):
    tok_w[...] = dot(to_windows(), tokens[...]).astype(BF16)
    for at in range(6):
        cols = slice(at * 512, at * 512 + 512)
        qkv[:, cols] = dot(tok_w[...], w_qkv[:, cols]).astype(BF16)

    table = jnp.concatenate(split3(rel_bias[...]), axis=0)
    entry = iota((256, 128), 0)
    query = iota((256, 128), 1) & 63

    @pl.loop(0, 16)
    def _(block):
        for inner in range(4):
            key = block * 4 + inner
            place = ((query >> 3) - (key >> 3) + WIN - 1) * (2 * WIN - 1) + (query & 7) - (key & 7) + WIN - 1
            found = dot(table, flag(entry == place))
            bias[pl.ds(key, HEADS, stride=64), :] = found[:32] + (found[32:64] + found[64:96])

    mask = head_mask()
    key = iota((256, 128), 0) & 63
    lane = iota((256, 128), 1)
    row_differs = ((key >> 5) ^ (lane >> 5)) & 1
    col_differs = ((key ^ lane) >> 2) & 1 & (lane >> 6)
    upper = flag(iota((128, 128), 0) < 64)
    for pair in range(2):
        apart = jnp.where((col_differs | (row_differs if pair else 0)) == 1, NEG, 0.0)
        for group in range(8):
            keys = by_head(qkv, pair, D + group * 128, mask)
            queries = by_window(qkv, pair, group * 128, upper)
            scores = dot_nt(keys, queries) * SCALE + bias[group * 256 : group * 256 + 256, :] + apart
            scores = scores.reshape(4, 64, 128)
            weights = jnp.exp(scores - jnp.max(scores, axis=1, keepdims=True))
            prob = (weights / jnp.sum(weights, axis=1, keepdims=True)).reshape(256, 128).astype(BF16)
            probs[pair, group] = prob
            both = dot_tn(prob, by_head(qkv, pair, 2 * D + group * 128, mask))
            for side in (0, 1):
                context[pair * 128 + side * 64 : pair * 128 + side * 64 + 64, group * 128 : group * 128 + 128] = both[
                    side * 64 : side * 64 + 64, side * 128 : side * 128 + 128
                ].astype(BF16)

    projected = dot(context[...], w_proj[...])
    attn_out[...] = projected
    unit, _ = normalise(projected)
    mid_w = (tok_w[...].astype(F32) + (unit * gain[...] + shift[...])).astype(BF16)
    mid[...] = dot(from_windows(), mid_w).astype(BF16)


def attend(tokens, w_qkv, w_proj, rel_bias, gain, shift):
    vmem = pl.BlockSpec(memory_space=pltpu.VMEM)
    return pl.pallas_call(
        attend_kernel,
        out_shape=(
            jax.ShapeDtypeStruct((ROWS, D), BF16),
            jax.ShapeDtypeStruct((ROWS, 3 * D), BF16),
            jax.ShapeDtypeStruct((2, 8, 256, 128), BF16),
            jax.ShapeDtypeStruct((ROWS, D), BF16),
            jax.ShapeDtypeStruct((ROWS, D), F32),
            jax.ShapeDtypeStruct((ROWS, D), BF16),
        ),
        in_specs=[vmem] * 6,
        out_specs=[vmem] * 6,
        scratch_shapes=[pltpu.VMEM((HEADS * 64, 128), F32)],
        compiler_params=pltpu.CompilerParams(vmem_limit_bytes=48 * MIB),
    )(tokens, w_qkv, w_proj, jnp.pad(rel_bias, ((0, 0), (0, 31))), gain.reshape(1, D), shift.reshape(1, D))


def expert_of_row(shape, dim):
    row = iota(shape, dim)
    return jnp.where(row < EXPERTS * 16, row >> 4, (row >> 2) & (EXPERTS - 1))


def rank_of_row(shape, dim):
    row = iota(shape, dim)
    return jnp.where(row < EXPERTS * 16, row & 15, 16 + (row & 3))


def fold_order(count):
    row, col = iota((16 * count, 16 * count), 0), iota((16 * count, 16 * count), 1)
    size = 4 * count
    block = sum([(row >= size * at).astype(jnp.int32) for at in (1, 2, 3)])
    inner = row - block * size
    return flag(col == ((inner >> 2) << 4) + (block << 2) + (inner & 3))


def unfold(ref, first, count, order, out, out_first):
    main = ref[first : first + count, :, :D].reshape(16 * count, D)
    rest = dot(order, ref[first : first + count, :, D:].reshape(16 * count, CHUNK - D)).astype(BF16)
    out[out_first : out_first + 16 * count, :] = main
    for block in range(4):
        out[out_first + 16 * count : out_first + 20 * count, block * 256 : block * 256 + 256] = rest[
            block * 4 * count : block * 4 * count + 4 * count
        ]


def fold(rows, count, order, ref, first):
    ref[first : first + count, :, :D] = rows[: 16 * count].astype(BF16).reshape(count, 16, D)
    rest = rows[16 * count :].astype(BF16)
    stacked = jnp.concatenate([rest[:, block * 256 : block * 256 + 256] for block in range(4)], axis=0)
    ref[first : first + count, :, D:] = dot_tn(order, stacked).astype(BF16).reshape(count, 16, CHUNK - D)


def gelu_parts(values):
    z = jnp.abs(values) * 0.7071067811865476
    t = 1.0 / (1.0 + 0.3275911 * z)
    bell = jnp.exp(-z * z)
    poly = ((((1.061405429 * t - 1.453152027) * t + 1.421413741) * t - 0.284496736) * t + 0.254829592) * t
    tail = 0.5 * poly * bell
    phi = jnp.where(values >= 0, 1.0 - tail, tail)
    return values * phi, phi + values * bell * 0.3989422804014327


def experts_kernel(
    mid, ids, cotangent, w_router, gain, shift, w_in, w_out,
    block_out, d_mid, d_router, grad_first, grad_second,
    w_first, w_second, out1, in1, out2, in2, out3, in3, out4, in4,
    rows, d_rows, hidden, slope, d_pre, back, select,
    send_sem, recv_sem, load_sem,
):
    g = lax.axis_index("group")
    z = lax.axis_index("node")
    me = g * 4 + z
    load_first = pltpu.make_async_copy(w_in, w_first, load_sem.at[0])
    load_second = pltpu.make_async_copy(w_out, w_second, load_sem.at[1])
    load_first.start()
    load_second.start()

    def peer(e):
        return {"group": e // 4, "node": lax.rem(e, 4)}

    barrier = pltpu.get_barrier_semaphore()

    @pl.loop(1, EXPERTS)
    def _(j):
        pl.semaphore_signal(barrier, inc=1, device_id=peer(lax.rem(me + j, EXPERTS)), device_id_type=MESH)

    def to_expert(route, source, target, j):
        e = lax.rem(me + j, EXPERTS)
        return pltpu.make_async_remote_copy(
            src_ref=source.at[e], dst_ref=target.at[j], send_sem=send_sem.at[route, j], recv_sem=recv_sem.at[route, j],
            device_id=peer(e), device_id_type=MESH,
        )

    def to_source(route, source, target, j):
        return pltpu.make_async_remote_copy(
            src_ref=source.at[j], dst_ref=target.at[me], send_sem=send_sem.at[route, j], recv_sem=recv_sem.at[route, j],
            device_id=peer(lax.rem(me + EXPERTS - j, EXPERTS)), device_id_type=MESH,
        )

    def start_all(make, route, source, target, first, last):
        @pl.loop(max(first, 1), last)
        def _(j):
            make(route, source, target, j).start()

    def receive(make, route, source, target, first, last):
        @pl.loop(max(first, 1), last)
        def _(j):
            make(route, source, target, j).wait_recv()

    expert_lane = iota((ROWS, EXPERTS), 1)
    chosen = [jnp.where(ids[:, k : k + 1] == expert_lane, 1.0, 0.0) for k in range(2)]
    earlier = flag(iota((ROWS, ROWS), 0) > iota((ROWS, ROWS), 1))
    rank = dot(earlier, (chosen[0] + chosen[1]).astype(BF16)) + 1.0
    places = [(one * rank).astype(BF16) for one in chosen]
    row_experts = flag(expert_of_row((EXPERTS * SLOTS, EXPERTS), 0) == iota((EXPERTS * SLOTS, EXPERTS), 1))
    row_ranks = rank_of_row((EXPERTS * SLOTS, ROWS), 0).astype(F32) + 1.0
    for k in range(2):
        select[:, k * ROWS : k * ROWS + ROWS] = flag(dot_nt(row_experts, places[k]) == row_ranks)
    order = fold_order(EXPERTS)
    batch_order = fold_order(BATCH)

    fold(dot(select[:, :ROWS] + select[:, ROWS:], mid[...]), EXPERTS, order, out1, 0)
    pl.semaphore_wait(barrier, EXPERTS - 1)
    start_all(to_expert, 0, out1, in1, 1, EXPERTS)
    in1[0] = out1[me]

    router = split3(w_router[...])
    logits = dot(mid[...], router[0]) + (dot(mid[...], router[1]) + dot(mid[...], router[2]))
    gating = []
    for k in range(2):
        logit = jnp.sum(logits * chosen[k], axis=1, keepdims=True)
        gating.append(1.0 / (1.0 + jnp.exp(-logit)))
    load_first.wait()
    load_second.wait()

    batch_rows = SLOTS * BATCH
    for batch in range(EXPERTS // BATCH):
        first, last = batch * BATCH, batch * BATCH + BATCH
        here = slice(batch * batch_rows, batch * batch_rows + batch_rows)
        receive(to_expert, 0, out1, in1, first, last)
        unfold(in1, first, BATCH, batch_order, rows, batch * batch_rows)
        for at in range(8):
            cols = slice(at * 256, at * 256 + 256)
            value, value_slope = gelu_parts(dot(rows[here, :], w_first[:, cols]))
            hidden[here, cols] = value.astype(BF16)
            slope[here, cols] = value_slope.astype(BF16)
        fold(dot(hidden[here, :], w_second[...]), BATCH, batch_order, out2, first)
        start_all(to_source, 1, out2, in2, first, last)
        if batch == 0:
            in2[me] = out2[0]

    lane_experts = flag(expert_of_row((EXPERTS * SLOTS, EXPERTS), 0) == iota((EXPERTS * SLOTS, EXPERTS), 1))
    lane_ranks = rank_of_row((ROWS, EXPERTS * SLOTS), 1).astype(F32) + 1.0
    picks = [flag(dot_nt(places[k], lane_experts) == lane_ranks) for k in range(2)]
    receive(to_source, 1, out2, in2, 1, EXPERTS)
    unfold(in2, 0, EXPERTS, order, back, 0)
    picked = [dot(picks[k], back[...]) for k in range(2)]
    unit, rstd = normalise(gating[0] * picked[0] + gating[1] * picked[1])
    block_out[...] = (mid[...].astype(F32) + (unit * gain[...] + shift[...])).astype(BF16)
    d_mixture = norm_pull(unit, rstd, cotangent[...].astype(F32) * gain[...])
    d_picked = jnp.concatenate([(gating[k] * d_mixture).astype(BF16) for k in range(2)], axis=0)
    fold(dot(select[...], d_picked), EXPERTS, order, out3, 0)
    start_all(to_expert, 2, out3, in3, 1, EXPERTS)
    in3[0] = out3[me]

    d_logits = jnp.zeros((ROWS, EXPERTS), F32)
    for k in range(2):
        d_gating = jnp.sum(d_mixture * picked[k], axis=1, keepdims=True)
        d_logits = d_logits + chosen[k] * (d_gating * gating[k] * (1.0 - gating[k]))
    d_high = d_logits.astype(BF16)
    d_low = (d_logits - d_high.astype(F32)).astype(BF16)
    d_router[...] = dot_tn(mid[...], d_high) + dot_tn(mid[...], d_low)
    from_router = dot_nt(d_high, router[0]) + (dot_nt(d_low, router[0]) + dot_nt(d_high, router[1]))
    d_direct = cotangent[...].astype(F32) + from_router

    for batch in range(EXPERTS // BATCH):
        first, last = batch * BATCH, batch * BATCH + BATCH
        here = slice(batch * batch_rows, batch * batch_rows + batch_rows)
        receive(to_expert, 2, out3, in3, first, last)
        unfold(in3, first, BATCH, batch_order, d_rows, batch * batch_rows)
        for at in range(8):
            cols = slice(at * 256, at * 256 + 256)
            d_hidden = dot_nt(d_rows[here, :], w_second[cols, :])
            d_pre[here, cols] = (d_hidden * slope[here, cols].astype(F32)).astype(BF16)
        fold(dot_nt(d_pre[here, :], w_first[...]), BATCH, batch_order, out4, first)
        start_all(to_source, 3, out4, in4, first, last)
        if batch == 0:
            in4[me] = out4[0]

    for at in range(8):
        cols = slice(at * 256, at * 256 + 256)
        grad_second[cols, :] = dot(hidden[:, cols].T, d_rows[...]).astype(BF16)
    for at in range(4):
        cols = slice(at * 256, at * 256 + 256)
        grad_first[cols, :] = dot(rows[:, cols].T, d_pre[...]).astype(BF16)

    receive(to_source, 3, out4, in4, 1, EXPERTS)
    unfold(in4, 0, EXPERTS, order, back, 0)
    d_mid[...] = (d_direct + dot(picks[0] + picks[1], back[...])).astype(BF16)

    @pl.loop(1, EXPERTS)
    def _(j):
        to_expert(0, out1, in1, j).wait_send()
        to_source(1, out2, in2, j).wait_send()
        to_expert(2, out3, in3, j).wait_send()
        to_source(3, out4, in4, j).wait_send()


def experts(mid, ids, cotangent, w_router, gain, shift, w_in, w_out):
    vmem = pl.BlockSpec(memory_space=pltpu.VMEM)
    anywhere = pl.BlockSpec(memory_space=pl.ANY)
    box = pltpu.VMEM((EXPERTS, 16, CHUNK), BF16)
    slots = EXPERTS * SLOTS
    return pl.pallas_call(
        experts_kernel,
        out_shape=(
            jax.ShapeDtypeStruct((ROWS, D), BF16),
            jax.ShapeDtypeStruct((ROWS, D), BF16),
            jax.ShapeDtypeStruct((D, EXPERTS), F32),
            jax.ShapeDtypeStruct((D, FF), BF16),
            jax.ShapeDtypeStruct((FF, D), BF16),
        ),
        in_specs=[vmem] * 6 + [anywhere] * 2,
        out_specs=[vmem] * 5,
        scratch_shapes=[
            pltpu.VMEM((D, FF), BF16),
            pltpu.VMEM((FF, D), BF16),
            box, box, box, box, box, box, box, box,
            pltpu.VMEM((slots, D), BF16),
            pltpu.VMEM((slots, D), BF16),
            pltpu.VMEM((slots, FF), BF16),
            pltpu.VMEM((slots, FF), BF16),
            pltpu.VMEM((slots, FF), BF16),
            pltpu.VMEM((slots, D), BF16),
            pltpu.VMEM((slots, 2 * ROWS), BF16),
            pltpu.SemaphoreType.DMA((4, EXPERTS)),
            pltpu.SemaphoreType.DMA((4, EXPERTS)),
            pltpu.SemaphoreType.DMA((2,)),
        ],
        compiler_params=pltpu.CompilerParams(
            collective_id=1, has_side_effects=True, vmem_limit_bytes=60 * MIB
        ),
    )(mid, ids, cotangent, w_router, gain.reshape(1, D), shift.reshape(1, D), w_in, w_out)


def attend_back(d_mid, tok_w, qkv, probs, context, attn_out, w_qkv, w_proj, gain, d_tokens, d_qkv, d_attn, d_context):
    d_mid_w = dot(to_windows(), d_mid[...])
    unit, rstd = normalise(attn_out[...])
    d_attn[...] = norm_pull(unit, rstd, d_mid_w * gain[...]).astype(BF16)
    d_context[...] = dot_nt(d_attn[...], w_proj[...]).astype(BF16)
    mask = head_mask()
    mask_f = mask.astype(F32)
    upper = flag(iota((128, 128), 0) < 64)

    def own_heads(values, side):
        return (values[:, side * 128 : side * 128 + 128] * mask_f).reshape(4, 64, 128).sum(axis=0)

    for pair in range(2):
        for group in range(8):
            first = group * 128
            values = by_head(qkv, pair, 2 * D + first, mask)
            keys = by_head(qkv, pair, D + first, mask)
            queries = by_window(qkv, pair, first, upper)
            d_out = by_window(d_context, pair, first, upper)
            prob = probs[pair, group]
            d_prob = dot_nt(values, d_out)
            prob_f = prob.astype(F32)
            inner = (prob_f * d_prob).reshape(4, 64, 128).sum(axis=1, keepdims=True)
            d_score = prob_f.reshape(4, 64, 128) * (d_prob.reshape(4, 64, 128) - inner) * SCALE
            d_score = d_score.reshape(256, 128).astype(BF16)
            d_value = dot(prob, d_out)
            d_key = dot(d_score, queries)
            d_query = dot_tn(d_score, keys)
            for side in (0, 1):
                rows = slice(pair * 128 + side * 64, pair * 128 + side * 64 + 64)
                d_qkv[rows, first : first + 128] = d_query[
                    side * 64 : side * 64 + 64, side * 128 : side * 128 + 128
                ].astype(BF16)
                d_qkv[rows, D + first : D + first + 128] = own_heads(d_key, side).astype(BF16)
                d_qkv[rows, 2 * D + first : 2 * D + first + 128] = own_heads(d_value, side).astype(BF16)

    d_tok_w = (d_mid_w + dot_nt(d_qkv[...], w_qkv[...])).astype(BF16)
    d_tokens[...] = dot(from_windows(), d_tok_w).astype(BF16)


def finish_kernel(
    d_mid, tok_w, qkv, probs, context, attn_out, w_qkv, w_proj, gain, d_router, first, second,
    d_tokens, out_shared, out_first, out_second,
    d_qkv, d_attn, d_context,
    shared, from_core, x_recv, x_sum, z_recv, z_sum, x_recv2, z_recv2, y_sum, y_recv,
    f_far, f_near, f_pass, f_done, s_far, s_near, s_pass, s_done,
    send_core, recv_core, send_a, recv_a, send_b, recv_b, send_c, recv_c, send_d, recv_d, send_y, recv_y,
    send_dp, recv_dp, load_dp,
):
    y = lax.axis_index("dp")
    g = lax.axis_index("group")
    z = lax.axis_index("node")
    x = g // 2
    c = g % 2
    in_x = pl.ds(0, COLS_X)
    in_z = pl.ds(COLS_X, WIDTH - COLS_X)

    def at_x(j):
        return {"group": lax.rem(x + j, 4) * 2 + c}

    def at_y(j):
        return {"dp": lax.rem(y + j, 4)}

    def at_z(j):
        return {"node": lax.rem(z + j, 4)}

    other = {"group": x * 2 + (1 - c)}
    barrier = pltpu.get_barrier_semaphore()
    peers = [other] + [at(j) for at in (at_x, at_y, at_z) for j in (1, 2, 3)]
    for peer in peers:
        pl.semaphore_signal(barrier, inc=1, device_id=peer, device_id_type=MESH)
    pl.semaphore_wait(barrier, len(peers))

    def send(src, dst, s_sem, r_sem, peer):
        copy = pltpu.make_async_remote_copy(
            src_ref=src, dst_ref=dst, send_sem=s_sem, recv_sem=r_sem, device_id=peer, device_id_type=MESH
        )
        copy.start()
        return copy

    right, left, far = lax.rem(y + 1, 4), lax.rem(y + 3, 4), lax.rem(y + 2, 4)
    dp_sets = ((first, f_far, f_near, f_pass, f_done, out_first), (second, s_far, s_near, s_pass, s_done, out_second))
    halves = [(pl.ds(0, grad.shape[1] // 2), pl.ds(grad.shape[1] // 2, grad.shape[1] // 2)) for grad in (first, second)]
    far_copies, near_copies, loads = [], [], []
    for at, (grad, far_in, near_in, passing, done_in, out) in enumerate(dp_sets):
        rows = halves[at]
        far_copies.append((
            send(grad.at[far, rows[0]], far_in.at[0], send_dp.at[at, 0, 0], recv_dp.at[at, 0, 0], at_y(1)),
            send(grad.at[far, rows[1]], far_in.at[1], send_dp.at[at, 0, 1], recv_dp.at[at, 0, 1], at_y(3)),
        ))
        loads.append((
            pltpu.make_async_copy(grad.at[right, rows[0]], passing.at[0], load_dp.at[at, 0]),
            pltpu.make_async_copy(grad.at[left, rows[1]], passing.at[1], load_dp.at[at, 1]),
            pltpu.make_async_copy(grad.at[y], out, load_dp.at[at, 2]),
        ))
        for copy in loads[at]:
            copy.start()
    for at, (grad, far_in, near_in, passing, done_in, out) in enumerate(dp_sets):
        rows = halves[at]
        near_copies.append((
            send(grad.at[left, rows[0]], near_in.at[0], send_dp.at[at, 1, 0], recv_dp.at[at, 1, 0], at_y(3)),
            send(grad.at[right, rows[1]], near_in.at[1], send_dp.at[at, 1, 1], recv_dp.at[at, 1, 1], at_y(1)),
        ))

    attend_back(d_mid, tok_w, qkv, probs, context, attn_out, w_qkv, w_proj, gain, d_tokens, d_qkv, d_attn, d_context)

    core_copies = []
    for block in range(8):
        rows = slice(block * 128, block * 128 + 128)
        yy, xx = block // 2, block % 2 * 2
        tok_t = tok_w[:, rows].T
        for half in range(2):
            cols = slice(half * 1024, half * 1024 + 1024)
            upper = dot(tok_t, d_qkv[:, cols]).reshape(16, 8, 1024)
            if half == 0:
                lower = dot(tok_t, d_qkv[:, 2 * D : 3 * D])
            else:
                lower = dot(context[:, rows].T, d_attn[...])
            folded = jnp.concatenate([upper, lower.reshape(16, 8, 1024)], axis=1).astype(BF16)
            shared[yy, xx : xx + 2, :, :, :, cols] = folded.reshape(2, 2, 4, 16, 1024)
        router = d_router[rows, :]
        high = router.astype(BF16).astype(F32)
        folded = jnp.concatenate([high.reshape(16, 8, 128), (router - high).reshape(16, 8, 128)], axis=1).astype(BF16)
        shared[yy, xx : xx + 2, :, :, :, 2 * D :] = folded.reshape(2, 2, 4, 16, 128)
        core_copies.append(send(
            shared.at[yy, xx : xx + 2, 1 - c], from_core.at[yy, xx : xx + 2], send_core.at[block], recv_core.at[block], other
        ))

    pass_copies = []
    step = 64
    for at, (grad, far_in, near_in, passing, done_in, out) in enumerate(dp_sets):
        half = halves[at][0].size
        for side, peer in enumerate((at_y(1), at_y(3))):
            loads[at][side].wait()
            far_copies[at][side].wait()

            @pl.loop(0, half // step)
            def _(i):
                here = pl.ds(pl.multiple_of(i * step, step), step)
                passing[side, here] = (passing[side, here].astype(F32) + far_in[side, here].astype(F32)).astype(BF16)

            pass_copies.append(
                send(passing.at[side], done_in.at[side], send_dp.at[at, 2, side], recv_dp.at[at, 2, side], peer)
            )

    for block in range(8):
        yy, xx = block // 2, block % 2 * 2
        core_copies[block].wait()

        @pl.loop(0, 8)
        def _(i):
            xi, zi = xx + i // 4, i % 4
            shared[yy, xi, c, zi] = (
                shared[yy, xi, c, zi].astype(F32) + from_core[yy, xi, zi].astype(F32)
            ).astype(BF16)

    a_copies = [
        send(
            shared.at[:, lax.rem(x + j, 4), c, :, :, in_x], x_recv.at[j - 1], send_a.at[j - 1], recv_a.at[j - 1], at_x(j)
        )
        for j in (1, 2, 3)
    ]
    b_copies = [
        send(
            shared.at[:, :, c, lax.rem(z + j, 4), :, in_z], z_recv.at[j - 1], send_b.at[j - 1], recv_b.at[j - 1], at_z(j)
        )
        for j in (1, 2, 3)
    ]
    for copy in a_copies:
        copy.wait()

    @pl.loop(0, 16)
    def _(i):
        yi, zi = i // 4, i % 4
        total = shared[yi, x, c, zi, :, in_x].astype(F32)
        for j in range(3):
            total = total + x_recv[j, yi, zi].astype(F32)
        x_sum[yi, zi] = total.astype(BF16)

    c_copies = [
        send(x_sum.at[:, lax.rem(z + j, 4)], x_recv2.at[j - 1], send_c.at[j - 1], recv_c.at[j - 1], at_z(j))
        for j in (1, 2, 3)
    ]
    for copy in b_copies:
        copy.wait()

    @pl.loop(0, 16)
    def _(i):
        yi, xi = i // 4, i % 4
        total = shared[yi, xi, c, z, :, in_z].astype(F32)
        for j in range(3):
            total = total + z_recv[j, yi, xi].astype(F32)
        z_sum[yi, xi] = total.astype(BF16)

    d_copies = [
        send(z_sum.at[:, lax.rem(x + j, 4)], z_recv2.at[j - 1], send_d.at[j - 1], recv_d.at[j - 1], at_x(j))
        for j in (1, 2, 3)
    ]
    for copy in c_copies + d_copies:
        copy.wait()

    @pl.loop(0, 4)
    def _(yi):
        total = x_sum[yi, z].astype(F32)
        other_total = z_sum[yi, x].astype(F32)
        for j in range(3):
            total = total + x_recv2[j, yi].astype(F32)
            other_total = other_total + z_recv2[j, yi].astype(F32)
        y_sum[yi, :, in_x] = total.astype(BF16)
        y_sum[yi, :, in_z] = other_total.astype(BF16)

    y_copies = [
        send(y_sum.at[lax.rem(y + j, 4)], y_recv.at[j - 1], send_y.at[j - 1], recv_y.at[j - 1], at_y(j))
        for j in (1, 2, 3)
    ]

    for at, (grad, far_in, near_in, passing, done_in, out) in enumerate(dp_sets):
        half = halves[at][0].size
        loads[at][2].wait()
        for side in (0, 1):
            near_copies[at][side].wait()
            pass_copies[2 * at + side].wait()

            @pl.loop(0, half // step)
            def _(i):
                here = pl.ds(pl.multiple_of(i * step, step), step)
                mine = pl.ds(pl.multiple_of(side * half + i * step, step), step)
                out[mine] = (
                    out[mine].astype(F32) + near_in[side, here].astype(F32) + done_in[side, here].astype(F32)
                ).astype(BF16)

    for copy in y_copies:
        copy.wait()
    total = y_sum[y].astype(F32)
    for j in range(3):
        total = total + y_recv[j].astype(F32)
    out_shared[...] = total


def finish(d_mid, tok_w, qkv, probs, context, attn_out, w_qkv, w_proj, gain, d_router, first, second):
    def both(rows, cols):
        return pltpu.VMEM((2, rows, cols), BF16)

    dma = pltpu.SemaphoreType.DMA
    rest = WIDTH - COLS_X
    vmem = pl.BlockSpec(memory_space=pltpu.VMEM)
    anywhere = pl.BlockSpec(memory_space=pl.ANY)
    f_half, s_half = D // 8, FF // 8
    return pl.pallas_call(
        finish_kernel,
        out_shape=(
            jax.ShapeDtypeStruct((ROWS, D), BF16),
            jax.ShapeDtypeStruct((16, WIDTH), F32),
            jax.ShapeDtypeStruct((2 * f_half, FF), BF16),
            jax.ShapeDtypeStruct((2 * s_half, D), BF16),
        ),
        in_specs=[vmem] * 10 + [anywhere] * 2,
        out_specs=[vmem] * 4,
        scratch_shapes=[
            pltpu.VMEM((ROWS, 3 * D), BF16),
            pltpu.VMEM((ROWS, D), BF16),
            pltpu.VMEM((ROWS, D), BF16),
            pltpu.VMEM((4, 4, 2, 4, 16, WIDTH), BF16),
            pltpu.VMEM((4, 4, 4, 16, WIDTH), BF16),
            pltpu.VMEM((3, 4, 4, 16, COLS_X), BF16),
            pltpu.VMEM((4, 4, 16, COLS_X), BF16),
            pltpu.VMEM((3, 4, 4, 16, rest), BF16),
            pltpu.VMEM((4, 4, 16, rest), BF16),
            pltpu.VMEM((3, 4, 16, COLS_X), BF16),
            pltpu.VMEM((3, 4, 16, rest), BF16),
            pltpu.VMEM((4, 16, WIDTH), BF16),
            pltpu.VMEM((3, 16, WIDTH), BF16),
            both(f_half, FF), both(f_half, FF), both(f_half, FF), both(f_half, FF),
            both(s_half, D), both(s_half, D), both(s_half, D), both(s_half, D),
            dma((8,)), dma((8,)),
            dma((3,)), dma((3,)), dma((3,)), dma((3,)), dma((3,)), dma((3,)), dma((3,)), dma((3,)), dma((3,)), dma((3,)),
            dma((2, 3, 2)), dma((2, 3, 2)), dma((2, 3)),
        ],
        compiler_params=pltpu.CompilerParams(
            collective_id=0, has_side_effects=True, vmem_limit_bytes=60 * MIB
        ),
    )(
        d_mid, tok_w, qkv, probs, context, attn_out, w_qkv, w_proj, gain.reshape(1, D),
        jnp.pad(d_router, ((0, 0), (0, 128 - EXPERTS))),
        first.reshape(4, 2 * f_half, FF),
        second.reshape(4, 2 * s_half, D),
    )


def unfold_shared(total):
    wide = jnp.concatenate([total[:8, : 2 * D], total[8:, : 2 * D]], axis=1)
    router = total[:8, 2 * D : 2 * D + EXPERTS] + total[8:, 2 * D : 2 * D + EXPERTS]
    return wide[:, : 3 * D].astype(BF16), wide[:, 3 * D :].astype(BF16), router


def per_device(
    tokens,
    w_qkv,
    w_proj,
    rel_bias,
    gain_attn,
    shift_attn,
    w_router,
    gain_moe,
    shift_moe,
    w_in,
    w_out,
    expert_ids,
    cotangent,
):
    tok_w, qkv, probs, context, attn_out, mid = attend(tokens, w_qkv, w_proj, rel_bias, gain_attn, shift_attn)
    block_out, d_mid, d_router, grad_first, grad_second = experts(
        mid, expert_ids, cotangent, w_router, gain_moe, shift_moe, w_in[0], w_out[0]
    )
    d_tokens, total, first_sum, second_sum = finish(
        d_mid, tok_w, qkv, probs, context, attn_out, w_qkv, w_proj, gain_attn, d_router, grad_first, grad_second
    )
    sum_qkv, sum_proj, sum_router = unfold_shared(total)
    return block_out, d_tokens, sum_qkv, sum_proj, sum_router, first_sum[None], second_sum[None]


def solution(mesh):
    split = P(("dp", "group", "node"), None)
    expert = P(("group", "node"), None, None)
    owned = P(("group", "node"), "dp", None)
    return jax.shard_map(
        per_device,
        mesh=mesh,
        in_specs=(split, P(), P(), P(), P(), P(), P(), P(), P(), expert, expert, split, split),
        out_specs=(split, split, split, split, split, owned, owned),
        check_vma=False,
    )
```

```python
import jax
import jax.numpy as jnp
from jax import lax
from jax.experimental import pallas as pl
from jax.experimental.pallas import tpu as pltpu
from jax.sharding import PartitionSpec as P

MESH = pl.DeviceIdType.MESH
F32 = jnp.float32
BF16 = jnp.bfloat16
MIB = 1 << 20
D = 1024
FF = 2048
HEADS = 32
HEAD_DIM = 32
WIN = 8
EXPERTS = 32
ROWS = 256
SLOTS = 20
EPS = 1e-05
NEG = -1e30
SCALE = HEAD_DIM ** (-0.5)
CHUNK = 1280
X_COLS = ((0, 256), (256, 512), (512, 1024))
Z_COLS = ((0, 256), (256, 768), (768, 1152))
BATCH = 16


def dot(a, b):
    return lax.dot_general(a, b, (((1,), (0,)), ((), ())), preferred_element_type=F32)


def dot_nt(a, b):
    return lax.dot_general(a, b, (((1,), (1,)), ((), ())), preferred_element_type=F32)


def dot_tn(a, b):
    return lax.dot_general(a, b, (((0,), (0,)), ((), ())), preferred_element_type=F32)


def iota(shape, dim):
    return lax.broadcasted_iota(jnp.int32, shape, dim)


def flag(cond):
    return jnp.where(cond, 1.0, 0.0).astype(BF16)


def split3(values):
    high = values.astype(BF16)
    rest = values - high.astype(F32)
    mid = rest.astype(BF16)
    return high, mid, (rest - mid.astype(F32)).astype(BF16)


def token_of(place):
    window, inner = place >> 6, place & 63
    row = (((window >> 1) << 3) + (inner >> 3) + WIN // 2) & 15
    col = (((window & 1) << 3) + (inner & 7) + WIN // 2) & 15
    return (row << 4) + col


def to_windows():
    return flag(iota((ROWS, ROWS), 1) == token_of(iota((ROWS, ROWS), 0)))


def from_windows():
    return flag(iota((ROWS, ROWS), 0) == token_of(iota((ROWS, ROWS), 1)))


def normalise(values):
    mean = jnp.mean(values, axis=-1, keepdims=True)
    centered = values - mean
    rstd = lax.rsqrt(jnp.mean(centered * centered, axis=-1, keepdims=True) + EPS)
    return centered * rstd, rstd


def norm_pull(unit, rstd, slope):
    return rstd * (
        slope - jnp.mean(slope, axis=-1, keepdims=True) - unit * jnp.mean(slope * unit, axis=-1, keepdims=True)
    )


def head_mask():
    return flag((iota((256, 128), 0) >> 6) == (iota((256, 128), 1) >> 5))


def by_head(ref, pair, first, mask):
    parts = []
    for side in (0, 1):
        rows = ref[pair * 128 + side * 64 : pair * 128 + side * 64 + 64, pl.ds(first, 128)]
        parts.append(jnp.concatenate([rows] * 4, axis=0) * mask)
    return jnp.concatenate(parts, axis=1)


def by_window(ref, pair, first, upper):
    rows = ref[pair * 128 : pair * 128 + 128, pl.ds(first, 128)]
    return jnp.concatenate([rows * upper, rows * (1 - upper)], axis=1)


def attend_kernel(
    tokens, w_qkv, w_proj, rel_bias, gain, shift,
    tok_t, qkv, probs, context_t, attn_out, mid,
    tok_w, context, bias,
):
    tok_w[...] = dot(to_windows(), tokens[...]).astype(BF16)
    for at in range(6):
        cols = slice(at * 512, at * 512 + 512)
        qkv[:, cols] = dot(tok_w[...], w_qkv[:, cols]).astype(BF16)

    table = jnp.concatenate(split3(rel_bias[...]), axis=0)
    entry = iota((256, 128), 0)
    query = iota((256, 128), 1) & 63

    @pl.loop(0, 16)
    def _(block):
        for inner in range(4):
            key = block * 4 + inner
            place = ((query >> 3) - (key >> 3) + WIN - 1) * (2 * WIN - 1) + (query & 7) - (key & 7) + WIN - 1
            found = dot(table, flag(entry == place))
            bias[pl.ds(key, HEADS, stride=64), :] = found[:32] + (found[32:64] + found[64:96])

    mask = head_mask()
    key = iota((256, 128), 0) & 63
    lane = iota((256, 128), 1)
    row_differs = ((key >> 5) ^ (lane >> 5)) & 1
    col_differs = ((key ^ lane) >> 2) & 1 & (lane >> 6)
    upper = flag(iota((128, 128), 0) < 64)
    for pair in range(2):
        apart = jnp.where((col_differs | (row_differs if pair else 0)) == 1, NEG, 0.0)
        for group in range(8):
            keys = by_head(qkv, pair, D + group * 128, mask)
            queries = by_window(qkv, pair, group * 128, upper)
            scores = dot_nt(keys, queries) * SCALE + bias[group * 256 : group * 256 + 256, :] + apart
            scores = scores.reshape(4, 64, 128)
            weights = jnp.exp(scores - jnp.max(scores, axis=1, keepdims=True))
            prob = (weights / jnp.sum(weights, axis=1, keepdims=True)).reshape(256, 128).astype(BF16)
            probs[pair, group] = prob
            both = dot_tn(prob, by_head(qkv, pair, 2 * D + group * 128, mask))
            for side in (0, 1):
                context[pair * 128 + side * 64 : pair * 128 + side * 64 + 64, group * 128 : group * 128 + 128] = both[
                    side * 64 : side * 64 + 64, side * 128 : side * 128 + 128
                ].astype(BF16)

    tok_t[...] = tok_w[...].T
    context_t[...] = context[...].T
    projected = dot(context[...], w_proj[...])
    attn_out[...] = projected
    unit, _ = normalise(projected)
    mid_w = (tok_w[...].astype(F32) + (unit * gain[...] + shift[...])).astype(BF16)
    mid[...] = dot(from_windows(), mid_w).astype(BF16)


def attend(tokens, w_qkv, w_proj, rel_bias, gain, shift):
    vmem = pl.BlockSpec(memory_space=pltpu.VMEM)
    return pl.pallas_call(
        attend_kernel,
        out_shape=(
            jax.ShapeDtypeStruct((D, ROWS), BF16),
            jax.ShapeDtypeStruct((ROWS, 3 * D), BF16),
            jax.ShapeDtypeStruct((2, 8, 256, 128), BF16),
            jax.ShapeDtypeStruct((D, ROWS), BF16),
            jax.ShapeDtypeStruct((ROWS, D), F32),
            jax.ShapeDtypeStruct((ROWS, D), BF16),
        ),
        in_specs=[vmem] * 6,
        out_specs=[vmem] * 6,
        scratch_shapes=[pltpu.VMEM((ROWS, D), BF16), pltpu.VMEM((ROWS, D), BF16), pltpu.VMEM((HEADS * 64, 128), F32)],
        compiler_params=pltpu.CompilerParams(vmem_limit_bytes=48 * MIB),
    )(tokens, w_qkv, w_proj, jnp.pad(rel_bias, ((0, 0), (0, 31))), gain.reshape(1, D), shift.reshape(1, D))


def expert_of_row(shape, dim):
    row = iota(shape, dim)
    return jnp.where(row < EXPERTS * 16, row >> 4, (row >> 2) & (EXPERTS - 1))


def rank_of_row(shape, dim):
    row = iota(shape, dim)
    return jnp.where(row < EXPERTS * 16, row & 15, 16 + (row & 3))


def fold_order(count):
    row, col = iota((16 * count, 16 * count), 0), iota((16 * count, 16 * count), 1)
    size = 4 * count
    block = sum([(row >= size * at).astype(jnp.int32) for at in (1, 2, 3)])
    inner = row - block * size
    return flag(col == ((inner >> 2) << 4) + (block << 2) + (inner & 3))


def unfold(ref, first, count, order, out, out_first):
    main = ref[first : first + count, :, :D].reshape(16 * count, D)
    rest = dot(order, ref[first : first + count, :, D:].reshape(16 * count, CHUNK - D)).astype(BF16)
    out[out_first : out_first + 16 * count, :] = main
    for block in range(4):
        out[out_first + 16 * count : out_first + 20 * count, block * 256 : block * 256 + 256] = rest[
            block * 4 * count : block * 4 * count + 4 * count
        ]


def fold(rows, count, order, ref, first):
    ref[first : first + count, :, :D] = rows[: 16 * count].astype(BF16).reshape(count, 16, D)
    rest = rows[16 * count :].astype(BF16)
    stacked = jnp.concatenate([rest[:, block * 256 : block * 256 + 256] for block in range(4)], axis=0)
    ref[first : first + count, :, D:] = dot_tn(order, stacked).astype(BF16).reshape(count, 16, CHUNK - D)


def gelu_parts(values):
    z = jnp.abs(values) * 0.7071067811865476
    t = 1.0 / (1.0 + 0.3275911 * z)
    bell = jnp.exp(-z * z)
    poly = ((((1.061405429 * t - 1.453152027) * t + 1.421413741) * t - 0.284496736) * t + 0.254829592) * t
    tail = 0.5 * poly * bell
    phi = jnp.where(values >= 0, 1.0 - tail, tail)
    return values * phi, phi + values * bell * 0.3989422804014327


def routes(me, peer, send_sem, recv_sem):
    def to_expert(route, source, target, j):
        e = lax.rem(me + j, EXPERTS)
        return pltpu.make_async_remote_copy(
            src_ref=source.at[e], dst_ref=target.at[j], send_sem=send_sem.at[route, j], recv_sem=recv_sem.at[route, j],
            device_id=peer(e), device_id_type=MESH,
        )

    def to_source(route, source, target, j):
        return pltpu.make_async_remote_copy(
            src_ref=source.at[j], dst_ref=target.at[me], send_sem=send_sem.at[route, j], recv_sem=recv_sem.at[route, j],
            device_id=peer(lax.rem(me + EXPERTS - j, EXPERTS)), device_id_type=MESH,
        )

    def start_all(make, route, source, target, first, last):
        @pl.loop(max(first, 1), last)
        def _(j):
            make(route, source, target, j).start()

    def receive(make, route, source, target, first, last):
        @pl.loop(max(first, 1), last)
        def _(j):
            make(route, source, target, j).wait_recv()

    return to_expert, to_source, start_all, receive


def experts_phase(
    env, w_first, w_second, out1, out2, out3, rows, d_rows, hidden, slope, back, select,
):
    (
        mid, ids, cotangent, w_router, gain, shift, w_in, w_out, block_out, in1, in2, in3, in4, out4,
        g_first, g_second, pick_sum, d_direct, router_own, router_other, load_sem, send_sem, recv_sem,
        me, c, peer, barrier, start_core, core_send,
    ) = env
    load_first = pltpu.make_async_copy(w_in, w_first, load_sem.at[0])
    load_second = pltpu.make_async_copy(w_out, w_second, load_sem.at[1])
    load_first.start()
    load_second.start()
    to_expert, to_source, start_all, receive = routes(me, peer, send_sem, recv_sem)

    expert_lane = iota((ROWS, EXPERTS), 1)
    chosen = [jnp.where(ids[:, k : k + 1] == expert_lane, 1.0, 0.0) for k in range(2)]
    earlier = flag(iota((ROWS, ROWS), 0) > iota((ROWS, ROWS), 1))
    rank = dot(earlier, (chosen[0] + chosen[1]).astype(BF16)) + 1.0
    places = [(one * rank).astype(BF16) for one in chosen]
    row_experts = flag(expert_of_row((EXPERTS * SLOTS, EXPERTS), 0) == iota((EXPERTS * SLOTS, EXPERTS), 1))
    row_ranks = rank_of_row((EXPERTS * SLOTS, ROWS), 0).astype(F32) + 1.0
    for k in range(2):
        select[:, k * ROWS : k * ROWS + ROWS] = flag(dot_nt(row_experts, places[k]) == row_ranks)
    order = fold_order(EXPERTS)
    batch_order = fold_order(BATCH)

    fold(dot(select[:, :ROWS] + select[:, ROWS:], mid[...]), EXPERTS, order, out1, 0)
    pl.semaphore_wait(barrier, EXPERTS + 2)
    start_core()
    start_all(to_expert, 0, out1, in1, 1, EXPERTS)
    in1[0] = out1[me]

    router = split3(w_router[...])
    logits = dot(mid[...], router[0]) + (dot(mid[...], router[1]) + dot(mid[...], router[2]))
    gating = []
    for k in range(2):
        logit = jnp.sum(logits * chosen[k], axis=1, keepdims=True)
        gating.append(1.0 / (1.0 + jnp.exp(-logit)))
    load_first.wait()
    load_second.wait()

    batch_rows = SLOTS * BATCH
    for batch in range(EXPERTS // BATCH):
        first, last = batch * BATCH, batch * BATCH + BATCH
        here = slice(batch * batch_rows, batch * batch_rows + batch_rows)
        receive(to_expert, 0, out1, in1, first, last)
        unfold(in1, first, BATCH, batch_order, rows, batch * batch_rows)
        for at in range(8):
            cols = slice(at * 256, at * 256 + 256)
            value, value_slope = gelu_parts(dot(rows[here, :], w_first[:, cols]))
            hidden[here, cols] = value.astype(BF16)
            slope[here, cols] = value_slope.astype(BF16)
        fold(dot(hidden[here, :], w_second[...]), BATCH, batch_order, out2, first)
        start_all(to_source, 1, out2, in2, first, last)
        if batch == 0:
            in2[me] = out2[0]

    lane_experts = flag(expert_of_row((EXPERTS * SLOTS, EXPERTS), 0) == iota((EXPERTS * SLOTS, EXPERTS), 1))
    lane_ranks = rank_of_row((ROWS, EXPERTS * SLOTS), 1).astype(F32) + 1.0
    picks = [flag(dot_nt(places[k], lane_experts) == lane_ranks) for k in range(2)]
    pick_sum[...] = picks[0] + picks[1]
    receive(to_source, 1, out2, in2, 1, EXPERTS)
    unfold(in2, 0, EXPERTS, order, back, 0)
    picked = [dot(picks[k], back[...]) for k in range(2)]
    unit, rstd = normalise(gating[0] * picked[0] + gating[1] * picked[1])
    block_out[...] = (mid[...].astype(F32) + (unit * gain[...] + shift[...])).astype(BF16)
    d_mixture = norm_pull(unit, rstd, cotangent[...].astype(F32) * gain[...])
    d_picked = jnp.concatenate([(gating[k] * d_mixture).astype(BF16) for k in range(2)], axis=0)
    fold(dot(select[...], d_picked), EXPERTS, order, out3, 0)
    start_all(to_expert, 2, out3, in3, 1, EXPERTS)
    in3[0] = out3[me]

    d_logits = jnp.zeros((ROWS, EXPERTS), F32)
    for k in range(2):
        d_gating = jnp.sum(d_mixture * picked[k], axis=1, keepdims=True)
        d_logits = d_logits + chosen[k] * (d_gating * gating[k] * (1.0 - gating[k]))
    d_high = d_logits.astype(BF16)
    d_low = (d_logits - d_high.astype(F32)).astype(BF16)
    wide = [jnp.concatenate([part, jnp.zeros((ROWS, 128 - EXPERTS), BF16)], axis=1) for part in (d_high, d_low)]
    d_router = (dot_tn(mid[...], wide[0]) + dot_tn(mid[...], wide[1])).reshape(16, 2, 4, 8, 128)
    high = d_router.astype(BF16).astype(F32)
    router_own[...] = jnp.concatenate([high, d_router - high], axis=3).astype(BF16)
    core_send(lambda: (router_own.at[:, 1 - c], router_other), 2)
    from_router = dot_nt(d_high, router[0]) + (dot_nt(d_low, router[0]) + dot_nt(d_high, router[1]))
    d_direct[...] = cotangent[...].astype(F32) + from_router

    for batch in range(EXPERTS // BATCH):
        first, last = batch * BATCH, batch * BATCH + BATCH
        here = slice(batch * batch_rows, batch * batch_rows + batch_rows)
        receive(to_expert, 2, out3, in3, first, last)
        unfold(in3, first, BATCH, batch_order, d_rows, batch * batch_rows)
        for at in range(8):
            cols = slice(at * 256, at * 256 + 256)
            d_hidden = dot_nt(d_rows[here, :], w_second[cols, :])
            slope[here, cols] = (d_hidden * slope[here, cols].astype(F32)).astype(BF16)
        fold(dot_nt(slope[here, :], w_first[...]), BATCH, batch_order, out4, first)
        start_all(to_source, 3, out4, in4, first, last)
        if batch == 0:
            in4[me] = out4[0]

    for at in range(8):
        cols = slice(at * 256, at * 256 + 256)
        g_second[at // 2, at % 2 * 256 : at % 2 * 256 + 256, :] = dot(hidden[:, cols].T, d_rows[...]).astype(BF16)
    for at in range(4):
        cols = slice(at * 256, at * 256 + 256)
        g_first[at, :, :] = dot(rows[:, cols].T, slope[...]).astype(BF16)

    @pl.loop(1, EXPERTS)
    def _(j):
        to_expert(0, out1, in1, j).wait_send()
        to_source(1, out2, in2, j).wait_send()
        to_expert(2, out3, in3, j).wait_send()


def attend_back_groups(groups, qkv, probs, d_context, d_qkv):
    mask = head_mask()
    mask_f = mask.astype(F32)
    upper = flag(iota((128, 128), 0) < 64)

    def own_heads(values, side):
        return (values[:, side * 128 : side * 128 + 128] * mask_f).reshape(4, 64, 128).sum(axis=0)

    for group in groups:
        for pair in range(2):
            first = group * 128
            values = by_head(qkv, pair, 2 * D + first, mask)
            keys = by_head(qkv, pair, D + first, mask)
            queries = by_window(qkv, pair, first, upper)
            d_out = by_window(d_context, pair, first, upper)
            prob = probs[pair, group]
            d_prob = dot_nt(values, d_out)
            prob_f = prob.astype(F32)
            inner = (prob_f * d_prob).reshape(4, 64, 128).sum(axis=1, keepdims=True)
            d_score = prob_f.reshape(4, 64, 128) * (d_prob.reshape(4, 64, 128) - inner) * SCALE
            d_score = d_score.reshape(256, 128).astype(BF16)
            d_value = dot(prob, d_out)
            d_key = dot(d_score, queries)
            d_query = dot_tn(d_score, keys)
            for side in (0, 1):
                rows = slice(pair * 128 + side * 64, pair * 128 + side * 64 + 64)
                d_qkv[rows, first : first + 128] = d_query[
                    side * 64 : side * 64 + 64, side * 128 : side * 128 + 128
                ].astype(BF16)
                d_qkv[rows, D + first : D + first + 128] = own_heads(d_key, side).astype(BF16)
                d_qkv[rows, 2 * D + first : 2 * D + first + 128] = own_heads(d_value, side).astype(BF16)


def finish_phase(
    env, qkv, probs, attn_out, w_qkv, w_proj, d_context, back, grad_x, grad_z, sum_x, sum_z, sum_y,
):
    (
        refs, gain_attn, d_tokens, out_qkv, out_proj, out_router, out_first, out_second,
        in4, out4, pick_sum, d_direct, router_own, router_other, tok_2, context_2, d_qkv_2, d_attn_2,
        g_first, g_second, f_far, f_near, f_done, s_far, s_near, s_done,
        x_far, x_near, x_done, z_far, z_near, z_done, x_recv, z_recv, y_recv,
        load_sem, send_sem, recv_sem, send_one, recv_one, send_two, recv_two, send_y, recv_y, send_dp, recv_dp,
        me, x, y, z, c, peer, core_send, core_wait,
    ) = env
    loads = [
        pltpu.make_async_copy(source, target, load_sem.at[2 + at])
        for at, (source, target) in enumerate(zip(refs, (attn_out, w_proj, qkv, probs, w_qkv)))
    ]
    for load in loads:
        load.start()
    to_expert, to_source, start_all, receive = routes(me, peer, send_sem, recv_sem)

    def at_x(j):
        return {"group": lax.rem(x + j, 4) * 2 + c}

    def at_y(j):
        return {"dp": lax.rem(y + j, 4)}

    def at_z(j):
        return {"node": lax.rem(z + j, 4)}

    def send(src, dst, s_sem, r_sem, target):
        copy = pltpu.make_async_remote_copy(
            src_ref=src, dst_ref=dst, send_sem=s_sem, recv_sem=r_sem, device_id=target, device_id_type=MESH
        )
        copy.start()
        return copy

    def add_into(ref, at, first, count, step, more):
        @pl.loop(0, count // step)
        def _(i):
            here = pl.ds(pl.multiple_of(i * step, step), step)
            mine = pl.ds(pl.multiple_of(first + i * step, step), step)
            total = ref[at, mine].astype(F32)
            for other, side in more:
                total = total + other[side, here].astype(F32)
            ref[at, mine] = total.astype(BF16)

    right, left, far = lax.rem(y + 1, 4), lax.rem(y + 3, 4), lax.rem(y + 2, 4)
    dp_sets = ((g_second, s_far, s_near, s_done, out_second), (g_first, f_far, f_near, f_done, out_first))
    halves = [grad.shape[1] // 2 for grad, *_ in dp_sets]
    dp_far, dp_near = [], []
    for at, (grad, far_in, near_in, done_in, out) in enumerate(dp_sets):
        rows = (pl.ds(0, halves[at]), pl.ds(halves[at], halves[at]))
        dp_far.append((
            send(grad.at[far, rows[0]], far_in.at[0], send_dp.at[at, 0, 0], recv_dp.at[at, 0, 0], at_y(1)),
            send(grad.at[far, rows[1]], far_in.at[1], send_dp.at[at, 0, 1], recv_dp.at[at, 0, 1], at_y(3)),
        ))
    for at, (grad, far_in, near_in, done_in, out) in enumerate(dp_sets):
        rows = (pl.ds(0, halves[at]), pl.ds(halves[at], halves[at]))
        dp_near.append((
            send(grad.at[left, rows[0]], near_in.at[0], send_dp.at[at, 1, 0], recv_dp.at[at, 1, 0], at_y(3)),
            send(grad.at[right, rows[1]], near_in.at[1], send_dp.at[at, 1, 1], recv_dp.at[at, 1, 1], at_y(1)),
        ))

    def dp_pass(at):
        grad, far_in, near_in, done_in, out = dp_sets[at]
        copies = []
        for side, (block, target) in enumerate(((right, at_y(1)), (left, at_y(3)))):
            dp_far[at][side].wait()
            add_into(grad, block, side * halves[at], halves[at], 64, ((far_in, side),))
            copies.append(send(
                grad.at[block, pl.ds(side * halves[at], halves[at])], done_in.at[side],
                send_dp.at[at, 2, side], recv_dp.at[at, 2, side], target,
            ))
        return copies

    def dp_finish(at, copies):
        grad, far_in, near_in, done_in, out = dp_sets[at]
        for side in (0, 1):
            dp_near[at][side].wait()
            copies[side].wait()
            add_into(grad, y, side * halves[at], halves[at], 64, ((near_in, side), (done_in, side)))
        write = pltpu.make_async_copy(grad.at[y], out, load_sem.at[7 + at])
        write.start()
        return write

    rings = (
        (grad_x, x_far, x_near, x_done, sum_x, x, at_x, X_COLS, 1),
        (grad_z, z_far, z_near, z_done, sum_z, z, at_z, Z_COLS, 2),
    )

    def block_of(ref, dim, half, place, cols):
        where = [pl.ds(2 * half, 2), slice(None), slice(None), slice(None), pl.ds(cols[0], cols[1] - cols[0])]
        where[dim] = place
        return ref.at[tuple(where)]

    def ring_start(part):
        copies = []
        for ring, (grad, far_in, near_in, done_in, total, own, at, cols, dim) in enumerate(rings):
            here = cols[part]
            span = pl.ds(here[0], here[1] - here[0])
            up, down, opposite = lax.rem(own + 1, 4), lax.rem(own + 3, 4), lax.rem(own + 2, 4)
            sems = lambda kind, side: (send_one.at[part, ring, kind, side], recv_one.at[part, ring, kind, side])
            copies.append((
                send(block_of(grad, dim, 0, opposite, here), far_in.at[0, :, :, :, span], *sems(0, 0), at(1)),
                send(block_of(grad, dim, 1, opposite, here), far_in.at[1, :, :, :, span], *sems(0, 1), at(3)),
                send(block_of(grad, dim, 0, down, here), near_in.at[0, :, :, :, span], *sems(1, 0), at(3)),
                send(block_of(grad, dim, 1, up, here), near_in.at[1, :, :, :, span], *sems(1, 1), at(1)),
            ))
        return copies

    def ring_pass(part, started):
        copies = []
        for ring, (grad, far_in, near_in, done_in, total, own, at, cols, dim) in enumerate(rings):
            here = cols[part]
            span = pl.ds(here[0], here[1] - here[0])
            for side, (place, hop) in enumerate(((lax.rem(own + 1, 4), 1), (lax.rem(own + 3, 4), 3))):
                started[ring][side].wait()

                @pl.loop(0, 8)
                def _(i):
                    yi, oi = i // 4, i % 4
                    index = (2 * side + yi, place, oi) if dim == 1 else (2 * side + yi, oi, place)
                    grad[(*index, slice(None), span)] = (
                        grad[(*index, slice(None), span)].astype(F32) + far_in[side, yi, oi, :, span].astype(F32)
                    ).astype(BF16)

                copies.append(send(
                    block_of(grad, dim, side, place, here), done_in.at[side, :, :, :, span],
                    send_one.at[part, ring, 2, side], recv_one.at[part, ring, 2, side], at(hop),
                ))
        return copies

    def ring_finish(ring, started, passed):
        grad, far_in, near_in, done_in, total, own, at, cols, dim = rings[ring]
        for part in range(3):
            for side in (0, 1):
                started[part][ring][2 + side].wait()
                passed[part][2 * ring + side].wait()

        @pl.loop(0, 16)
        def _(i):
            yi, oi = i // 4, i % 4
            side, inner = yi // 2, yi % 2
            index = (yi, own, oi) if dim == 1 else (yi, oi, own)
            total[yi, oi] = (
                grad[index].astype(F32) + near_in[side, inner, oi].astype(F32) + done_in[side, inner, oi].astype(F32)
            ).astype(BF16)

    def folded(left_t, right, cols):
        parts = dot(left_t[...].reshape(512, 512), right[:, cols : cols + 512]).reshape(64, 8, 512)
        return jnp.concatenate([parts[:, :, :256], parts[:, :, 256:]], axis=1).astype(BF16).reshape(4, 4, 4, 16, 256)

    receive(to_source, 3, out4, in4, 1, EXPERTS)
    unfold(in4, 0, EXPERTS, fold_order(EXPERTS), back, 0)
    d_mid = (d_direct[...] + dot(pick_sum[...], back[...])).astype(BF16)
    d_mid_w = dot(to_windows(), d_mid)
    d_direct[...] = d_mid_w
    loads[0].wait()
    loads[1].wait()
    unit, rstd = normalise(attn_out[...])
    d_attn_2[:ROWS, :] = norm_pull(unit, rstd, d_mid_w * gain_attn[...]).astype(BF16)
    core_send(lambda: (d_attn_2.at[pl.ds(0, ROWS)], d_attn_2.at[pl.ds(ROWS, ROWS)]), 3)
    d_context[...] = dot_nt(d_attn_2[:ROWS, :], w_proj[...]).astype(BF16)
    loads[2].wait()
    loads[3].wait()

    def core_send_heads(half):
        for at in range(3):
            cols = pl.ds(at * D + half * 512, 512)
            core_send(
                lambda cols=cols: (d_qkv_2.at[pl.ds(0, ROWS), cols], d_qkv_2.at[pl.ds(ROWS, ROWS), cols]),
                4 + 3 * half + at,
            )

    started, passed = [], []
    attend_back_groups(range(4), qkv, probs, d_context, d_qkv_2)
    core_send_heads(0)
    core_wait(1)
    core_wait(3)
    grad_x[..., 0:256] = folded(context_2, d_attn_2, 0)
    grad_z[..., 0:256] = folded(context_2, d_attn_2, 512)
    started.append(ring_start(0))
    attend_back_groups(range(4, 8), qkv, probs, d_context, d_qkv_2)
    core_send_heads(1)
    core_wait(0)
    for at in range(3):
        core_wait(4 + at)
    grad_x[..., 256:512] = folded(tok_2, d_qkv_2, 0)
    grad_z[..., 256:512] = folded(tok_2, d_qkv_2, D)
    grad_z[..., 512:768] = folded(tok_2, d_qkv_2, 2 * D)
    started.append(ring_start(1))
    passed.append(ring_pass(0, started[0]))
    core_wait(2)
    for at in range(3):
        core_wait(7 + at)
    grad_x[..., 512:768] = folded(tok_2, d_qkv_2, 512)
    grad_x[..., 768:1024] = folded(tok_2, d_qkv_2, D + 512)
    grad_z[..., 768:1024] = folded(tok_2, d_qkv_2, 2 * D + 512)
    grad_z[..., 1024:1152] = (
        (router_own[:, c].astype(F32) + router_other[...].astype(F32)).astype(BF16).reshape(4, 4, 4, 16, 128)
    )
    started.append(ring_start(2))
    passed.append(ring_pass(1, started[1]))
    loads[4].wait()
    d_tok_w = (d_direct[...] + dot_nt(d_qkv_2[:ROWS, :], w_qkv[...])).astype(BF16)
    d_tokens[...] = dot(from_windows(), d_tok_w).astype(BF16)
    dp_passed = [dp_pass(0)]
    passed.append(ring_pass(2, started[2]))
    dp_passed.append(dp_pass(1))

    second = []
    for ring, (total, recv, at) in enumerate(((sum_x, x_recv, at_z), (sum_z, z_recv, at_x))):
        ring_finish(ring, started, passed)
        place = (z, x)[ring]
        second.append([
            send(
                total.at[:, lax.rem(place + j, 4)], recv.at[j - 1],
                send_two.at[ring, j - 1], recv_two.at[ring, j - 1], at(j),
            )
            for j in (1, 2, 3)
        ])
    for copy in second[0] + second[1]:
        copy.wait()

    @pl.loop(0, 4)
    def _(yi):
        total_x = sum_x[yi, z].astype(F32)
        total_z = sum_z[yi, x].astype(F32)
        for j in range(3):
            total_x = total_x + x_recv[j, yi].astype(F32)
            total_z = total_z + z_recv[j, yi].astype(F32)
        sum_y[yi, :, :1024] = total_x.astype(BF16)
        sum_y[yi, :, 1024:] = total_z.astype(BF16)

    third = [
        send(sum_y.at[lax.rem(y + j, 4)], y_recv.at[j - 1], send_y.at[j - 1], recv_y.at[j - 1], at_y(j))
        for j in (1, 2, 3)
    ]
    writes = [dp_finish(at, dp_passed[at]) for at in range(2)]
    for copy in third:
        copy.wait()
    total = sum_y[y].astype(F32)
    for j in range(3):
        total = total + y_recv[j].astype(F32)

    def unfolded(first):
        return jnp.concatenate([total[:8, first : first + 256], total[8:, first : first + 256]], axis=1)

    out_proj[...] = jnp.concatenate([unfolded(0), unfolded(1024)], axis=1).astype(BF16)
    out_qkv[...] = jnp.concatenate(
        [unfolded(first) for first in (256, 512, 1280, 768, 1536, 1792)], axis=1
    ).astype(BF16)
    out_router[...] = total[:8, 2048:] + total[8:, 2048:]

    @pl.loop(1, EXPERTS)
    def _(j):
        to_source(3, out4, in4, j).wait_send()

    for write in writes:
        write.wait()


def main_kernel(
    mid, ids, cotangent, w_router, gain, shift, gain_attn,
    w_in, w_out, tok_t, context_t, attn_out, w_proj, qkv, probs, w_qkv,
    block_out, d_tokens, out_qkv, out_proj, out_router, out_first, out_second,
    in1, in2, in3, in4, out4, g_first, g_second, pick_sum, d_direct, router_own, router_other,
    tok_2, context_2, d_qkv_2, d_attn_2,
    f_far, f_near, f_done, s_far, s_near, s_done,
    x_far, x_near, x_done, z_far, z_near, z_done, x_recv, z_recv, y_recv,
    load_sem, send_sem, recv_sem, send_core, recv_core, send_one, recv_one, send_two, recv_two,
    send_y, recv_y, send_dp, recv_dp,
):
    y = lax.axis_index("dp")
    g = lax.axis_index("group")
    z = lax.axis_index("node")
    x = g // 2
    c = g % 2
    me = g * 4 + z
    other = {"group": x * 2 + (1 - c)}

    def peer(e):
        return {"group": e // 4, "node": lax.rem(e, 4)}

    barrier = pltpu.get_barrier_semaphore()

    @pl.loop(1, EXPERTS)
    def _(j):
        pl.semaphore_signal(barrier, inc=1, device_id=peer(lax.rem(me + j, EXPERTS)), device_id_type=MESH)

    for j in (1, 2, 3):
        pl.semaphore_signal(barrier, inc=1, device_id={"dp": lax.rem(y + j, 4)}, device_id_type=MESH)

    def core_copy(src, dst, at):
        return pltpu.make_async_remote_copy(
            src_ref=src, dst_ref=dst, send_sem=send_core.at[at], recv_sem=recv_core.at[at],
            device_id=other, device_id_type=MESH,
        )

    core_ends = {}

    def core_send(ends, at):
        core_ends[at] = ends
        core_copy(*ends(), at).start()

    def core_wait(at):
        core_copy(*core_ends[at](), at).wait()

    own = pl.ds(0, ROWS)
    theirs = pl.ds(ROWS, ROWS)
    keep = [
        pltpu.make_async_copy(source.at[:, c], target.at[:, :, own], load_sem.at[9 + at])
        for at, (source, target) in enumerate(((tok_t, tok_2), (context_t, context_2)))
    ]

    def start_core():
        for at, (source, target) in enumerate(((tok_t, tok_2), (context_t, context_2))):
            keep[at].start()
            core_send(lambda source=source, target=target: (source.at[:, 1 - c], target.at[:, :, theirs]), at)

    first_env = (
        mid, ids, cotangent, w_router, gain, shift, w_in, w_out, block_out, in1, in2, in3, in4, out4,
        g_first, g_second, pick_sum, d_direct, router_own, router_other, load_sem, send_sem, recv_sem,
        me, c, peer, barrier, start_core, core_send,
    )
    slots = EXPERTS * SLOTS
    box = pltpu.VMEM((EXPERTS, 16, CHUNK), BF16)
    pl.run_scoped(
        lambda *scratch: experts_phase(first_env, *scratch),
        pltpu.VMEM((D, FF), BF16), pltpu.VMEM((FF, D), BF16), box, box, box,
        pltpu.VMEM((slots, D), BF16), pltpu.VMEM((slots, D), BF16),
        pltpu.VMEM((slots, FF), BF16), pltpu.VMEM((slots, FF), BF16),
        pltpu.VMEM((slots, D), BF16), pltpu.VMEM((slots, 2 * ROWS), BF16),
    )
    for copy in keep:
        copy.wait()
    last_env = (
        (attn_out, w_proj, qkv, probs, w_qkv),
        gain_attn, d_tokens, out_qkv, out_proj, out_router, out_first, out_second,
        in4, out4, pick_sum, d_direct, router_own, router_other, tok_2, context_2, d_qkv_2, d_attn_2,
        g_first, g_second, f_far, f_near, f_done, s_far, s_near, s_done,
        x_far, x_near, x_done, z_far, z_near, z_done, x_recv, z_recv, y_recv,
        load_sem, send_sem, recv_sem, send_one, recv_one, send_two, recv_two, send_y, recv_y, send_dp, recv_dp,
        me, x, y, z, c, peer, core_send, core_wait,
    )
    pl.run_scoped(
        lambda *scratch: finish_phase(last_env, *scratch),
        pltpu.VMEM((ROWS, 3 * D), BF16), pltpu.VMEM((2, 8, 256, 128), BF16), pltpu.VMEM((ROWS, D), F32),
        pltpu.VMEM((D, 3 * D), BF16), pltpu.VMEM((D, D), BF16), pltpu.VMEM((ROWS, D), BF16),
        pltpu.VMEM((slots, D), BF16),
        pltpu.VMEM((4, 4, 4, 16, 1024), BF16), pltpu.VMEM((4, 4, 4, 16, 1152), BF16),
        pltpu.VMEM((4, 4, 16, 1024), BF16), pltpu.VMEM((4, 4, 16, 1152), BF16), pltpu.VMEM((4, 16, 2176), BF16),
    )


def main(mid, ids, cotangent, w_router, gain, shift, gain_attn, w_in, w_out, tok_t, context_t, attn_out, w_proj, qkv, probs, w_qkv):
    vmem = pl.BlockSpec(memory_space=pltpu.VMEM)
    anywhere = pl.BlockSpec(memory_space=pl.ANY)
    dma = pltpu.SemaphoreType.DMA
    slots = EXPERTS * SLOTS

    def hold(*shape):
        return pltpu.VMEM(shape, BF16)

    box = hold(EXPERTS, 16, CHUNK)
    return pl.pallas_call(
        main_kernel,
        out_shape=(
            jax.ShapeDtypeStruct((ROWS, D), BF16),
            jax.ShapeDtypeStruct((ROWS, D), BF16),
            jax.ShapeDtypeStruct((8, 3 * D), BF16),
            jax.ShapeDtypeStruct((8, D), BF16),
            jax.ShapeDtypeStruct((8, 128), F32),
            jax.ShapeDtypeStruct((D // 4, FF), BF16),
            jax.ShapeDtypeStruct((FF // 4, D), BF16),
        ),
        in_specs=[vmem] * 7 + [anywhere] * 9,
        out_specs=[vmem] * 5 + [anywhere] * 2,
        scratch_shapes=[
            box, box, box, box, box,
            hold(4, D // 4, FF), hold(4, FF // 4, D), hold(ROWS, slots), pltpu.VMEM((ROWS, D), F32),
            hold(16, 2, 4, 16, 128), hold(16, 4, 16, 128),
            hold(16, 32, 2 * ROWS), hold(16, 32, 2 * ROWS), hold(2 * ROWS, 3 * D), hold(2 * ROWS, D),
            *[hold(2, D // 8, FF)] * 3, *[hold(2, FF // 8, D)] * 3,
            *[hold(2, 2, 4, 16, 1024)] * 3, *[hold(2, 2, 4, 16, 1152)] * 3,
            hold(3, 4, 16, 1024), hold(3, 4, 16, 1152), hold(3, 16, 2176),
            dma((11,)), dma((4, EXPERTS)), dma((4, EXPERTS)), dma((10,)), dma((10,)),
            dma((3, 2, 3, 2)), dma((3, 2, 3, 2)), dma((2, 3)), dma((2, 3)), dma((3,)), dma((3,)),
            dma((2, 3, 2)), dma((2, 3, 2)),
        ],
        compiler_params=pltpu.CompilerParams(
            collective_id=0, has_side_effects=True, vmem_limit_bytes=62 * MIB
        ),
    )(
        mid, ids, cotangent, w_router, gain.reshape(1, D), shift.reshape(1, D), gain_attn.reshape(1, D),
        w_in, w_out, tok_t.reshape(16, 2, 32, ROWS), context_t.reshape(16, 2, 32, ROWS),
        attn_out, w_proj, qkv, probs, w_qkv,
    )


def per_device(
    tokens, w_qkv, w_proj, rel_bias, gain_attn, shift_attn, w_router, gain_moe, shift_moe, w_in, w_out, expert_ids, cotangent
):
    tok_t, qkv, probs, context_t, attn_out, mid = attend(tokens, w_qkv, w_proj, rel_bias, gain_attn, shift_attn)
    block_out, d_tokens, sum_qkv, sum_proj, sum_router, first_sum, second_sum = main(
        mid, expert_ids, cotangent, w_router, gain_moe, shift_moe, gain_attn, w_in[0], w_out[0],
        tok_t, context_t, attn_out, w_proj, qkv, probs, w_qkv,
    )
    return block_out, d_tokens, sum_qkv, sum_proj, sum_router[:, :EXPERTS], first_sum[None], second_sum[None]


def solution(mesh):
    split = P(("dp", "group", "node"), None)
    expert = P(("group", "node"), None, None)
    owned = P(("group", "node"), "dp", None)
    return jax.shard_map(
        per_device,
        mesh=mesh,
        in_specs=(split, P(), P(), P(), P(), P(), P(), P(), P(), expert, expert, split, split),
        out_specs=(split, split, split, split, split, owned, owned),
        check_vma=False,
    )
```

```python
import jax
import jax.numpy as jnp
from jax import lax
from jax.experimental import pallas as pl
from jax.experimental.pallas import tpu as pltpu
from jax.sharding import PartitionSpec as P

MESH = pl.DeviceIdType.MESH
F32 = jnp.float32
BF16 = jnp.bfloat16
MIB = 1 << 20
D = 1024
FF = 2048
HEADS = 32
HEAD_DIM = 32
WIN = 8
EXPERTS = 32
ROWS = 256
SLOTS = 20
EPS = 1e-05
NEG = -1e30
SCALE = HEAD_DIM ** (-0.5)
CHUNK = 1280
X_COLS = ((0, 256), (256, 512), (512, 1024))
Z_COLS = ((0, 256), (256, 768), (768, 1152))
BATCH = 16


def dot(a, b):
    return lax.dot_general(a, b, (((1,), (0,)), ((), ())), preferred_element_type=F32)


def dot_nt(a, b):
    return lax.dot_general(a, b, (((1,), (1,)), ((), ())), preferred_element_type=F32)


def dot_tn(a, b):
    return lax.dot_general(a, b, (((0,), (0,)), ((), ())), preferred_element_type=F32)


def iota(shape, dim):
    return lax.broadcasted_iota(jnp.int32, shape, dim)


def flag(cond):
    return jnp.where(cond, 1.0, 0.0).astype(BF16)


def split3(values):
    high = values.astype(BF16)
    rest = values - high.astype(F32)
    mid = rest.astype(BF16)
    return high, mid, (rest - mid.astype(F32)).astype(BF16)


def token_of(place):
    window, inner = place >> 6, place & 63
    row = (((window >> 1) << 3) + (inner >> 3) + WIN // 2) & 15
    col = (((window & 1) << 3) + (inner & 7) + WIN // 2) & 15
    return (row << 4) + col


def to_windows():
    return flag(iota((ROWS, ROWS), 1) == token_of(iota((ROWS, ROWS), 0)))


def from_windows():
    return flag(iota((ROWS, ROWS), 0) == token_of(iota((ROWS, ROWS), 1)))


def normalise(values):
    mean = jnp.mean(values, axis=-1, keepdims=True)
    centered = values - mean
    rstd = lax.rsqrt(jnp.mean(centered * centered, axis=-1, keepdims=True) + EPS)
    return centered * rstd, rstd


def norm_pull(unit, rstd, slope):
    return rstd * (
        slope - jnp.mean(slope, axis=-1, keepdims=True) - unit * jnp.mean(slope * unit, axis=-1, keepdims=True)
    )


def head_mask():
    return flag((iota((256, 128), 0) >> 6) == (iota((256, 128), 1) >> 5))


def by_head(ref, pair, first, mask):
    parts = []
    for side in (0, 1):
        rows = ref[pair * 128 + side * 64 : pair * 128 + side * 64 + 64, pl.ds(first, 128)]
        parts.append(jnp.concatenate([rows] * 4, axis=0) * mask)
    return jnp.concatenate(parts, axis=1)


def by_window(ref, pair, first, upper):
    rows = ref[pair * 128 : pair * 128 + 128, pl.ds(first, 128)]
    return jnp.concatenate([rows * upper, rows * (1 - upper)], axis=1)


def attend_phase(
    env, tokens_v, w_qkv_v, w_proj_v, tok_w, context, bias,
):
    (
        tokens, w_qkv, w_proj, rel_bias, gain, shift, tok_own, context_own, tok_2, context_2,
        qkv, probs, attn_out, mid, load_sem, c, small_wait,
    ) = env
    load_tokens = pltpu.make_async_copy(tokens, tokens_v, load_sem.at[0])
    load_tokens.start()
    parts = [
        pltpu.make_async_copy(
            w_qkv.at[:, pl.ds(at * D, D)], w_qkv_v.at[:, pl.ds(at * D, D)], load_sem.at[1 + at]
        )
        for at in range(3)
    ]
    parts.append(pltpu.make_async_copy(w_proj, w_proj_v, load_sem.at[4]))
    for part in parts:
        part.start()
    small_wait()

    table = jnp.concatenate(split3(rel_bias[...]), axis=0)
    entry = iota((225, 128), 0)
    query = iota((225, 128), 1) & 63

    @pl.loop(0, 16)
    def _(block):
        for inner in range(4):
            key = block * 4 + inner
            place = ((query >> 3) - (key >> 3) + WIN - 1) * (2 * WIN - 1) + (query & 7) - (key & 7) + WIN - 1
            found = dot(table, flag(entry == place))
            bias[pl.ds(key, HEADS, stride=64), :] = found[:32] + (found[32:64] + found[64:96])

    load_tokens.wait()
    tok_w[...] = dot(to_windows(), tokens_v[...]).astype(BF16)
    for at in range(6):
        cols = slice(at * 512, at * 512 + 512)
        if at % 2 == 0:
            parts[at // 2].wait()
        qkv[:ROWS, cols] = dot(tok_w[...], w_qkv_v[:, cols]).astype(BF16)
    tok_own[...] = tok_w[...].T.reshape(16, 2, 32, ROWS)
    tok_2[:, :, :ROWS] = tok_own[:, c]

    mask = head_mask()
    key = iota((256, 128), 0) & 63
    lane = iota((256, 128), 1)
    row_differs = ((key >> 5) ^ (lane >> 5)) & 1
    col_differs = ((key ^ lane) >> 2) & 1 & (lane >> 6)
    upper = flag(iota((128, 128), 0) < 64)
    for pair in range(2):
        apart = jnp.where((col_differs | (row_differs if pair else 0)) == 1, NEG, 0.0)
        for group in range(8):
            keys = by_head(qkv, pair, D + group * 128, mask)
            queries = by_window(qkv, pair, group * 128, upper)
            scores = dot_nt(keys, queries) * SCALE + bias[group * 256 : group * 256 + 256, :] + apart
            scores = scores.reshape(4, 64, 128)
            weights = jnp.exp(scores - jnp.max(scores, axis=1, keepdims=True))
            prob = (weights / jnp.sum(weights, axis=1, keepdims=True)).reshape(256, 128).astype(BF16)
            probs[pair, group] = prob
            both = dot_tn(prob, by_head(qkv, pair, 2 * D + group * 128, mask))
            for side in (0, 1):
                context[pair * 128 + side * 64 : pair * 128 + side * 64 + 64, group * 128 : group * 128 + 128] = both[
                    side * 64 : side * 64 + 64, side * 128 : side * 128 + 128
                ].astype(BF16)

    context_own[...] = context[...].T.reshape(16, 2, 32, ROWS)
    context_2[:, :, :ROWS] = context_own[:, c]
    parts[3].wait()
    projected = dot(context[...], w_proj_v[...])
    attn_out[...] = projected
    unit, _ = normalise(projected)
    mid_w = (tok_w[...].astype(F32) + (unit * gain[...] + shift[...])).astype(BF16)
    mid[...] = dot(from_windows(), mid_w).astype(BF16)


def expert_of_row(shape, dim):
    row = iota(shape, dim)
    return jnp.where(row < EXPERTS * 16, row >> 4, (row >> 2) & (EXPERTS - 1))


def rank_of_row(shape, dim):
    row = iota(shape, dim)
    return jnp.where(row < EXPERTS * 16, row & 15, 16 + (row & 3))


def fold_order(count):
    row, col = iota((16 * count, 16 * count), 0), iota((16 * count, 16 * count), 1)
    size = 4 * count
    block = sum([(row >= size * at).astype(jnp.int32) for at in (1, 2, 3)])
    inner = row - block * size
    return flag(col == ((inner >> 2) << 4) + (block << 2) + (inner & 3))


def unfold(ref, first, count, order, out, out_first):
    main = ref[first : first + count, :, :D].reshape(16 * count, D)
    rest = dot(order, ref[first : first + count, :, D:].reshape(16 * count, CHUNK - D)).astype(BF16)
    out[out_first : out_first + 16 * count, :] = main
    for block in range(4):
        out[out_first + 16 * count : out_first + 20 * count, block * 256 : block * 256 + 256] = rest[
            block * 4 * count : block * 4 * count + 4 * count
        ]


def fold(rows, count, order, ref, first):
    ref[first : first + count, :, :D] = rows[: 16 * count].astype(BF16).reshape(count, 16, D)
    rest = rows[16 * count :].astype(BF16)
    stacked = jnp.concatenate([rest[:, block * 256 : block * 256 + 256] for block in range(4)], axis=0)
    ref[first : first + count, :, D:] = dot_tn(order, stacked).astype(BF16).reshape(count, 16, CHUNK - D)


def gelu_parts(values):
    z = jnp.abs(values) * 0.7071067811865476
    t = 1.0 / (1.0 + 0.3275911 * z)
    bell = jnp.exp(-z * z)
    poly = ((((1.061405429 * t - 1.453152027) * t + 1.421413741) * t - 0.284496736) * t + 0.254829592) * t
    tail = 0.5 * poly * bell
    phi = jnp.where(values >= 0, 1.0 - tail, tail)
    return values * phi, phi + values * bell * 0.3989422804014327


def routes(me, peer, send_sem, recv_sem):
    def to_expert(route, source, target, j):
        e = lax.rem(me + j, EXPERTS)
        return pltpu.make_async_remote_copy(
            src_ref=source.at[e], dst_ref=target.at[j], send_sem=send_sem.at[route, j], recv_sem=recv_sem.at[route, j],
            device_id=peer(e), device_id_type=MESH,
        )

    def to_source(route, source, target, j):
        return pltpu.make_async_remote_copy(
            src_ref=source.at[j], dst_ref=target.at[me], send_sem=send_sem.at[route, j], recv_sem=recv_sem.at[route, j],
            device_id=peer(lax.rem(me + EXPERTS - j, EXPERTS)), device_id_type=MESH,
        )

    def start_all(make, route, source, target, first, last):
        @pl.loop(max(first, 1), last)
        def _(j):
            make(route, source, target, j).start()

    def receive(make, route, source, target, first, last):
        @pl.loop(max(first, 1), last)
        def _(j):
            make(route, source, target, j).wait_recv()

    return to_expert, to_source, start_all, receive


def expert_sums(y, sets, send_dp, recv_dp):
    up, down, far = lax.rem(y + 1, 4), lax.rem(y + 3, 4), lax.rem(y + 2, 4)

    def copy(at, kind, side):
        grad, *targets = sets[at]
        half = grad.shape[1] // 2
        upwards = (side == 0) != (kind == 1)
        block = far if kind == 0 else up if upwards else down
        return pltpu.make_async_remote_copy(
            src_ref=grad.at[block, pl.ds(side * half, half)], dst_ref=targets[kind].at[side],
            send_sem=send_dp.at[at, kind, side], recv_sem=recv_dp.at[at, kind, side],
            device_id={"dp": up if upwards else down}, device_id_type=MESH,
        )

    def start(at, kind):
        for side in (0, 1):
            copy(at, kind, side).start()

    def add_into(grad, block, first, count, more):
        step = 64

        @pl.loop(0, count // step)
        def _(i):
            here = pl.ds(pl.multiple_of(i * step, step), step)
            mine = pl.ds(pl.multiple_of(first + i * step, step), step)
            total = grad[block, mine].astype(F32)
            for other, side in more:
                total = total + other[side, here].astype(F32)
            grad[block, mine] = total.astype(BF16)

    def pass_on(at):
        grad, far_in, near_in, done_in = sets[at]
        half = grad.shape[1] // 2
        for side, block in enumerate((up, down)):
            copy(at, 0, side).wait()
            add_into(grad, block, side * half, half, ((far_in, side),))
            copy(at, 2, side).start()

    def complete(at):
        grad, far_in, near_in, done_in = sets[at]
        half = grad.shape[1] // 2
        for side in (0, 1):
            copy(at, 1, side).wait()
            copy(at, 2, side).wait()
            add_into(grad, y, side * half, half, ((near_in, side), (done_in, side)))

    return start, pass_on, complete


def experts_phase(
    env, w_first, w_second, out1, out2, rows, d_rows, hidden, slope, select, cotangent,
):
    (
        mid, ids, cot, w_router, gain, shift, w_in, w_out, block_out, in1, in2, in3, in4, out4,
        g_first, g_second, pick_sum, d_direct, router_own, router_other, load_sem, send_sem, recv_sem,
        me, y, c, peer, barrier, start_core, core_send, sums_start,
    ) = env
    load_first = pltpu.make_async_copy(w_in, w_first, load_sem.at[0])
    load_second = pltpu.make_async_copy(w_out, w_second, load_sem.at[1])
    load_cot = pltpu.make_async_copy(cot, cotangent, load_sem.at[2])
    load_first.start()
    load_second.start()
    load_cot.start()
    to_expert, to_source, start_all, receive = routes(me, peer, send_sem, recv_sem)
    back = d_rows

    expert_row = iota((EXPERTS, ROWS), 0)
    chosen = [jnp.where(ids[k : k + 1, :] == expert_row, 1.0, 0.0).T for k in range(2)]
    earlier = flag(iota((ROWS, ROWS), 0) > iota((ROWS, ROWS), 1))
    rank = dot(earlier, (chosen[0] + chosen[1]).astype(BF16)) + 1.0
    places = [(one * rank).astype(BF16) for one in chosen]
    row_experts = flag(expert_of_row((EXPERTS * SLOTS, EXPERTS), 0) == iota((EXPERTS * SLOTS, EXPERTS), 1))
    row_ranks = rank_of_row((EXPERTS * SLOTS, ROWS), 0).astype(F32) + 1.0
    for k in range(2):
        select[:, k * ROWS : k * ROWS + ROWS] = flag(dot_nt(row_experts, places[k]) == row_ranks)
    order = fold_order(EXPERTS)
    batch_order = fold_order(BATCH)

    fold(dot(select[:, :ROWS] + select[:, ROWS:], mid[...]), EXPERTS, order, out1, 0)
    pl.semaphore_wait(barrier, EXPERTS + 2)
    start_core()
    start_all(to_expert, 0, out1, in1, 1, EXPERTS)
    in1[0] = out1[me]

    router = split3(w_router[...])
    logits = dot_nt(mid[...], router[0]) + (dot_nt(mid[...], router[1]) + dot_nt(mid[...], router[2]))
    gating = []
    for k in range(2):
        logit = jnp.sum(logits * chosen[k], axis=1, keepdims=True)
        gating.append(1.0 / (1.0 + jnp.exp(-logit)))
    load_first.wait()
    load_second.wait()

    batch_rows = SLOTS * BATCH
    for batch in range(EXPERTS // BATCH):
        first, last = batch * BATCH, batch * BATCH + BATCH
        here = slice(batch * batch_rows, batch * batch_rows + batch_rows)
        receive(to_expert, 0, out1, in1, first, last)
        unfold(in1, first, BATCH, batch_order, rows, batch * batch_rows)
        for at in range(8):
            cols = slice(at * 256, at * 256 + 256)
            value, value_slope = gelu_parts(dot(rows[here, :], w_first[:, cols]))
            hidden[here, cols] = value.astype(BF16)
            slope[here, cols] = value_slope.astype(BF16)
        fold(dot(hidden[here, :], w_second[...]), BATCH, batch_order, out2, first)
        start_all(to_source, 1, out2, in2, first, last)
        if batch == 0:
            in2[me] = out2[0]

    lane_experts = flag(expert_of_row((EXPERTS * SLOTS, EXPERTS), 0) == iota((EXPERTS * SLOTS, EXPERTS), 1))
    lane_ranks = rank_of_row((ROWS, EXPERTS * SLOTS), 1).astype(F32) + 1.0
    picks = [flag(dot_nt(places[k], lane_experts) == lane_ranks) for k in range(2)]
    pick_sum[...] = picks[0] + picks[1]
    receive(to_source, 1, out2, in2, 1, EXPERTS)
    unfold(in2, 0, EXPERTS, order, back, 0)
    picked = [dot(picks[k], back[...]) for k in range(2)]
    unit, rstd = normalise(gating[0] * picked[0] + gating[1] * picked[1])
    load_cot.wait()
    d_direct[...] = cotangent[...].astype(F32)
    cotangent[...] = (mid[...].astype(F32) + (unit * gain[...] + shift[...])).astype(BF16)
    write_block = pltpu.make_async_copy(cotangent, block_out, load_sem.at[3])
    write_block.start()
    d_mixture = norm_pull(unit, rstd, d_direct[...] * gain[...])
    d_picked = jnp.concatenate([(gating[k] * d_mixture).astype(BF16) for k in range(2)], axis=0)
    @pl.loop(1, EXPERTS)
    def _(j):
        to_expert(0, out1, in1, j).wait_send()

    fold(dot(select[...], d_picked), EXPERTS, order, out1, 0)
    start_all(to_expert, 2, out1, in3, 1, EXPERTS)
    in3[0] = out1[me]

    d_logits = jnp.zeros((ROWS, EXPERTS), F32)
    for k in range(2):
        d_gating = jnp.sum(d_mixture * picked[k], axis=1, keepdims=True)
        d_logits = d_logits + chosen[k] * (d_gating * gating[k] * (1.0 - gating[k]))
    d_high = d_logits.astype(BF16)
    d_low = (d_logits - d_high.astype(F32)).astype(BF16)
    wide = [jnp.concatenate([part, jnp.zeros((ROWS, 128 - EXPERTS), BF16)], axis=1) for part in (d_high, d_low)]
    d_router = (dot_tn(mid[...], wide[0]) + dot_tn(mid[...], wide[1])).reshape(16, 2, 4, 8, 128)
    high = d_router.astype(BF16).astype(F32)
    router_own[...] = jnp.concatenate([high, d_router - high], axis=3).astype(BF16)
    core_send(lambda: (router_own.at[:, 1 - c], router_other), 2)
    from_router = dot(d_high, router[0]) + (dot(d_low, router[0]) + dot(d_high, router[1]))
    d_direct[...] += from_router

    far = lax.rem(y + 2, 4)

    def second_block(place):
        for at in range(2):
            cols = pl.ds(pl.multiple_of(place * 512 + at * 256, 256), 256)
            g_second[place, at * 256 : at * 256 + 256, :] = dot(hidden[:, cols].T, d_rows[...]).astype(BF16)

    def first_block(place):
        cols = pl.ds(pl.multiple_of(place * 256, 256), 256)
        g_first[place, :, :] = dot(rows[:, cols].T, slope[...]).astype(BF16)

    for batch in range(EXPERTS // BATCH):
        first, last = batch * BATCH, batch * BATCH + BATCH
        here = slice(batch * batch_rows, batch * batch_rows + batch_rows)
        receive(to_expert, 2, out1, in3, first, last)
        unfold(in3, first, BATCH, batch_order, d_rows, batch * batch_rows)
        if last == EXPERTS:
            second_block(far)
            sums_start(0, 0)
        for at in range(8):
            cols = slice(at * 256, at * 256 + 256)
            d_hidden = dot_nt(d_rows[here, :], w_second[cols, :])
            slope[here, cols] = (d_hidden * slope[here, cols].astype(F32)).astype(BF16)
        fold(dot_nt(slope[here, :], w_first[...]), BATCH, batch_order, out4, first)
        start_all(to_source, 3, out4, in4, first, last)
        if batch == 0:
            in4[me] = out4[0]

    second_block(lax.rem(y + 3, 4))
    second_block(lax.rem(y + 1, 4))
    sums_start(0, 1)
    first_block(far)
    sums_start(1, 0)
    first_block(lax.rem(y + 3, 4))
    first_block(lax.rem(y + 1, 4))
    sums_start(1, 1)
    second_block(y)
    first_block(y)

    @pl.loop(1, EXPERTS)
    def _(j):
        to_source(1, out2, in2, j).wait_send()
        to_expert(2, out1, in3, j).wait_send()

    write_block.wait()


def attend_back_groups(groups, qkv, probs, d_context, d_qkv):
    mask = head_mask()
    mask_f = mask.astype(F32)
    upper = flag(iota((128, 128), 0) < 64)

    def own_heads(values, side):
        return (values[:, side * 128 : side * 128 + 128] * mask_f).reshape(4, 64, 128).sum(axis=0)

    for group in groups:
        for pair in range(2):
            first = group * 128
            values = by_head(qkv, pair, 2 * D + first, mask)
            keys = by_head(qkv, pair, D + first, mask)
            queries = by_window(qkv, pair, first, upper)
            d_out = by_window(d_context, pair, first, upper)
            prob = probs[pair, group]
            d_prob = dot_nt(values, d_out)
            prob_f = prob.astype(F32)
            inner = (prob_f * d_prob).reshape(4, 64, 128).sum(axis=1, keepdims=True)
            d_score = prob_f.reshape(4, 64, 128) * (d_prob.reshape(4, 64, 128) - inner) * SCALE
            d_score = d_score.reshape(256, 128).astype(BF16)
            d_value = dot(prob, d_out)
            d_key = dot(d_score, queries)
            d_query = dot_tn(d_score, keys)
            for side in (0, 1):
                rows = slice(pair * 128 + side * 64, pair * 128 + side * 64 + 64)
                d_qkv[rows, first : first + 128] = d_query[
                    side * 64 : side * 64 + 64, side * 128 : side * 128 + 128
                ].astype(BF16)
                d_qkv[rows, D + first : D + first + 128] = own_heads(d_key, side).astype(BF16)
                d_qkv[rows, 2 * D + first : 2 * D + first + 128] = own_heads(d_value, side).astype(BF16)


def finish_phase(
    env, w_qkv, w_proj, d_context, back, d_tok_v, grad_x, grad_z, sum_x, sum_z, sum_y,
):
    (
        refs, qkv, probs, attn_out, gain_attn, d_tokens, out_qkv, out_proj, out_router, out_first, out_second,
        in4, out4, pick_sum, d_direct, router_own, router_other, tok_2, context_2, d_qkv_2, d_attn_2,
        g_first, g_second, sums_pass, sums_complete, x_far, x_near, x_done, z_far, z_near, z_done, x_recv, z_recv, y_recv,
        load_sem, send_sem, recv_sem, send_one, recv_one, send_two, recv_two, send_y, recv_y,
        me, x, y, z, c, peer, core_send, core_wait,
    ) = env
    loads = [
        pltpu.make_async_copy(source, target, load_sem.at[2 + at])
        for at, (source, target) in enumerate(zip(refs, (w_proj, w_qkv)))
    ]
    for load in loads:
        load.start()
    to_expert, to_source, start_all, receive = routes(me, peer, send_sem, recv_sem)

    def at_x(j):
        return {"group": lax.rem(x + j, 4) * 2 + c}

    def at_y(j):
        return {"dp": lax.rem(y + j, 4)}

    def at_z(j):
        return {"node": lax.rem(z + j, 4)}

    def send(src, dst, s_sem, r_sem, target):
        copy = pltpu.make_async_remote_copy(
            src_ref=src, dst_ref=dst, send_sem=s_sem, recv_sem=r_sem, device_id=target, device_id_type=MESH
        )
        copy.start()
        return copy

    rings = (
        (grad_x, x_far, x_near, x_done, sum_x, x, at_x, X_COLS, 1),
        (grad_z, z_far, z_near, z_done, sum_z, z, at_z, Z_COLS, 2),
    )

    def block_of(ref, dim, half, place, cols):
        where = [pl.ds(2 * half, 2), slice(None), slice(None), slice(None), pl.ds(cols[0], cols[1] - cols[0])]
        where[dim] = place
        return ref.at[tuple(where)]

    def ring_start(part):
        copies = []
        for ring, (grad, far_in, near_in, done_in, total, own, at, cols, dim) in enumerate(rings):
            here = cols[part]
            span = pl.ds(here[0], here[1] - here[0])
            up, down, opposite = lax.rem(own + 1, 4), lax.rem(own + 3, 4), lax.rem(own + 2, 4)
            sems = lambda kind, side: (send_one.at[part, ring, kind, side], recv_one.at[part, ring, kind, side])
            copies.append((
                send(block_of(grad, dim, 0, opposite, here), far_in.at[0, :, :, :, span], *sems(0, 0), at(1)),
                send(block_of(grad, dim, 1, opposite, here), far_in.at[1, :, :, :, span], *sems(0, 1), at(3)),
                send(block_of(grad, dim, 0, down, here), near_in.at[0, :, :, :, span], *sems(1, 0), at(3)),
                send(block_of(grad, dim, 1, up, here), near_in.at[1, :, :, :, span], *sems(1, 1), at(1)),
            ))
        return copies

    def ring_pass(part, started):
        copies = []
        for ring, (grad, far_in, near_in, done_in, total, own, at, cols, dim) in enumerate(rings):
            here = cols[part]
            span = pl.ds(here[0], here[1] - here[0])
            for side, (place, hop) in enumerate(((lax.rem(own + 1, 4), 1), (lax.rem(own + 3, 4), 3))):
                started[ring][side].wait()

                @pl.loop(0, 8)
                def _(i):
                    yi, oi = i // 4, i % 4
                    index = (2 * side + yi, place, oi) if dim == 1 else (2 * side + yi, oi, place)
                    grad[(*index, slice(None), span)] = (
                        grad[(*index, slice(None), span)].astype(F32) + far_in[side, yi, oi, :, span].astype(F32)
                    ).astype(BF16)

                copies.append(send(
                    block_of(grad, dim, side, place, here), done_in.at[side, :, :, :, span],
                    send_one.at[part, ring, 2, side], recv_one.at[part, ring, 2, side], at(hop),
                ))
        return copies

    def ring_finish(ring, started, passed):
        grad, far_in, near_in, done_in, total, own, at, cols, dim = rings[ring]
        for part in range(3):
            for side in (0, 1):
                started[part][ring][2 + side].wait()
                passed[part][2 * ring + side].wait()

        @pl.loop(0, 16)
        def _(i):
            yi, oi = i // 4, i % 4
            side, inner = yi // 2, yi % 2
            index = (yi, own, oi) if dim == 1 else (yi, oi, own)
            total[yi, oi] = (
                grad[index].astype(F32) + near_in[side, inner, oi].astype(F32) + done_in[side, inner, oi].astype(F32)
            ).astype(BF16)

    def folded(left_t, right, cols):
        parts = dot(left_t[...].reshape(512, 512), right[:, cols : cols + 512]).reshape(64, 8, 512)
        return jnp.concatenate([parts[:, :, :256], parts[:, :, 256:]], axis=1).astype(BF16).reshape(4, 4, 4, 16, 256)

    sums_pass(0)

    receive(to_source, 3, out4, in4, 1, EXPERTS)
    unfold(in4, 0, EXPERTS, fold_order(EXPERTS), back, 0)
    d_mid = (d_direct[...] + dot(pick_sum[...], back[...])).astype(BF16)
    d_mid_w = dot(to_windows(), d_mid)
    d_direct[...] = d_mid_w
    unit, rstd = normalise(attn_out[...])
    d_attn_2[:ROWS, :] = norm_pull(unit, rstd, d_mid_w * gain_attn[...]).astype(BF16)
    core_send(lambda: (d_attn_2.at[pl.ds(0, ROWS)], d_attn_2.at[pl.ds(ROWS, ROWS)]), 3)
    loads[0].wait()
    d_context[...] = dot_nt(d_attn_2[:ROWS, :], w_proj[...]).astype(BF16)

    def core_send_heads(half):
        for at in range(3):
            cols = pl.ds(at * D + half * 512, 512)
            core_send(
                lambda cols=cols: (d_qkv_2.at[pl.ds(0, ROWS), cols], d_qkv_2.at[pl.ds(ROWS, ROWS), cols]),
                4 + 3 * half + at,
            )

    started, passed = [], []
    attend_back_groups(range(4), qkv, probs, d_context, d_qkv_2)
    core_send_heads(0)
    core_wait(1)
    core_wait(3)
    grad_x[..., 0:256] = folded(context_2, d_attn_2, 0)
    grad_z[..., 0:256] = folded(context_2, d_attn_2, 512)
    started.append(ring_start(0))
    attend_back_groups(range(4, 8), qkv, probs, d_context, d_qkv_2)
    core_send_heads(1)
    core_wait(0)
    for at in range(3):
        core_wait(4 + at)
    grad_x[..., 256:512] = folded(tok_2, d_qkv_2, 0)
    grad_z[..., 256:512] = folded(tok_2, d_qkv_2, D)
    grad_z[..., 512:768] = folded(tok_2, d_qkv_2, 2 * D)
    started.append(ring_start(1))
    passed.append(ring_pass(0, started[0]))
    sums_pass(1)
    core_wait(2)
    for at in range(3):
        core_wait(7 + at)
    grad_x[..., 512:768] = folded(tok_2, d_qkv_2, 512)
    grad_x[..., 768:1024] = folded(tok_2, d_qkv_2, D + 512)
    grad_z[..., 768:1024] = folded(tok_2, d_qkv_2, 2 * D + 512)
    grad_z[..., 1024:1152] = (
        (router_own[:, c].astype(F32) + router_other[...].astype(F32)).astype(BF16).reshape(4, 4, 4, 16, 128)
    )
    started.append(ring_start(2))
    passed.append(ring_pass(1, started[1]))
    loads[1].wait()
    d_tok_w = (d_direct[...] + dot_nt(d_qkv_2[:ROWS, :], w_qkv[...])).astype(BF16)
    d_tok_v[...] = dot(from_windows(), d_tok_w).astype(BF16)
    write_tokens = pltpu.make_async_copy(d_tok_v, d_tokens, load_sem.at[4])
    write_tokens.start()
    passed.append(ring_pass(2, started[2]))

    second = []
    for ring, (total, recv, at) in enumerate(((sum_x, x_recv, at_z), (sum_z, z_recv, at_x))):
        ring_finish(ring, started, passed)
        place = (z, x)[ring]
        second.append([
            send(
                total.at[:, lax.rem(place + j, 4)], recv.at[j - 1],
                send_two.at[ring, j - 1], recv_two.at[ring, j - 1], at(j),
            )
            for j in (1, 2, 3)
        ])
    for copy in second[0] + second[1]:
        copy.wait()

    @pl.loop(0, 4)
    def _(yi):
        total_x = sum_x[yi, z].astype(F32)
        total_z = sum_z[yi, x].astype(F32)
        for j in range(3):
            total_x = total_x + x_recv[j, yi].astype(F32)
            total_z = total_z + z_recv[j, yi].astype(F32)
        sum_y[yi, :, :1024] = total_x.astype(BF16)
        sum_y[yi, :, 1024:] = total_z.astype(BF16)

    third = [
        send(sum_y.at[lax.rem(y + j, 4)], y_recv.at[j - 1], send_y.at[j - 1], recv_y.at[j - 1], at_y(j))
        for j in (1, 2, 3)
    ]
    writes = []
    for at, (grad, out) in enumerate(((g_second, out_second), (g_first, out_first))):
        sums_complete(at)
        writes.append(pltpu.make_async_copy(grad.at[y], out, load_sem.at[7 + at]))
        writes[at].start()
    for copy in third:
        copy.wait()
    total = sum_y[y].astype(F32)
    for j in range(3):
        total = total + y_recv[j].astype(F32)

    def unfolded(first):
        return jnp.concatenate([total[:8, first : first + 256], total[8:, first : first + 256]], axis=1)

    out_proj[...] = jnp.concatenate([unfolded(0), unfolded(1024)], axis=1).astype(BF16)
    out_qkv[...] = jnp.concatenate(
        [unfolded(first) for first in (256, 512, 1280, 768, 1536, 1792)], axis=1
    ).astype(BF16)
    out_router[...] = total[:8, 2048:] + total[8:, 2048:]

    @pl.loop(1, EXPERTS)
    def _(j):
        to_source(3, out4, in4, j).wait_send()

    for write in writes + [write_tokens]:
        write.wait()


def main_kernel(
    tokens, w_qkv, w_proj, rel_bias_in, gain_attn_in, shift_attn_in, router_in, gain_moe_in, shift_moe_in, w_in, w_out, ids_in,
    cotangent,
    block_out, d_tokens, out_qkv, out_proj, out_router, out_first, out_second,
    rel_bias, gain_attn, shift_attn, w_router, gain, shift, ids, tok_own, context_own, probs, attn_out, mid, small_sem,
    in1, in2, in3, in4, out4, g_first, g_second, pick_sum, d_direct, router_own, router_other,
    tok_2, context_2, d_qkv_2, d_attn_2,
    f_far, f_near, f_done, s_far, s_near, s_done,
    x_far, x_near, x_done, z_far, z_near, z_done, x_recv, z_recv, y_recv,
    load_sem, send_sem, recv_sem, send_core, recv_core, send_one, recv_one, send_two, recv_two,
    send_y, recv_y, send_dp, recv_dp,
):
    y = lax.axis_index("dp")
    g = lax.axis_index("group")
    z = lax.axis_index("node")
    x = g // 2
    c = g % 2
    me = g * 4 + z
    other = {"group": x * 2 + (1 - c)}
    qkv = d_qkv_2

    def peer(e):
        return {"group": e // 4, "node": lax.rem(e, 4)}

    barrier = pltpu.get_barrier_semaphore()

    @pl.loop(1, EXPERTS)
    def _(j):
        pl.semaphore_signal(barrier, inc=1, device_id=peer(lax.rem(me + j, EXPERTS)), device_id_type=MESH)

    for j in (1, 2, 3):
        pl.semaphore_signal(barrier, inc=1, device_id={"dp": lax.rem(y + j, 4)}, device_id_type=MESH)

    sums_start, sums_pass, sums_complete = expert_sums(
        y, ((g_second, s_far, s_near, s_done), (g_first, f_far, f_near, f_done)), send_dp, recv_dp
    )

    def core_copy(src, dst, at):
        return pltpu.make_async_remote_copy(
            src_ref=src, dst_ref=dst, send_sem=send_core.at[at], recv_sem=recv_core.at[at],
            device_id=other, device_id_type=MESH,
        )

    core_ends = {}

    def core_send(ends, at):
        core_ends[at] = ends
        core_copy(*ends(), at).start()

    def core_wait(at):
        core_copy(*core_ends[at](), at).wait()

    theirs = pl.ds(ROWS, ROWS)

    def start_core():
        for at, (source, target) in enumerate(((tok_own, tok_2), (context_own, context_2))):
            core_send(lambda source=source, target=target: (source.at[:, 1 - c], target.at[:, :, theirs]), at)

    small = [
        pltpu.make_async_copy(source, target, small_sem.at[at])
        for at, (source, target) in enumerate((
            (rel_bias_in, rel_bias), (gain_attn_in, gain_attn), (shift_attn_in, shift_attn), (router_in, w_router),
            (gain_moe_in, gain), (shift_moe_in, shift), (ids_in, ids),
        ))
    ]
    for copy in small:
        copy.start()

    def small_wait():
        for copy in small:
            copy.wait()

    attend_env = (
        tokens, w_qkv, w_proj, rel_bias, gain_attn, shift_attn, tok_own, context_own, tok_2, context_2,
        qkv, probs, attn_out, mid, load_sem, c, small_wait,
    )
    pl.run_scoped(
        lambda *scratch: attend_phase(attend_env, *scratch),
        pltpu.VMEM((ROWS, D), BF16), pltpu.VMEM((D, 3 * D), BF16), pltpu.VMEM((D, D), BF16),
        pltpu.VMEM((ROWS, D), BF16), pltpu.VMEM((ROWS, D), BF16), pltpu.VMEM((HEADS * 64, 128), F32),
    )
    first_env = (
        mid, ids, cotangent, w_router, gain, shift, w_in, w_out, block_out, in1, in2, in3, in4, out4,
        g_first, g_second, pick_sum, d_direct, router_own, router_other, load_sem, send_sem, recv_sem,
        me, y, c, peer, barrier, start_core, core_send, sums_start,
    )
    slots = EXPERTS * SLOTS
    box = pltpu.VMEM((EXPERTS, 16, CHUNK), BF16)
    pl.run_scoped(
        lambda *scratch: experts_phase(first_env, *scratch),
        pltpu.VMEM((D, FF), BF16), pltpu.VMEM((FF, D), BF16), box, box,
        pltpu.VMEM((slots, D), BF16), pltpu.VMEM((slots, D), BF16),
        pltpu.VMEM((slots, FF), BF16), pltpu.VMEM((slots, FF), BF16),
        pltpu.VMEM((slots, 2 * ROWS), BF16), pltpu.VMEM((ROWS, D), BF16),
    )
    last_env = (
        (w_proj, w_qkv), qkv, probs, attn_out,
        gain_attn, d_tokens, out_qkv, out_proj, out_router, out_first, out_second,
        in4, out4, pick_sum, d_direct, router_own, router_other, tok_2, context_2, d_qkv_2, d_attn_2,
        g_first, g_second, sums_pass, sums_complete, x_far, x_near, x_done, z_far, z_near, z_done, x_recv, z_recv, y_recv,
        load_sem, send_sem, recv_sem, send_one, recv_one, send_two, recv_two, send_y, recv_y,
        me, x, y, z, c, peer, core_send, core_wait,
    )
    pl.run_scoped(
        lambda *scratch: finish_phase(last_env, *scratch),
        pltpu.VMEM((D, 3 * D), BF16), pltpu.VMEM((D, D), BF16), pltpu.VMEM((ROWS, D), BF16),
        pltpu.VMEM((slots, D), BF16), pltpu.VMEM((ROWS, D), BF16),
        pltpu.VMEM((4, 4, 4, 16, 1024), BF16), pltpu.VMEM((4, 4, 4, 16, 1152), BF16),
        pltpu.VMEM((4, 4, 16, 1024), BF16), pltpu.VMEM((4, 4, 16, 1152), BF16), pltpu.VMEM((4, 16, 2176), BF16),
    )


def main(
    tokens, w_qkv, w_proj, rel_bias, gain_attn, shift_attn, w_router, gain_moe, shift_moe, w_in, w_out, expert_ids, cotangent
):
    vmem = pl.BlockSpec(memory_space=pltpu.VMEM)
    anywhere = pl.BlockSpec(memory_space=pl.ANY)
    dma = pltpu.SemaphoreType.DMA
    slots = EXPERTS * SLOTS

    def hold(*shape):
        return pltpu.VMEM(shape, BF16)

    box = hold(EXPERTS, 16, CHUNK)
    return pl.pallas_call(
        main_kernel,
        out_shape=(
            jax.ShapeDtypeStruct((ROWS, D), BF16),
            jax.ShapeDtypeStruct((ROWS, D), BF16),
            jax.ShapeDtypeStruct((8, 3 * D), BF16),
            jax.ShapeDtypeStruct((8, D), BF16),
            jax.ShapeDtypeStruct((8, 128), F32),
            jax.ShapeDtypeStruct((D // 4, FF), BF16),
            jax.ShapeDtypeStruct((FF // 4, D), BF16),
        ),
        in_specs=[anywhere] * 13,
        out_specs=[anywhere] * 2 + [vmem] * 3 + [anywhere] * 2,
        scratch_shapes=[
            pltpu.VMEM((HEADS, 225), F32), pltpu.VMEM((1, D), F32), pltpu.VMEM((1, D), F32), pltpu.VMEM((EXPERTS, D), F32),
            pltpu.VMEM((1, D), F32), pltpu.VMEM((1, D), F32), pltpu.VMEM((2, ROWS), jnp.int32),
            hold(16, 2, 32, ROWS), hold(16, 2, 32, ROWS), hold(2, 8, 256, 128),
            pltpu.VMEM((ROWS, D), F32), hold(ROWS, D), dma((7,)),
            box, box, box, box, box,
            hold(4, D // 4, FF), hold(4, FF // 4, D), hold(ROWS, slots), pltpu.VMEM((ROWS, D), F32),
            hold(16, 2, 4, 16, 128), hold(16, 4, 16, 128),
            hold(16, 32, 2 * ROWS), hold(16, 32, 2 * ROWS), hold(2 * ROWS, 3 * D), hold(2 * ROWS, D),
            *[hold(2, D // 8, FF)] * 3, *[hold(2, FF // 8, D)] * 3,
            *[hold(2, 2, 4, 16, 1024)] * 3, *[hold(2, 2, 4, 16, 1152)] * 3,
            hold(3, 4, 16, 1024), hold(3, 4, 16, 1152), hold(3, 16, 2176),
            dma((11,)), dma((4, EXPERTS)), dma((4, EXPERTS)), dma((10,)), dma((10,)),
            dma((3, 2, 3, 2)), dma((3, 2, 3, 2)), dma((2, 3)), dma((2, 3)), dma((3,)), dma((3,)),
            dma((2, 3, 2)), dma((2, 3, 2)),
        ],
        compiler_params=pltpu.CompilerParams(
            collective_id=0, has_side_effects=True, vmem_limit_bytes=62 * MIB
        ),
    )(
        tokens, w_qkv, w_proj, rel_bias, gain_attn.reshape(1, D), shift_attn.reshape(1, D), w_router.T,
        gain_moe.reshape(1, D), shift_moe.reshape(1, D), w_in, w_out, expert_ids.T, cotangent,
    )


def place_kernel(*refs):
    count = len(refs) // 2
    for at in range(count):
        refs[count + at][...] = refs[at][:, : refs[count + at].shape[1]]


def place(values, router):
    steps = 4
    blocks = []
    for v in values:
        by_rows = v.shape[0] >= 8 * steps * 2
        shape = (v.shape[0] // steps, v.shape[1]) if by_rows else (v.shape[0], v.shape[1] // steps)
        blocks.append(pl.BlockSpec(shape, (lambda i: (i, 0)) if by_rows else (lambda i: (0, i))))
    return pl.pallas_call(
        place_kernel,
        grid=(steps,),
        out_shape=tuple(jax.ShapeDtypeStruct(v.shape, v.dtype) for v in values) + (jax.ShapeDtypeStruct((8, EXPERTS), F32),),
        in_specs=blocks + [pl.BlockSpec((8, 128), lambda i: (0, 0))],
        out_specs=blocks + [pl.BlockSpec((8, EXPERTS), lambda i: (0, 0))],
    )(*values, router)


def per_device(
    tokens, w_qkv, w_proj, rel_bias, gain_attn, shift_attn, w_router, gain_moe, shift_moe, w_in, w_out, expert_ids, cotangent
):
    block_out, d_tokens, sum_qkv, sum_proj, sum_router, first_sum, second_sum = main(
        tokens, w_qkv, w_proj, rel_bias, gain_attn, shift_attn, w_router, gain_moe, shift_moe, w_in[0], w_out[0], expert_ids,
        cotangent,
    )
    *placed, sum_router = place((block_out, d_tokens, sum_qkv, sum_proj, first_sum, second_sum), sum_router)
    block_out, d_tokens, sum_qkv, sum_proj, first_sum, second_sum = placed
    return block_out, d_tokens, sum_qkv, sum_proj, sum_router, first_sum[None], second_sum[None]


def solution(mesh):
    split = P(("dp", "group", "node"), None)
    expert = P(("group", "node"), None, None)
    owned = P(("group", "node"), "dp", None)
    return jax.shard_map(
        per_device,
        mesh=mesh,
        in_specs=(split, P(), P(), P(), P(), P(), P(), P(), P(), expert, expert, split, split),
        out_specs=(split, split, split, split, split, owned, owned),
        check_vma=False,
    )
```

```python
import jax
import jax.numpy as jnp
from jax import lax
from jax.experimental import pallas as pl
from jax.experimental.pallas import tpu as pltpu
from jax.sharding import PartitionSpec as P

MESH = pl.DeviceIdType.MESH
F32 = jnp.float32
BF16 = jnp.bfloat16
MIB = 1 << 20
D = 1024
FF = 2048
HEADS = 32
HEAD_DIM = 32
WIN = 8
EXPERTS = 32
ROWS = 256
SLOTS = 20
EPS = 1e-05
NEG = -1e30
SCALE = HEAD_DIM ** (-0.5)
CHUNK = 1280
X_COLS = ((0, 256), (256, 512), (512, 1024))
Z_COLS = ((0, 256), (256, 768), (768, 1152))
BATCH = 16


def dot(a, b):
    return lax.dot_general(a, b, (((1,), (0,)), ((), ())), preferred_element_type=F32)


def dot_nt(a, b):
    return lax.dot_general(a, b, (((1,), (1,)), ((), ())), preferred_element_type=F32)


def dot_tn(a, b):
    return lax.dot_general(a, b, (((0,), (0,)), ((), ())), preferred_element_type=F32)


def iota(shape, dim):
    return lax.broadcasted_iota(jnp.int32, shape, dim)


def flag(cond):
    return jnp.where(cond, 1.0, 0.0).astype(BF16)


def split3(values):
    high = values.astype(BF16)
    rest = values - high.astype(F32)
    mid = rest.astype(BF16)
    return high, mid, (rest - mid.astype(F32)).astype(BF16)


def token_of(place):
    window, inner = place >> 6, place & 63
    row = (((window >> 1) << 3) + (inner >> 3) + WIN // 2) & 15
    col = (((window & 1) << 3) + (inner & 7) + WIN // 2) & 15
    return (row << 4) + col


def to_windows():
    return flag(iota((ROWS, ROWS), 1) == token_of(iota((ROWS, ROWS), 0)))


def from_windows():
    return flag(iota((ROWS, ROWS), 0) == token_of(iota((ROWS, ROWS), 1)))


def normalise(values):
    mean = jnp.mean(values, axis=-1, keepdims=True)
    centered = values - mean
    rstd = lax.rsqrt(jnp.mean(centered * centered, axis=-1, keepdims=True) + EPS)
    return centered * rstd, rstd


def norm_pull(unit, rstd, slope):
    return rstd * (
        slope - jnp.mean(slope, axis=-1, keepdims=True) - unit * jnp.mean(slope * unit, axis=-1, keepdims=True)
    )


def head_mask():
    return flag((iota((256, 128), 0) >> 6) == (iota((256, 128), 1) >> 5))


def by_head(ref, pair, first, mask):
    parts = []
    for side in (0, 1):
        rows = ref[pair * 128 + side * 64 : pair * 128 + side * 64 + 64, pl.ds(first, 128)]
        parts.append(jnp.concatenate([rows] * 4, axis=0) * mask)
    return jnp.concatenate(parts, axis=1)


def by_window(ref, pair, first, upper):
    rows = ref[pair * 128 : pair * 128 + 128, pl.ds(first, 128)]
    return jnp.concatenate([rows * upper, rows * (1 - upper)], axis=1)


def attend_phase(
    env, tokens_v, w_qkv_v, w_proj_v, tok_w, context, bias,
):
    (
        tokens, w_qkv, w_proj, rel_bias, gain, shift, tok_own, context_own, tok_2, context_2,
        qkv, probs, attn_out, mid, load_sem, c, small_wait, choices,
    ) = env
    load_tokens = pltpu.make_async_copy(tokens, tokens_v, load_sem.at[0])
    load_tokens.start()
    parts = [
        pltpu.make_async_copy(
            w_qkv.at[:, pl.ds(at * D, D)], w_qkv_v.at[:, pl.ds(at * D, D)], load_sem.at[1 + at]
        )
        for at in range(3)
    ]
    parts.append(pltpu.make_async_copy(w_proj, w_proj_v, load_sem.at[4]))
    for part in parts:
        part.start()
    def share(rows, own, others):
        halves = rows[...].T.reshape(16, 2, 32, ROWS)
        own[:, :, :ROWS] = jnp.where(c == 0, halves[:, 0], halves[:, 1])
        others[...] = jnp.where(c == 0, halves[:, 1], halves[:, 0])

    small_wait()
    choices()

    table = jnp.concatenate(split3(rel_bias[...]), axis=0)
    entry = iota((225, 128), 0)
    place = (iota((225, 128), 1) >> 3) * (2 * WIN - 1) + (iota((225, 128), 1) & 7) + WIN - 1
    low = iota((HEADS, 128), 1) < 64
    for key_col in range(WIN):
        found = dot(table, flag(entry == place - key_col))
        found = found[:32] + (found[32:64] + found[64:96])
        for key_row in range(WIN):
            first = (WIN - 1 - key_row) * WIN
            bias[pl.ds(key_row * WIN + key_col, HEADS, stride=64), :] = jnp.where(
                low, pltpu.roll(found, (128 - first) % 128, 1), pltpu.roll(found, 64 - first if first <= 64 else 192 - first, 1)
            )

    load_tokens.wait()
    tok_w[...] = dot(to_windows(), tokens_v[...]).astype(BF16)
    for at in range(6):
        cols = slice(at * 512, at * 512 + 512)
        if at % 2 == 0:
            parts[at // 2].wait()
        qkv[:ROWS, cols] = dot(tok_w[...], w_qkv_v[:, cols]).astype(BF16)
    share(tok_w, tok_2, tok_own)

    mask = head_mask()
    key = iota((256, 128), 0) & 63
    lane = iota((256, 128), 1)
    row_differs = ((key >> 5) ^ (lane >> 5)) & 1
    col_differs = ((key ^ lane) >> 2) & 1 & (lane >> 6)
    upper = flag(iota((128, 128), 0) < 64)
    for pair in range(2):
        apart = jnp.where((col_differs | (row_differs if pair else 0)) == 1, NEG, 0.0)
        for group in range(8):
            keys = by_head(qkv, pair, D + group * 128, mask)
            queries = by_window(qkv, pair, group * 128, upper)
            scores = dot_nt(keys, queries) * SCALE + bias[group * 256 : group * 256 + 256, :] + apart
            scores = scores.reshape(4, 64, 128)
            weights = jnp.exp(scores - jnp.max(scores, axis=1, keepdims=True))
            prob = (weights * (1.0 / jnp.sum(weights, axis=1, keepdims=True))).reshape(256, 128).astype(BF16)
            probs[pair, group] = prob
            both = dot_tn(prob, by_head(qkv, pair, 2 * D + group * 128, mask))
            for side in (0, 1):
                context[pair * 128 + side * 64 : pair * 128 + side * 64 + 64, group * 128 : group * 128 + 128] = both[
                    side * 64 : side * 64 + 64, side * 128 : side * 128 + 128
                ].astype(BF16)

    share(context, context_2, context_own)
    parts[3].wait()
    projected = dot(context[...], w_proj_v[...])
    attn_out[...] = projected
    unit, _ = normalise(projected)
    mid_w = (tok_w[...].astype(F32) + (unit * gain[...] + shift[...])).astype(BF16)
    mid[...] = dot(from_windows(), mid_w).astype(BF16)


def expert_of_row(shape, dim):
    row = iota(shape, dim)
    return jnp.where(row < EXPERTS * 16, row >> 4, (row >> 2) & (EXPERTS - 1))


def rank_of_row(shape, dim):
    row = iota(shape, dim)
    return jnp.where(row < EXPERTS * 16, row & 15, 16 + (row & 3))


def fold_order(count, back=False):
    row, col = iota((16 * count, 16 * count), int(back)), iota((16 * count, 16 * count), 1 - int(back))
    size = 4 * count
    block = sum([(row >= size * at).astype(jnp.int32) for at in (1, 2, 3)])
    inner = row - block * size
    return flag(col == ((inner >> 2) << 4) + (block << 2) + (inner & 3))


def unfold(ref, first, count, order, out, out_first):
    main = ref[first : first + count, :, :D].reshape(16 * count, D)
    rest = dot(order, ref[first : first + count, :, D:].reshape(16 * count, CHUNK - D)).astype(BF16)
    out[out_first : out_first + 16 * count, :] = main
    for block in range(4):
        out[out_first + 16 * count : out_first + 20 * count, block * 256 : block * 256 + 256] = rest[
            block * 4 * count : block * 4 * count + 4 * count
        ]


def fold(rows, count, order_back, ref, first):
    ref[first : first + count, :, :D] = rows[: 16 * count].astype(BF16).reshape(count, 16, D)
    rest = rows[16 * count :].astype(BF16)
    stacked = jnp.concatenate([rest[:, block * 256 : block * 256 + 256] for block in range(4)], axis=0)
    ref[first : first + count, :, D:] = dot(order_back, stacked).astype(BF16).reshape(count, 16, CHUNK - D)


def gelu_parts(values):
    z = jnp.abs(values) * 0.7071067811865476
    t = 1.0 / (1.0 + 0.3275911 * z)
    bell = jnp.exp(-z * z)
    poly = ((((1.061405429 * t - 1.453152027) * t + 1.421413741) * t - 0.284496736) * t + 0.254829592) * t
    tail = 0.5 * poly * bell
    phi = jnp.where(values >= 0, 1.0 - tail, tail)
    return values * phi, phi + values * bell * 0.3989422804014327


def routes(me, peer, send_sem, recv_sem):
    def to_expert(route, source, target, j):
        e = lax.rem(me + j, EXPERTS)
        return pltpu.make_async_remote_copy(
            src_ref=source.at[e], dst_ref=target.at[j], send_sem=send_sem.at[route, j], recv_sem=recv_sem.at[route, j],
            device_id=peer(e), device_id_type=MESH,
        )

    def to_source(route, source, target, j):
        return pltpu.make_async_remote_copy(
            src_ref=source.at[j], dst_ref=target.at[me], send_sem=send_sem.at[route, j], recv_sem=recv_sem.at[route, j],
            device_id=peer(lax.rem(me + EXPERTS - j, EXPERTS)), device_id_type=MESH,
        )

    def start_all(make, route, source, target, first, last):
        @pl.loop(max(first, 1), last)
        def _(j):
            make(route, source, target, j).start()

    def receive(make, route, source, target, first, last):
        @pl.loop(max(first, 1), last)
        def _(j):
            make(route, source, target, j).wait_recv()

    return to_expert, to_source, start_all, receive


def expert_sums(y, sets, send_dp, recv_dp):
    up, down, far = lax.rem(y + 1, 4), lax.rem(y + 3, 4), lax.rem(y + 2, 4)

    def copy(at, kind, side):
        grad, *targets = sets[at]
        half = grad.shape[1] // 2
        upwards = (side == 0) != (kind == 1)
        block = far if kind == 0 else up if upwards else down
        return pltpu.make_async_remote_copy(
            src_ref=grad.at[block, pl.ds(side * half, half)], dst_ref=targets[kind].at[side],
            send_sem=send_dp.at[at, kind, side], recv_sem=recv_dp.at[at, kind, side],
            device_id={"dp": up if upwards else down}, device_id_type=MESH,
        )

    def start(at, kind):
        for side in (0, 1):
            copy(at, kind, side).start()

    def add_into(grad, block, first, count, more):
        step = 64

        @pl.loop(0, count // step)
        def _(i):
            here = pl.ds(pl.multiple_of(i * step, step), step)
            mine = pl.ds(pl.multiple_of(first + i * step, step), step)
            total = grad[block, mine].astype(F32)
            for other, side in more:
                total = total + other[side, here].astype(F32)
            grad[block, mine] = total.astype(BF16)

    def pass_on(at):
        grad, far_in, near_in, done_in = sets[at]
        half = grad.shape[1] // 2
        for side, block in enumerate((up, down)):
            copy(at, 0, side).wait()
            add_into(grad, block, side * half, half, ((far_in, side),))
            copy(at, 2, side).start()

    def complete(at):
        grad, far_in, near_in, done_in = sets[at]
        half = grad.shape[1] // 2
        for side in (0, 1):
            copy(at, 1, side).wait()
            copy(at, 2, side).wait()
            add_into(grad, y, side * half, half, ((near_in, side), (done_in, side)))

    return start, pass_on, complete


def choices_of(ids):
    expert_row = iota((EXPERTS, ROWS), 0)
    return [jnp.where(ids[k : k + 1, :] == expert_row, 1.0, 0.0).T for k in range(2)]


def place_choices(ids, select, pick):
    chosen = choices_of(ids)
    earlier = flag(iota((ROWS, ROWS), 0) > iota((ROWS, ROWS), 1))
    rank = dot(earlier, (chosen[0] + chosen[1]).astype(BF16)) + 1.0
    places = [(one * rank).astype(BF16) for one in chosen]
    row_experts = flag(expert_of_row((EXPERTS * SLOTS, EXPERTS), 0) == iota((EXPERTS * SLOTS, EXPERTS), 1))
    row_ranks = rank_of_row((EXPERTS * SLOTS, ROWS), 0).astype(F32) + 1.0
    for k in range(2):
        select[:, k * ROWS : k * ROWS + ROWS] = flag(dot_nt(row_experts, places[k]) == row_ranks)
    lane_experts = flag(expert_of_row((EXPERTS * SLOTS, EXPERTS), 0) == iota((EXPERTS * SLOTS, EXPERTS), 1))
    lane_ranks = rank_of_row((ROWS, EXPERTS * SLOTS), 1).astype(F32) + 1.0
    for k in range(2):
        pick[:, k * EXPERTS * SLOTS : (k + 1) * EXPERTS * SLOTS] = flag(dot_nt(places[k], lane_experts) == lane_ranks)


def experts_phase(
    env, w_first, w_second, out1, out2, rows, d_rows, hidden, slope, cotangent,
):
    (
        mid, ids, select, pick, cot, w_router, gain, shift, w_in, w_out, block_out, in1, in2, in3, out4,
        g_first, g_second, d_direct, router_own, router_other, load_sem, send_sem, recv_sem,
        me, y, c, peer, barrier, start_core, core_send, sums_start,
    ) = env
    load_first = pltpu.make_async_copy(w_in, w_first, load_sem.at[0])
    load_second = pltpu.make_async_copy(w_out, w_second, load_sem.at[1])
    load_cot = pltpu.make_async_copy(cot, cotangent, load_sem.at[2])
    load_first.start()
    load_second.start()
    load_cot.start()
    to_expert, to_source, start_all, receive = routes(me, peer, send_sem, recv_sem)
    back = d_rows
    chosen = choices_of(ids)

    order = fold_order(EXPERTS)
    batch_order = fold_order(BATCH)
    order_back = fold_order(EXPERTS, back=True)
    batch_back = fold_order(BATCH, back=True)

    fold(dot(select[:, :ROWS] + select[:, ROWS:], mid[...]), EXPERTS, order_back, out1, 0)
    pl.semaphore_wait(barrier, EXPERTS + 2)
    start_core()
    start_all(to_expert, 0, out1, in1, 1, EXPERTS)
    in1[0] = out1[me]

    router = split3(w_router[...])
    logits = dot_nt(mid[...], router[0]) + (dot_nt(mid[...], router[1]) + dot_nt(mid[...], router[2]))
    gating = []
    for k in range(2):
        logit = jnp.sum(logits * chosen[k], axis=1, keepdims=True)
        gating.append(1.0 / (1.0 + jnp.exp(-logit)))
    load_first.wait()
    load_second.wait()

    batch_rows = SLOTS * BATCH
    for batch in range(EXPERTS // BATCH):
        first, last = batch * BATCH, batch * BATCH + BATCH
        here = slice(batch * batch_rows, batch * batch_rows + batch_rows)
        receive(to_expert, 0, out1, in1, first, last)
        unfold(in1, first, BATCH, batch_order, rows, batch * batch_rows)
        for at in range(8):
            cols = slice(at * 256, at * 256 + 256)
            value, value_slope = gelu_parts(dot(rows[here, :], w_first[:, cols]))
            hidden[here, cols] = value.astype(BF16)
            slope[here, cols] = value_slope.astype(BF16)
        fold(dot(hidden[here, :], w_second[...]), BATCH, batch_back, out2, first)
        start_all(to_source, 1, out2, in2, first, last)
        if batch == 0:
            in2[me] = out2[0]

    picks = [pick[:, k * EXPERTS * SLOTS : (k + 1) * EXPERTS * SLOTS] for k in range(2)]
    receive(to_source, 1, out2, in2, 1, EXPERTS)
    unfold(in2, 0, EXPERTS, order, back, 0)
    picked = [dot(picks[k], back[...]) for k in range(2)]
    unit, rstd = normalise(gating[0] * picked[0] + gating[1] * picked[1])
    load_cot.wait()
    d_mixture = norm_pull(unit, rstd, cotangent[...].astype(F32) * gain[...])
    d_picked = jnp.concatenate([(gating[k] * d_mixture).astype(BF16) for k in range(2)], axis=0)
    @pl.loop(1, EXPERTS)
    def _(j):
        to_expert(0, out1, in1, j).wait_send()

    fold(dot(select[...], d_picked), EXPERTS, order_back, out1, 0)
    start_all(to_expert, 2, out1, in3, 1, EXPERTS)
    in3[0] = out1[me]

    d_direct[...] = cotangent[...].astype(F32)
    cotangent[...] = (mid[...].astype(F32) + (unit * gain[...] + shift[...])).astype(BF16)
    write_block = pltpu.make_async_copy(cotangent, block_out, load_sem.at[3])
    write_block.start()

    d_logits = jnp.zeros((ROWS, EXPERTS), F32)
    for k in range(2):
        d_gating = jnp.sum(d_mixture * picked[k], axis=1, keepdims=True)
        d_logits = d_logits + chosen[k] * (d_gating * gating[k] * (1.0 - gating[k]))
    d_high = d_logits.astype(BF16)
    d_low = (d_logits - d_high.astype(F32)).astype(BF16)
    wide = [jnp.concatenate([part, jnp.zeros((ROWS, 128 - EXPERTS), BF16)], axis=1) for part in (d_high, d_low)]
    d_router = (dot_tn(mid[...], wide[0]) + dot_tn(mid[...], wide[1])).reshape(16, 2, 4, 8, 128)
    high = d_router.astype(BF16).astype(F32)
    router_own[...] = jnp.concatenate([high, d_router - high], axis=3).astype(BF16)
    core_send(lambda: (router_own.at[:, 1 - c], router_other), 2)
    from_router = dot(d_high, router[0]) + (dot(d_low, router[0]) + dot(d_high, router[1]))
    d_direct[...] += from_router

    far = lax.rem(y + 2, 4)

    def second_block(place):
        for at in range(2):
            cols = pl.ds(pl.multiple_of(place * 512 + at * 256, 256), 256)
            g_second[place, at * 256 : at * 256 + 256, :] = dot(hidden[:, cols].T, d_rows[...]).astype(BF16)

    def first_block(place):
        cols = pl.ds(pl.multiple_of(place * 256, 256), 256)
        g_first[place, :, :] = dot(rows[:, cols].T, slope[...]).astype(BF16)

    for batch in range(EXPERTS // BATCH):
        first, last = batch * BATCH, batch * BATCH + BATCH
        here = slice(batch * batch_rows, batch * batch_rows + batch_rows)
        receive(to_expert, 2, out1, in3, first, last)
        unfold(in3, first, BATCH, batch_order, d_rows, batch * batch_rows)
        if last == EXPERTS:
            second_block(far)
            sums_start(0, 0)
        for at in range(8):
            cols = slice(at * 256, at * 256 + 256)
            d_hidden = dot_nt(d_rows[here, :], w_second[cols, :])
            slope[here, cols] = (d_hidden * slope[here, cols].astype(F32)).astype(BF16)
        fold(dot_nt(slope[here, :], w_first[...]), BATCH, batch_back, out4, first)
        start_all(to_source, 3, out4, in2, first, last)
        if batch == 0:
            in2[me] = out4[0]

    second_block(lax.rem(y + 3, 4))
    second_block(lax.rem(y + 1, 4))
    sums_start(0, 1)
    first_block(far)
    sums_start(1, 0)
    first_block(lax.rem(y + 3, 4))
    first_block(lax.rem(y + 1, 4))
    sums_start(1, 1)
    second_block(y)
    first_block(y)

    @pl.loop(1, EXPERTS)
    def _(j):
        to_source(1, out2, in2, j).wait_send()
        to_expert(2, out1, in3, j).wait_send()

    write_block.wait()


def attend_back_groups(groups, qkv, probs, d_context, d_qkv):
    mask = head_mask()
    mask_f = mask.astype(F32)
    upper = flag(iota((128, 128), 0) < 64)

    def own_heads(values, side):
        return (values[:, side * 128 : side * 128 + 128] * mask_f).reshape(4, 64, 128).sum(axis=0)

    for group in groups:
        for pair in range(2):
            first = group * 128
            values = by_head(qkv, pair, 2 * D + first, mask)
            keys = by_head(qkv, pair, D + first, mask)
            queries = by_window(qkv, pair, first, upper)
            d_out = by_window(d_context, pair, first, upper)
            prob = probs[pair, group]
            d_prob = dot_nt(values, d_out)
            prob_f = prob.astype(F32)
            inner = (prob_f * d_prob).reshape(4, 64, 128).sum(axis=1, keepdims=True)
            d_score = prob_f.reshape(4, 64, 128) * (d_prob.reshape(4, 64, 128) - inner) * SCALE
            d_score = d_score.reshape(256, 128).astype(BF16)
            d_value = dot(prob, d_out)
            d_key = dot(d_score, queries)
            d_query = dot_tn(d_score, keys)
            for side in (0, 1):
                rows = slice(pair * 128 + side * 64, pair * 128 + side * 64 + 64)
                d_qkv[rows, first : first + 128] = d_query[
                    side * 64 : side * 64 + 64, side * 128 : side * 128 + 128
                ].astype(BF16)
                d_qkv[rows, D + first : D + first + 128] = own_heads(d_key, side).astype(BF16)
                d_qkv[rows, 2 * D + first : 2 * D + first + 128] = own_heads(d_value, side).astype(BF16)


def finish_phase(
    env, w_qkv, w_proj, d_context, back, d_tok_v, grad_x, grad_z, sum_x, sum_z, sum_y,
):
    (
        refs, qkv, probs, attn_out, gain_attn, d_tokens, out_qkv, out_proj, out_router, out_first, out_second,
        in2, out4, pick, d_direct, router_own, router_other, tok_2, context_2, d_qkv_2, d_attn_2,
        g_first, g_second, sums_pass, sums_complete, x_far, x_near, x_done, z_far, z_near, z_done, x_recv, z_recv, y_recv,
        load_sem, send_sem, recv_sem, send_one, recv_one, send_two, recv_two, send_y, recv_y,
        me, x, y, z, c, peer, core_send, core_wait,
    ) = env
    loads = [
        pltpu.make_async_copy(source, target, load_sem.at[2 + at])
        for at, (source, target) in enumerate(zip(refs, (w_proj, w_qkv)))
    ]
    for load in loads:
        load.start()
    to_expert, to_source, start_all, receive = routes(me, peer, send_sem, recv_sem)

    def at_x(j):
        return {"group": lax.rem(x + j, 4) * 2 + c}

    def at_y(j):
        return {"dp": lax.rem(y + j, 4)}

    def at_z(j):
        return {"node": lax.rem(z + j, 4)}

    def send(src, dst, s_sem, r_sem, target):
        copy = pltpu.make_async_remote_copy(
            src_ref=src, dst_ref=dst, send_sem=s_sem, recv_sem=r_sem, device_id=target, device_id_type=MESH
        )
        copy.start()
        return copy

    rings = (
        (grad_x, x_far, x_near, x_done, sum_x, x, at_x, X_COLS, 1),
        (grad_z, z_far, z_near, z_done, sum_z, z, at_z, Z_COLS, 2),
    )

    def block_of(ref, dim, half, place, cols):
        where = [pl.ds(2 * half, 2), slice(None), slice(None), slice(None), pl.ds(cols[0], cols[1] - cols[0])]
        where[dim] = place
        return ref.at[tuple(where)]

    def ring_start(part):
        copies = []
        for ring, (grad, far_in, near_in, done_in, total, own, at, cols, dim) in enumerate(rings):
            here = cols[part]
            span = pl.ds(here[0], here[1] - here[0])
            up, down, opposite = lax.rem(own + 1, 4), lax.rem(own + 3, 4), lax.rem(own + 2, 4)
            sems = lambda kind, side: (send_one.at[part, ring, kind, side], recv_one.at[part, ring, kind, side])
            copies.append((
                send(block_of(grad, dim, 0, opposite, here), far_in.at[0, :, :, :, span], *sems(0, 0), at(1)),
                send(block_of(grad, dim, 1, opposite, here), far_in.at[1, :, :, :, span], *sems(0, 1), at(3)),
                send(block_of(grad, dim, 0, down, here), near_in.at[0, :, :, :, span], *sems(1, 0), at(3)),
                send(block_of(grad, dim, 1, up, here), near_in.at[1, :, :, :, span], *sems(1, 1), at(1)),
            ))
        return copies

    def ring_pass(part, started):
        copies = []
        for ring, (grad, far_in, near_in, done_in, total, own, at, cols, dim) in enumerate(rings):
            here = cols[part]
            span = pl.ds(here[0], here[1] - here[0])
            for side, (place, hop) in enumerate(((lax.rem(own + 1, 4), 1), (lax.rem(own + 3, 4), 3))):
                started[ring][side].wait()

                @pl.loop(0, 8)
                def _(i):
                    yi, oi = i // 4, i % 4
                    index = (2 * side + yi, place, oi) if dim == 1 else (2 * side + yi, oi, place)
                    grad[(*index, slice(None), span)] = (
                        grad[(*index, slice(None), span)].astype(F32) + far_in[side, yi, oi, :, span].astype(F32)
                    ).astype(BF16)

                copies.append(send(
                    block_of(grad, dim, side, place, here), done_in.at[side, :, :, :, span],
                    send_one.at[part, ring, 2, side], recv_one.at[part, ring, 2, side], at(hop),
                ))
        return copies

    def ring_finish(part, started, passed):
        copies = []
        for ring, (grad, far_in, near_in, done_in, total, own, at, cols, dim) in enumerate(rings):
            span = pl.ds(cols[part][0], cols[part][1] - cols[part][0])
            for side in (0, 1):
                started[ring][2 + side].wait()
                passed[2 * ring + side].wait()

            @pl.loop(0, 16)
            def _(i):
                yi, oi = i // 4, i % 4
                side, inner = yi // 2, yi % 2
                index = (yi, own, oi) if dim == 1 else (yi, oi, own)
                total[yi, oi, :, span] = (
                    grad[(*index, slice(None), span)].astype(F32)
                    + near_in[side, inner, oi, :, span].astype(F32)
                    + done_in[side, inner, oi, :, span].astype(F32)
                ).astype(BF16)

            recv, place, hop = ((x_recv, z, at_z), (z_recv, x, at_x))[ring]
            copies += [
                send(
                    total.at[:, lax.rem(place + j, 4), :, span], recv.at[j - 1, :, :, span],
                    send_two.at[part, ring, j - 1], recv_two.at[part, ring, j - 1], hop(j),
                )
                for j in (1, 2, 3)
            ]
        return copies

    def folded(left_t, right, cols):
        parts = dot(left_t[...].reshape(512, 512), right[:, cols : cols + 512]).reshape(64, 8, 512)
        return jnp.concatenate([parts[:, :, :256], parts[:, :, 256:]], axis=1).astype(BF16).reshape(4, 4, 4, 16, 256)

    sums_pass(0)

    receive(to_source, 3, out4, in2, 1, EXPERTS)
    unfold(in2, 0, EXPERTS, fold_order(EXPERTS), back, 0)
    d_mid = (d_direct[...] + dot(pick[:, : EXPERTS * SLOTS] + pick[:, EXPERTS * SLOTS :], back[...])).astype(BF16)
    d_mid_w = dot(to_windows(), d_mid)
    d_direct[...] = d_mid_w
    unit, rstd = normalise(attn_out[...])
    d_attn_2[:ROWS, :] = norm_pull(unit, rstd, d_mid_w * gain_attn[...]).astype(BF16)
    core_send(lambda: (d_attn_2.at[pl.ds(0, ROWS)], d_attn_2.at[pl.ds(ROWS, ROWS)]), 3)
    loads[0].wait()
    d_context[...] = dot_nt(d_attn_2[:ROWS, :], w_proj[...]).astype(BF16)

    def core_send_heads(half):
        for at in range(3):
            cols = pl.ds(at * D + half * 512, 512)
            core_send(
                lambda cols=cols: (d_qkv_2.at[pl.ds(0, ROWS), cols], d_qkv_2.at[pl.ds(ROWS, ROWS), cols]),
                4 + 3 * half + at,
            )

    started, passed = [], []
    attend_back_groups(range(4), qkv, probs, d_context, d_qkv_2)
    core_send_heads(0)
    core_wait(1)
    core_wait(3)
    grad_x[..., 0:256] = folded(context_2, d_attn_2, 0)
    grad_z[..., 0:256] = folded(context_2, d_attn_2, 512)
    started.append(ring_start(0))
    attend_back_groups(range(4, 8), qkv, probs, d_context, d_qkv_2)
    core_send_heads(1)
    core_wait(0)
    for at in range(3):
        core_wait(4 + at)
    grad_x[..., 256:512] = folded(tok_2, d_qkv_2, 0)
    grad_z[..., 256:512] = folded(tok_2, d_qkv_2, D)
    grad_z[..., 512:768] = folded(tok_2, d_qkv_2, 2 * D)
    started.append(ring_start(1))
    passed.append(ring_pass(0, started[0]))
    core_wait(2)
    for at in range(3):
        core_wait(7 + at)
    grad_x[..., 512:768] = folded(tok_2, d_qkv_2, 512)
    grad_x[..., 768:1024] = folded(tok_2, d_qkv_2, D + 512)
    grad_z[..., 768:1024] = folded(tok_2, d_qkv_2, 2 * D + 512)
    grad_z[..., 1024:1152] = (
        (router_own[:, c].astype(F32) + router_other[...].astype(F32)).astype(BF16).reshape(4, 4, 4, 16, 128)
    )
    started.append(ring_start(2))
    passed.append(ring_pass(1, started[1]))
    second = ring_finish(0, started[0], passed[0])
    loads[1].wait()
    d_tok_w = (d_direct[...] + dot_nt(d_qkv_2[:ROWS, :], w_qkv[...])).astype(BF16)
    d_tok_v[...] = dot(from_windows(), d_tok_w).astype(BF16)
    write_tokens = pltpu.make_async_copy(d_tok_v, d_tokens, load_sem.at[4])
    write_tokens.start()
    sums_pass(1)
    passed.append(ring_pass(2, started[2]))
    second += ring_finish(1, started[1], passed[1])
    second += ring_finish(2, started[2], passed[2])
    for copy in second:
        copy.wait()

    @pl.loop(0, 4)
    def _(yi):
        total_x = sum_x[yi, z].astype(F32)
        total_z = sum_z[yi, x].astype(F32)
        for j in range(3):
            total_x = total_x + x_recv[j, yi].astype(F32)
            total_z = total_z + z_recv[j, yi].astype(F32)
        sum_y[yi, :, :1024] = total_x.astype(BF16)
        sum_y[yi, :, 1024:] = total_z.astype(BF16)

    third = [
        send(sum_y.at[lax.rem(y + j, 4)], y_recv.at[j - 1], send_y.at[j - 1], recv_y.at[j - 1], at_y(j))
        for j in (1, 2, 3)
    ]
    def complete(at):
        grad, out = ((g_second, out_second), (g_first, out_first))[at]
        sums_complete(at)
        write = pltpu.make_async_copy(grad.at[y], out, load_sem.at[7 + at])
        write.start()
        return write

    writes = [complete(0)]
    for copy in third:
        copy.wait()
    total = sum_y[y].astype(F32)
    for j in range(3):
        total = total + y_recv[j].astype(F32)

    def unfolded(first):
        return jnp.concatenate([total[:8, first : first + 256], total[8:, first : first + 256]], axis=1)

    out_proj[...] = jnp.concatenate([unfolded(0), unfolded(1024)], axis=1).astype(BF16)
    out_qkv[...] = jnp.concatenate(
        [unfolded(first) for first in (256, 512, 1280, 768, 1536, 1792)], axis=1
    ).astype(BF16)
    out_router[...] = total[:8, 2048:] + total[8:, 2048:]
    writes.append(complete(1))

    @pl.loop(1, EXPERTS)
    def _(j):
        to_source(3, out4, in2, j).wait_send()

    for write in writes + [write_tokens]:
        write.wait()


def main_kernel(
    tokens, w_qkv, w_proj, rel_bias_in, gain_attn_in, shift_attn_in, router_in, gain_moe_in, shift_moe_in, w_in, w_out, ids_in,
    cotangent,
    block_out, d_tokens, out_qkv, out_proj, out_router, out_first, out_second,
    rel_bias, gain_attn, shift_attn, w_router, gain, shift, ids, tok_own, context_own, probs, attn_out, mid, small_sem, select, pick,
    in1, in2, in3, out4, g_first, g_second, d_direct, router_own, router_other,
    tok_2, context_2, d_qkv_2, d_attn_2,
    f_far, f_near, f_done, s_far, s_near, s_done,
    x_far, x_near, x_done, z_far, z_near, z_done, x_recv, z_recv, y_recv,
    load_sem, send_sem, recv_sem, send_core, recv_core, send_one, recv_one, send_two, recv_two,
    send_y, recv_y, send_dp, recv_dp,
):
    y = lax.axis_index("dp")
    g = lax.axis_index("group")
    z = lax.axis_index("node")
    x = g // 2
    c = g % 2
    me = g * 4 + z
    other = {"group": x * 2 + (1 - c)}
    qkv = d_qkv_2

    def peer(e):
        return {"group": e // 4, "node": lax.rem(e, 4)}

    barrier = pltpu.get_barrier_semaphore()

    @pl.loop(1, EXPERTS)
    def _(j):
        pl.semaphore_signal(barrier, inc=1, device_id=peer(lax.rem(me + j, EXPERTS)), device_id_type=MESH)

    for j in (1, 2, 3):
        pl.semaphore_signal(barrier, inc=1, device_id={"dp": lax.rem(y + j, 4)}, device_id_type=MESH)

    sums_start, sums_pass, sums_complete = expert_sums(
        y, ((g_second, s_far, s_near, s_done), (g_first, f_far, f_near, f_done)), send_dp, recv_dp
    )

    def core_copy(src, dst, at):
        return pltpu.make_async_remote_copy(
            src_ref=src, dst_ref=dst, send_sem=send_core.at[at], recv_sem=recv_core.at[at],
            device_id=other, device_id_type=MESH,
        )

    core_ends = {}

    def core_send(ends, at):
        core_ends[at] = ends
        core_copy(*ends(), at).start()

    def core_wait(at):
        core_copy(*core_ends[at](), at).wait()

    theirs = pl.ds(ROWS, ROWS)

    def start_core():
        for at, (source, target) in enumerate(((tok_own, tok_2), (context_own, context_2))):
            core_send(lambda source=source, target=target: (source, target.at[:, :, theirs]), at)

    small = [
        pltpu.make_async_copy(source, target, small_sem.at[at])
        for at, (source, target) in enumerate((
            (rel_bias_in, rel_bias), (gain_attn_in, gain_attn), (shift_attn_in, shift_attn), (router_in, w_router),
            (gain_moe_in, gain), (shift_moe_in, shift), (ids_in, ids),
        ))
    ]
    for copy in small:
        copy.start()

    def small_wait():
        for copy in small:
            copy.wait()

    attend_env = (
        tokens, w_qkv, w_proj, rel_bias, gain_attn, shift_attn, tok_own, context_own, tok_2, context_2,
        qkv, probs, attn_out, mid, load_sem, c, small_wait, lambda: place_choices(ids, select, pick),
    )
    pl.run_scoped(
        lambda *scratch: attend_phase(attend_env, *scratch),
        pltpu.VMEM((ROWS, D), BF16), pltpu.VMEM((D, 3 * D), BF16), pltpu.VMEM((D, D), BF16),
        pltpu.VMEM((ROWS, D), BF16), pltpu.VMEM((ROWS, D), BF16), pltpu.VMEM((HEADS * 64, 128), F32),
    )
    first_env = (
        mid, ids, select, pick, cotangent, w_router, gain, shift, w_in, w_out, block_out, in1, in2, in3, out4,
        g_first, g_second, d_direct, router_own, router_other, load_sem, send_sem, recv_sem,
        me, y, c, peer, barrier, start_core, core_send, sums_start,
    )
    slots = EXPERTS * SLOTS
    box = pltpu.VMEM((EXPERTS, 16, CHUNK), BF16)
    pl.run_scoped(
        lambda *scratch: experts_phase(first_env, *scratch),
        pltpu.VMEM((D, FF), BF16), pltpu.VMEM((FF, D), BF16), box, box,
        pltpu.VMEM((slots, D), BF16), pltpu.VMEM((slots, D), BF16),
        pltpu.VMEM((slots, FF), BF16), pltpu.VMEM((slots, FF), BF16),
        pltpu.VMEM((ROWS, D), BF16),
    )
    last_env = (
        (w_proj, w_qkv), qkv, probs, attn_out,
        gain_attn, d_tokens, out_qkv, out_proj, out_router, out_first, out_second,
        in2, out4, pick, d_direct, router_own, router_other, tok_2, context_2, d_qkv_2, d_attn_2,
        g_first, g_second, sums_pass, sums_complete, x_far, x_near, x_done, z_far, z_near, z_done, x_recv, z_recv, y_recv,
        load_sem, send_sem, recv_sem, send_one, recv_one, send_two, recv_two, send_y, recv_y,
        me, x, y, z, c, peer, core_send, core_wait,
    )
    pl.run_scoped(
        lambda *scratch: finish_phase(last_env, *scratch),
        pltpu.VMEM((D, 3 * D), BF16), pltpu.VMEM((D, D), BF16), pltpu.VMEM((ROWS, D), BF16),
        pltpu.VMEM((slots, D), BF16), pltpu.VMEM((ROWS, D), BF16),
        pltpu.VMEM((4, 4, 4, 16, 1024), BF16), pltpu.VMEM((4, 4, 4, 16, 1152), BF16),
        pltpu.VMEM((4, 4, 16, 1024), BF16), pltpu.VMEM((4, 4, 16, 1152), BF16), pltpu.VMEM((4, 16, 2176), BF16),
    )


def main(
    tokens, w_qkv, w_proj, rel_bias, gain_attn, shift_attn, w_router, gain_moe, shift_moe, w_in, w_out, expert_ids, cotangent
):
    vmem = pl.BlockSpec(memory_space=pltpu.VMEM)
    anywhere = pl.BlockSpec(memory_space=pl.ANY)
    dma = pltpu.SemaphoreType.DMA
    slots = EXPERTS * SLOTS

    def hold(*shape):
        return pltpu.VMEM(shape, BF16)

    box = hold(EXPERTS, 16, CHUNK)
    return pl.pallas_call(
        main_kernel,
        out_shape=(
            jax.ShapeDtypeStruct((ROWS, D), BF16),
            jax.ShapeDtypeStruct((ROWS, D), BF16),
            jax.ShapeDtypeStruct((8, 3 * D), BF16),
            jax.ShapeDtypeStruct((8, D), BF16),
            jax.ShapeDtypeStruct((8, 128), F32),
            jax.ShapeDtypeStruct((D // 4, FF), BF16),
            jax.ShapeDtypeStruct((FF // 4, D), BF16),
        ),
        in_specs=[anywhere] * 13,
        out_specs=[anywhere] * 2 + [vmem] * 3 + [anywhere] * 2,
        scratch_shapes=[
            pltpu.VMEM((HEADS, 225), F32), pltpu.VMEM((1, D), F32), pltpu.VMEM((1, D), F32), pltpu.VMEM((EXPERTS, D), F32),
            pltpu.VMEM((1, D), F32), pltpu.VMEM((1, D), F32), pltpu.VMEM((2, ROWS), jnp.int32),
            hold(16, 32, ROWS), hold(16, 32, ROWS), hold(2, 8, 256, 128),
            pltpu.VMEM((ROWS, D), F32), hold(ROWS, D), dma((7,)),
            hold(slots, 2 * ROWS), hold(ROWS, 2 * slots),
            box, box, box, box,
            hold(4, D // 4, FF), hold(4, FF // 4, D), pltpu.VMEM((ROWS, D), F32),
            hold(16, 2, 4, 16, 128), hold(16, 4, 16, 128),
            hold(16, 32, 2 * ROWS), hold(16, 32, 2 * ROWS), hold(2 * ROWS, 3 * D), hold(2 * ROWS, D),
            *[hold(2, D // 8, FF)] * 3, *[hold(2, FF // 8, D)] * 3,
            *[hold(2, 2, 4, 16, 1024)] * 3, *[hold(2, 2, 4, 16, 1152)] * 3,
            hold(3, 4, 16, 1024), hold(3, 4, 16, 1152), hold(3, 16, 2176),
            dma((11,)), dma((4, EXPERTS)), dma((4, EXPERTS)), dma((10,)), dma((10,)),
            dma((3, 2, 3, 2)), dma((3, 2, 3, 2)), dma((3, 2, 3)), dma((3, 2, 3)), dma((3,)), dma((3,)),
            dma((2, 3, 2)), dma((2, 3, 2)),
        ],
        compiler_params=pltpu.CompilerParams(
            collective_id=0, has_side_effects=True, vmem_limit_bytes=62 * MIB
        ),
    )(
        tokens, w_qkv, w_proj, rel_bias, gain_attn.reshape(1, D), shift_attn.reshape(1, D), w_router.T,
        gain_moe.reshape(1, D), shift_moe.reshape(1, D), w_in, w_out, expert_ids.T, cotangent,
    )


def place_kernel(*refs):
    count = (len(refs) - 2) // 3
    sources, targets, held, (narrow, sems) = refs[:count], refs[count : 2 * count], refs[2 * count : 3 * count], refs[3 * count :]
    reads = [pltpu.make_async_copy(sources[at], held[at], sems.at[0, at]) for at in range(count)]
    for read in reads:
        read.start()
    writes = []
    for at in range(count):
        reads[at].wait()
        source = held[at]
        if at == count - 1:
            narrow[...] = held[at][:, :EXPERTS]
            source = narrow
        writes.append(pltpu.make_async_copy(source, targets[at], sems.at[1, at]))
        writes[at].start()
    for write in writes:
        write.wait()


def place(*values):
    anywhere = pl.BlockSpec(memory_space=pl.ANY)
    count = len(values)
    return pl.pallas_call(
        place_kernel,
        out_shape=tuple(jax.ShapeDtypeStruct(v.shape, v.dtype) for v in values[:-1]) + (jax.ShapeDtypeStruct((8, EXPERTS), F32),),
        in_specs=[anywhere] * count,
        out_specs=[anywhere] * count,
        scratch_shapes=[pltpu.VMEM(v.shape, v.dtype) for v in values]
        + [pltpu.VMEM((8, EXPERTS), F32), pltpu.SemaphoreType.DMA((2, count))],
        compiler_params=pltpu.CompilerParams(vmem_limit_bytes=62 * MIB),
    )(*values)


def per_device(
    tokens, w_qkv, w_proj, rel_bias, gain_attn, shift_attn, w_router, gain_moe, shift_moe, w_in, w_out, expert_ids, cotangent
):
    block_out, d_tokens, sum_qkv, sum_proj, sum_router, first_sum, second_sum = main(
        tokens, w_qkv, w_proj, rel_bias, gain_attn, shift_attn, w_router, gain_moe, shift_moe, w_in[0], w_out[0], expert_ids,
        cotangent,
    )
    block_out, d_tokens, sum_qkv, sum_proj, first_sum, second_sum, sum_router = place(
        block_out, d_tokens, sum_qkv, sum_proj, first_sum, second_sum, sum_router
    )
    return block_out, d_tokens, sum_qkv, sum_proj, sum_router, first_sum[None], second_sum[None]


def solution(mesh):
    split = P(("dp", "group", "node"), None)
    expert = P(("group", "node"), None, None)
    owned = P(("group", "node"), "dp", None)
    return jax.shard_map(
        per_device,
        mesh=mesh,
        in_specs=(split, P(), P(), P(), P(), P(), P(), P(), P(), expert, expert, split, split),
        out_specs=(split, split, split, split, split, owned, owned),
        check_vma=False,
    )
```

```python
import jax
import jax.numpy as jnp
from jax import lax
from jax.experimental import pallas as pl
from jax.experimental.pallas import tpu as pltpu
from jax.sharding import PartitionSpec as P

MESH = pl.DeviceIdType.MESH
F32 = jnp.float32
BF16 = jnp.bfloat16
MIB = 1 << 20
D = 1024
FF = 2048
HEADS = 32
HEAD_DIM = 32
WIN = 8
EXPERTS = 32
ROWS = 256
SLOTS = 20
EPS = 1e-05
NEG = -1e30
SCALE = HEAD_DIM ** (-0.5)
CHUNK = 1280
X_COLS = ((0, 256), (256, 512), (512, 1024))
Z_COLS = ((0, 256), (256, 768), (768, 1152))
BATCHES = ((0, 8), (8, 16), (16, 32))


def dot(a, b):
    return lax.dot_general(a, b, (((1,), (0,)), ((), ())), preferred_element_type=F32)


def dot_nt(a, b):
    return lax.dot_general(a, b, (((1,), (1,)), ((), ())), preferred_element_type=F32)


def dot_tn(a, b):
    return lax.dot_general(a, b, (((0,), (0,)), ((), ())), preferred_element_type=F32)


def iota(shape, dim):
    return lax.broadcasted_iota(jnp.int32, shape, dim)


def flag(cond):
    return jnp.where(cond, 1.0, 0.0).astype(BF16)


def split3(values):
    high = values.astype(BF16)
    rest = values - high.astype(F32)
    mid = rest.astype(BF16)
    return high, mid, (rest - mid.astype(F32)).astype(BF16)


def token_of(place):
    window, inner = place >> 6, place & 63
    row = (((window >> 1) << 3) + (inner >> 3) + WIN // 2) & 15
    col = (((window & 1) << 3) + (inner & 7) + WIN // 2) & 15
    return (row << 4) + col


def to_windows():
    return flag(iota((ROWS, ROWS), 1) == token_of(iota((ROWS, ROWS), 0)))


def from_windows():
    return flag(iota((ROWS, ROWS), 0) == token_of(iota((ROWS, ROWS), 1)))


def normalise(values):
    mean = jnp.mean(values, axis=-1, keepdims=True)
    centered = values - mean
    rstd = lax.rsqrt(jnp.mean(centered * centered, axis=-1, keepdims=True) + EPS)
    return centered * rstd, rstd


def norm_pull(unit, rstd, slope):
    return rstd * (
        slope - jnp.mean(slope, axis=-1, keepdims=True) - unit * jnp.mean(slope * unit, axis=-1, keepdims=True)
    )


def head_mask():
    return flag((iota((256, 128), 0) >> 6) == (iota((256, 128), 1) >> 5))


def by_head(ref, pair, first, mask):
    parts = []
    for side in (0, 1):
        rows = ref[pair * 128 + side * 64 : pair * 128 + side * 64 + 64, pl.ds(first, 128)]
        parts.append(jnp.concatenate([rows] * 4, axis=0) * mask)
    return jnp.concatenate(parts, axis=1)


def by_window(ref, pair, first, upper):
    rows = ref[pair * 128 : pair * 128 + 128, pl.ds(first, 128)]
    return jnp.concatenate([rows * upper, rows * (1 - upper)], axis=1)


def attend_phase(
    env, tokens_v, w_qkv_v, w_proj_v, tok_w, context, bias,
):
    (
        tokens, w_qkv, w_proj, rel_bias, gain, shift, tok_own, context_own, tok_2, context_2,
        qkv, probs, attn_out, mid, load_sem, c, small_wait, choices,
    ) = env
    load_tokens = pltpu.make_async_copy(tokens, tokens_v, load_sem.at[0])
    load_tokens.start()
    parts = [
        pltpu.make_async_copy(
            w_qkv.at[:, pl.ds(at * D, D)], w_qkv_v.at[:, pl.ds(at * D, D)], load_sem.at[1 + at]
        )
        for at in range(3)
    ]
    parts.append(pltpu.make_async_copy(w_proj, w_proj_v, load_sem.at[4]))
    for part in parts:
        part.start()
    def share(rows, own, others):
        halves = rows[...].T.reshape(16, 2, 32, ROWS)
        own[:, :, :ROWS] = jnp.where(c == 0, halves[:, 0], halves[:, 1])
        others[...] = jnp.where(c == 0, halves[:, 1], halves[:, 0])

    small_wait()
    choices()

    table = jnp.concatenate(split3(rel_bias[...]), axis=0)
    entry = iota((225, 128), 0)
    place = (iota((225, 128), 1) >> 3) * (2 * WIN - 1) + (iota((225, 128), 1) & 7) + WIN - 1
    low = iota((HEADS, 128), 1) < 64
    for key_col in range(WIN):
        found = dot(table, flag(entry == place - key_col))
        found = found[:32] + (found[32:64] + found[64:96])
        for key_row in range(WIN):
            first = (WIN - 1 - key_row) * WIN
            bias[pl.ds(key_row * WIN + key_col, HEADS, stride=64), :] = jnp.where(
                low, pltpu.roll(found, (128 - first) % 128, 1), pltpu.roll(found, 64 - first if first <= 64 else 192 - first, 1)
            )

    load_tokens.wait()
    tok_w[...] = dot(to_windows(), tokens_v[...]).astype(BF16)
    for at in range(6):
        cols = slice(at * 512, at * 512 + 512)
        if at % 2 == 0:
            parts[at // 2].wait()
        qkv[:ROWS, cols] = dot(tok_w[...], w_qkv_v[:, cols]).astype(BF16)
    share(tok_w, tok_2, tok_own)

    mask = head_mask()
    key = iota((256, 128), 0) & 63
    lane = iota((256, 128), 1)
    row_differs = ((key >> 5) ^ (lane >> 5)) & 1
    col_differs = ((key ^ lane) >> 2) & 1 & (lane >> 6)
    upper = flag(iota((128, 128), 0) < 64)
    for pair in range(2):
        apart = jnp.where((col_differs | (row_differs if pair else 0)) == 1, NEG, 0.0)
        for group in range(8):
            keys = by_head(qkv, pair, D + group * 128, mask)
            queries = by_window(qkv, pair, group * 128, upper)
            scores = dot_nt(keys, queries) * SCALE + bias[group * 256 : group * 256 + 256, :] + apart
            scores = scores.reshape(4, 64, 128)
            weights = jnp.exp(scores - jnp.max(scores, axis=1, keepdims=True))
            prob = (weights * (1.0 / jnp.sum(weights, axis=1, keepdims=True))).reshape(256, 128).astype(BF16)
            probs[pair, group] = prob
            both = dot_tn(prob, by_head(qkv, pair, 2 * D + group * 128, mask))
            for side in (0, 1):
                context[pair * 128 + side * 64 : pair * 128 + side * 64 + 64, group * 128 : group * 128 + 128] = both[
                    side * 64 : side * 64 + 64, side * 128 : side * 128 + 128
                ].astype(BF16)

    share(context, context_2, context_own)
    parts[3].wait()
    projected = dot(context[...], w_proj_v[...])
    attn_out[...] = projected
    unit, _ = normalise(projected)
    mid_w = (tok_w[...].astype(F32) + (unit * gain[...] + shift[...])).astype(BF16)
    mid[...] = dot(from_windows(), mid_w).astype(BF16)


def expert_of_row(shape, dim):
    row = iota(shape, dim)
    return jnp.where(row < EXPERTS * 16, row >> 4, (row >> 2) & (EXPERTS - 1))


def rank_of_row(shape, dim):
    row = iota(shape, dim)
    return jnp.where(row < EXPERTS * 16, row & 15, 16 + (row & 3))


def fold_order(count, back=False):
    row, col = iota((16 * count, 16 * count), int(back)), iota((16 * count, 16 * count), 1 - int(back))
    size = 4 * count
    block = sum([(row >= size * at).astype(jnp.int32) for at in (1, 2, 3)])
    inner = row - block * size
    return flag(col == ((inner >> 2) << 4) + (block << 2) + (inner & 3))


def unfold(ref, first, count, order, out, out_first):
    main = ref[first : first + count, :, :D].reshape(16 * count, D)
    rest = dot(order, ref[first : first + count, :, D:].reshape(16 * count, CHUNK - D)).astype(BF16)
    out[out_first : out_first + 16 * count, :] = main
    for block in range(4):
        out[out_first + 16 * count : out_first + 20 * count, block * 256 : block * 256 + 256] = rest[
            block * 4 * count : block * 4 * count + 4 * count
        ]


def fold(rows, count, order_back, ref, first):
    ref[first : first + count, :, :D] = rows[: 16 * count].astype(BF16).reshape(count, 16, D)
    rest = rows[16 * count :].astype(BF16)
    stacked = jnp.concatenate([rest[:, block * 256 : block * 256 + 256] for block in range(4)], axis=0)
    ref[first : first + count, :, D:] = dot(order_back, stacked).astype(BF16).reshape(count, 16, CHUNK - D)


def gelu_parts(values):
    z = jnp.abs(values) * 0.7071067811865476
    t = 1.0 / (1.0 + 0.3275911 * z)
    bell = jnp.exp(-z * z)
    poly = ((((1.061405429 * t - 1.453152027) * t + 1.421413741) * t - 0.284496736) * t + 0.254829592) * t
    tail = 0.5 * poly * bell
    phi = jnp.where(values >= 0, 1.0 - tail, tail)
    return values * phi, phi + values * bell * 0.3989422804014327


def routes(me, peer, send_sem, recv_sem):
    def to_expert(route, source, target, j):
        e = lax.rem(me + j, EXPERTS)
        return pltpu.make_async_remote_copy(
            src_ref=source.at[e], dst_ref=target.at[j], send_sem=send_sem.at[route, j], recv_sem=recv_sem.at[route, j],
            device_id=peer(e), device_id_type=MESH,
        )

    def to_source(route, source, target, j):
        return pltpu.make_async_remote_copy(
            src_ref=source.at[j], dst_ref=target.at[me], send_sem=send_sem.at[route, j], recv_sem=recv_sem.at[route, j],
            device_id=peer(lax.rem(me + EXPERTS - j, EXPERTS)), device_id_type=MESH,
        )

    def start_all(make, route, source, target, first, last):
        @pl.loop(max(first, 1), last)
        def _(j):
            make(route, source, target, j).start()

    def receive(make, route, source, target, first, last):
        @pl.loop(max(first, 1), last)
        def _(j):
            make(route, source, target, j).wait_recv()

    return to_expert, to_source, start_all, receive


def expert_sums(y, sets, send_dp, recv_dp):
    up, down, far = lax.rem(y + 1, 4), lax.rem(y + 3, 4), lax.rem(y + 2, 4)

    def copy(at, kind, side):
        grad, *targets = sets[at]
        half = grad.shape[1] // 2
        upwards = (side == 0) != (kind == 1)
        block = far if kind == 0 else up if upwards else down
        return pltpu.make_async_remote_copy(
            src_ref=grad.at[block, pl.ds(side * half, half)], dst_ref=targets[kind].at[side],
            send_sem=send_dp.at[at, kind, side], recv_sem=recv_dp.at[at, kind, side],
            device_id={"dp": up if upwards else down}, device_id_type=MESH,
        )

    def start(at, kind):
        for side in (0, 1):
            copy(at, kind, side).start()

    def add_into(grad, block, first, count, more):
        step = 64

        @pl.loop(0, count // step)
        def _(i):
            here = pl.ds(pl.multiple_of(i * step, step), step)
            mine = pl.ds(pl.multiple_of(first + i * step, step), step)
            total = grad[block, mine].astype(F32)
            for other, side in more:
                total = total + other[side, here].astype(F32)
            grad[block, mine] = total.astype(BF16)

    def pass_on(at):
        grad, far_in, near_in, done_in = sets[at]
        half = grad.shape[1] // 2
        for side, block in enumerate((up, down)):
            copy(at, 0, side).wait()
            add_into(grad, block, side * half, half, ((far_in, side),))
            copy(at, 2, side).start()

    def complete(at):
        grad, far_in, near_in, done_in = sets[at]
        half = grad.shape[1] // 2
        for side in (0, 1):
            copy(at, 1, side).wait()
            copy(at, 2, side).wait()
            add_into(grad, y, side * half, half, ((near_in, side), (done_in, side)))

    return start, pass_on, complete


def choices_of(ids):
    expert_row = iota((EXPERTS, ROWS), 0)
    return [jnp.where(ids[k : k + 1, :] == expert_row, 1.0, 0.0).T for k in range(2)]


def place_choices(ids, select, pick):
    chosen = choices_of(ids)
    earlier = flag(iota((ROWS, ROWS), 0) > iota((ROWS, ROWS), 1))
    rank = dot(earlier, (chosen[0] + chosen[1]).astype(BF16)) + 1.0
    places = [(one * rank).astype(BF16) for one in chosen]
    row_experts = flag(expert_of_row((EXPERTS * SLOTS, EXPERTS), 0) == iota((EXPERTS * SLOTS, EXPERTS), 1))
    row_ranks = rank_of_row((EXPERTS * SLOTS, ROWS), 0).astype(F32) + 1.0
    for k in range(2):
        select[:, k * ROWS : k * ROWS + ROWS] = flag(dot_nt(row_experts, places[k]) == row_ranks)
    lane_experts = flag(expert_of_row((EXPERTS * SLOTS, EXPERTS), 0) == iota((EXPERTS * SLOTS, EXPERTS), 1))
    lane_ranks = rank_of_row((ROWS, EXPERTS * SLOTS), 1).astype(F32) + 1.0
    for k in range(2):
        pick[:, k * EXPERTS * SLOTS : (k + 1) * EXPERTS * SLOTS] = flag(dot_nt(places[k], lane_experts) == lane_ranks)


def experts_phase(
    env, w_first, w_second, out1, out2, rows, d_rows, hidden, slope, cotangent,
):
    (
        mid, ids, select, pick, cot, w_router, gain, shift, w_in, w_out, block_out, in1, in2, in3, out4,
        g_first, g_second, d_direct, router_own, router_other, load_sem, send_sem, recv_sem,
        me, y, c, peer, barrier, start_core, core_send, sums_start,
    ) = env
    load_first = pltpu.make_async_copy(w_in, w_first, load_sem.at[0])
    load_second = pltpu.make_async_copy(w_out, w_second, load_sem.at[1])
    load_cot = pltpu.make_async_copy(cot, cotangent, load_sem.at[2])
    load_first.start()
    load_second.start()
    load_cot.start()
    to_expert, to_source, start_all, receive = routes(me, peer, send_sem, recv_sem)
    back = d_rows
    chosen = choices_of(ids)

    order = fold_order(EXPERTS)
    batch_order = {count: fold_order(count) for count in (8, 16)}
    order_back = fold_order(EXPERTS, back=True)
    batch_back = {count: fold_order(count, back=True) for count in (8, 16)}

    fold(dot(select[:, :ROWS] + select[:, ROWS:], mid[...]), EXPERTS, order_back, out1, 0)
    pl.semaphore_wait(barrier, EXPERTS + 2)
    start_core()
    start_all(to_expert, 0, out1, in1, 1, EXPERTS)
    in1[0] = out1[me]

    router = split3(w_router[...])
    logits = dot_nt(mid[...], router[0]) + (dot_nt(mid[...], router[1]) + dot_nt(mid[...], router[2]))
    gating = []
    for k in range(2):
        logit = jnp.sum(logits * chosen[k], axis=1, keepdims=True)
        gating.append(1.0 / (1.0 + jnp.exp(-logit)))
    load_first.wait()
    load_second.wait()

    for first, last in BATCHES:
        count = last - first
        here = slice(SLOTS * first, SLOTS * last)
        receive(to_expert, 0, out1, in1, first, last)
        unfold(in1, first, count, batch_order[count], rows, SLOTS * first)
        for at in range(8):
            cols = slice(at * 256, at * 256 + 256)
            value, value_slope = gelu_parts(dot(rows[here, :], w_first[:, cols]))
            hidden[here, cols] = value.astype(BF16)
            slope[here, cols] = value_slope.astype(BF16)
        fold(dot(hidden[here, :], w_second[...]), count, batch_back[count], out2, first)
        start_all(to_source, 1, out2, in2, first, last)
        if first == 0:
            in2[me] = out2[0]

    picks = [pick[:, k * EXPERTS * SLOTS : (k + 1) * EXPERTS * SLOTS] for k in range(2)]
    receive(to_source, 1, out2, in2, 1, EXPERTS)
    unfold(in2, 0, EXPERTS, order, back, 0)
    picked = [dot(picks[k], back[...]) for k in range(2)]
    unit, rstd = normalise(gating[0] * picked[0] + gating[1] * picked[1])
    load_cot.wait()
    d_mixture = norm_pull(unit, rstd, cotangent[...].astype(F32) * gain[...])
    d_picked = jnp.concatenate([(gating[k] * d_mixture).astype(BF16) for k in range(2)], axis=0)
    @pl.loop(1, EXPERTS)
    def _(j):
        to_expert(0, out1, in1, j).wait_send()

    fold(dot(select[...], d_picked), EXPERTS, order_back, out1, 0)
    start_all(to_expert, 2, out1, in3, 1, EXPERTS)
    in3[0] = out1[me]

    d_direct[...] = cotangent[...].astype(F32)
    cotangent[...] = (mid[...].astype(F32) + (unit * gain[...] + shift[...])).astype(BF16)
    write_block = pltpu.make_async_copy(cotangent, block_out, load_sem.at[3])
    write_block.start()

    d_logits = jnp.zeros((ROWS, EXPERTS), F32)
    for k in range(2):
        d_gating = jnp.sum(d_mixture * picked[k], axis=1, keepdims=True)
        d_logits = d_logits + chosen[k] * (d_gating * gating[k] * (1.0 - gating[k]))
    d_high = d_logits.astype(BF16)
    d_low = (d_logits - d_high.astype(F32)).astype(BF16)
    wide = [jnp.concatenate([part, jnp.zeros((ROWS, 128 - EXPERTS), BF16)], axis=1) for part in (d_high, d_low)]
    d_router = (dot_tn(mid[...], wide[0]) + dot_tn(mid[...], wide[1])).reshape(16, 2, 4, 8, 128)
    high = d_router.astype(BF16).astype(F32)
    router_own[...] = jnp.concatenate([high, d_router - high], axis=3).astype(BF16)
    core_send(lambda: (router_own.at[:, 1 - c], router_other), 2)
    from_router = dot(d_high, router[0]) + (dot(d_low, router[0]) + dot(d_high, router[1]))
    d_direct[...] += from_router

    far = lax.rem(y + 2, 4)

    def second_block(place):
        for at in range(2):
            cols = pl.ds(pl.multiple_of(place * 512 + at * 256, 256), 256)
            g_second[place, at * 256 : at * 256 + 256, :] = dot(hidden[:, cols].T, d_rows[...]).astype(BF16)

    def first_block(place):
        cols = pl.ds(pl.multiple_of(place * 256, 256), 256)
        g_first[place, :, :] = dot(rows[:, cols].T, slope[...]).astype(BF16)

    for first, last in BATCHES:
        count = last - first
        here = slice(SLOTS * first, SLOTS * last)
        receive(to_expert, 2, out1, in3, first, last)
        unfold(in3, first, count, batch_order[count], d_rows, SLOTS * first)
        if last == EXPERTS:
            second_block(far)
            sums_start(0, 0)
        for at in range(8):
            cols = slice(at * 256, at * 256 + 256)
            d_hidden = dot_nt(d_rows[here, :], w_second[cols, :])
            slope[here, cols] = (d_hidden * slope[here, cols].astype(F32)).astype(BF16)
        fold(dot_nt(slope[here, :], w_first[...]), count, batch_back[count], out4, first)
        start_all(to_source, 3, out4, in2, first, last)
        if first == 0:
            in2[me] = out4[0]

    second_block(lax.rem(y + 3, 4))
    second_block(lax.rem(y + 1, 4))
    sums_start(0, 1)
    first_block(far)
    sums_start(1, 0)
    first_block(lax.rem(y + 3, 4))
    first_block(lax.rem(y + 1, 4))
    sums_start(1, 1)
    second_block(y)
    first_block(y)

    @pl.loop(1, EXPERTS)
    def _(j):
        to_source(1, out2, in2, j).wait_send()
        to_expert(2, out1, in3, j).wait_send()

    write_block.wait()


def attend_back_groups(groups, qkv, probs, d_context, d_qkv):
    mask = head_mask()
    mask_f = mask.astype(F32)
    upper = flag(iota((128, 128), 0) < 64)

    def own_heads(values, side):
        return (values[:, side * 128 : side * 128 + 128] * mask_f).reshape(4, 64, 128).sum(axis=0)

    for group in groups:
        for pair in range(2):
            first = group * 128
            values = by_head(qkv, pair, 2 * D + first, mask)
            keys = by_head(qkv, pair, D + first, mask)
            queries = by_window(qkv, pair, first, upper)
            d_out = by_window(d_context, pair, first, upper)
            prob = probs[pair, group]
            d_prob = dot_nt(values, d_out)
            prob_f = prob.astype(F32)
            inner = (prob_f * d_prob).reshape(4, 64, 128).sum(axis=1, keepdims=True)
            d_score = prob_f.reshape(4, 64, 128) * (d_prob.reshape(4, 64, 128) - inner) * SCALE
            d_score = d_score.reshape(256, 128).astype(BF16)
            d_value = dot(prob, d_out)
            d_key = dot(d_score, queries)
            d_query = dot_tn(d_score, keys)
            for side in (0, 1):
                rows = slice(pair * 128 + side * 64, pair * 128 + side * 64 + 64)
                d_qkv[rows, first : first + 128] = d_query[
                    side * 64 : side * 64 + 64, side * 128 : side * 128 + 128
                ].astype(BF16)
                d_qkv[rows, D + first : D + first + 128] = own_heads(d_key, side).astype(BF16)
                d_qkv[rows, 2 * D + first : 2 * D + first + 128] = own_heads(d_value, side).astype(BF16)


def finish_phase(
    env, w_qkv, w_proj, d_context, back, d_tok_v, grad_x, grad_z, sum_x, sum_z, sum_y,
):
    (
        refs, qkv, probs, attn_out, gain_attn, d_tokens, out_qkv, out_proj, out_router, out_first, out_second,
        in2, out4, pick, d_direct, router_own, router_other, tok_2, context_2, d_qkv_2, d_attn_2,
        g_first, g_second, sums_pass, sums_complete, x_far, x_near, x_done, z_far, z_near, z_done, x_recv, z_recv, y_recv,
        load_sem, send_sem, recv_sem, send_one, recv_one, send_two, recv_two, send_y, recv_y,
        me, x, y, z, c, peer, core_send, core_wait,
    ) = env
    loads = [
        pltpu.make_async_copy(source, target, load_sem.at[2 + at])
        for at, (source, target) in enumerate(zip(refs, (w_proj, w_qkv)))
    ]
    for load in loads:
        load.start()
    to_expert, to_source, start_all, receive = routes(me, peer, send_sem, recv_sem)

    def at_x(j):
        return {"group": lax.rem(x + j, 4) * 2 + c}

    def at_y(j):
        return {"dp": lax.rem(y + j, 4)}

    def at_z(j):
        return {"node": lax.rem(z + j, 4)}

    def send(src, dst, s_sem, r_sem, target):
        copy = pltpu.make_async_remote_copy(
            src_ref=src, dst_ref=dst, send_sem=s_sem, recv_sem=r_sem, device_id=target, device_id_type=MESH
        )
        copy.start()
        return copy

    rings = (
        (grad_x, x_far, x_near, x_done, sum_x, x, at_x, X_COLS, 1),
        (grad_z, z_far, z_near, z_done, sum_z, z, at_z, Z_COLS, 2),
    )

    def block_of(ref, dim, half, place, cols):
        where = [pl.ds(2 * half, 2), slice(None), slice(None), slice(None), pl.ds(cols[0], cols[1] - cols[0])]
        where[dim] = place
        return ref.at[tuple(where)]

    def ring_start(part):
        copies = []
        for ring, (grad, far_in, near_in, done_in, total, own, at, cols, dim) in enumerate(rings):
            here = cols[part]
            span = pl.ds(here[0], here[1] - here[0])
            up, down, opposite = lax.rem(own + 1, 4), lax.rem(own + 3, 4), lax.rem(own + 2, 4)
            sems = lambda kind, side: (send_one.at[part, ring, kind, side], recv_one.at[part, ring, kind, side])
            copies.append((
                send(block_of(grad, dim, 0, opposite, here), far_in.at[0, :, :, :, span], *sems(0, 0), at(1)),
                send(block_of(grad, dim, 1, opposite, here), far_in.at[1, :, :, :, span], *sems(0, 1), at(3)),
                send(block_of(grad, dim, 0, down, here), near_in.at[0, :, :, :, span], *sems(1, 0), at(3)),
                send(block_of(grad, dim, 1, up, here), near_in.at[1, :, :, :, span], *sems(1, 1), at(1)),
            ))
        return copies

    def ring_pass(part, started):
        copies = []
        for ring, (grad, far_in, near_in, done_in, total, own, at, cols, dim) in enumerate(rings):
            here = cols[part]
            span = pl.ds(here[0], here[1] - here[0])
            for side, (place, hop) in enumerate(((lax.rem(own + 1, 4), 1), (lax.rem(own + 3, 4), 3))):
                started[ring][side].wait()

                @pl.loop(0, 8)
                def _(i):
                    yi, oi = i // 4, i % 4
                    index = (2 * side + yi, place, oi) if dim == 1 else (2 * side + yi, oi, place)
                    grad[(*index, slice(None), span)] = (
                        grad[(*index, slice(None), span)].astype(F32) + far_in[side, yi, oi, :, span].astype(F32)
                    ).astype(BF16)

                copies.append(send(
                    block_of(grad, dim, side, place, here), done_in.at[side, :, :, :, span],
                    send_one.at[part, ring, 2, side], recv_one.at[part, ring, 2, side], at(hop),
                ))
        return copies

    def ring_finish(part, started, passed):
        copies = []
        for ring, (grad, far_in, near_in, done_in, total, own, at, cols, dim) in enumerate(rings):
            span = pl.ds(cols[part][0], cols[part][1] - cols[part][0])
            for side in (0, 1):
                started[ring][2 + side].wait()
                passed[2 * ring + side].wait()

            @pl.loop(0, 16)
            def _(i):
                yi, oi = i // 4, i % 4
                side, inner = yi // 2, yi % 2
                index = (yi, own, oi) if dim == 1 else (yi, oi, own)
                total[yi, oi, :, span] = (
                    grad[(*index, slice(None), span)].astype(F32)
                    + near_in[side, inner, oi, :, span].astype(F32)
                    + done_in[side, inner, oi, :, span].astype(F32)
                ).astype(BF16)

            recv, place, hop = ((x_recv, z, at_z), (z_recv, x, at_x))[ring]
            copies += [
                send(
                    total.at[:, lax.rem(place + j, 4), :, span], recv.at[j - 1, :, :, span],
                    send_two.at[part, ring, j - 1], recv_two.at[part, ring, j - 1], hop(j),
                )
                for j in (1, 2, 3)
            ]
        return copies

    def folded(left_t, right, cols):
        parts = dot(left_t[...].reshape(512, 512), right[:, cols : cols + 512]).reshape(64, 8, 512)
        return jnp.concatenate([parts[:, :, :256], parts[:, :, 256:]], axis=1).astype(BF16).reshape(4, 4, 4, 16, 256)

    receive(to_source, 3, out4, in2, 1, EXPERTS)
    unfold(in2, 0, EXPERTS, fold_order(EXPERTS), back, 0)
    d_mid = (d_direct[...] + dot(pick[:, : EXPERTS * SLOTS] + pick[:, EXPERTS * SLOTS :], back[...])).astype(BF16)
    d_mid_w = dot(to_windows(), d_mid)
    d_direct[...] = d_mid_w
    unit, rstd = normalise(attn_out[...])
    d_attn_2[:ROWS, :] = norm_pull(unit, rstd, d_mid_w * gain_attn[...]).astype(BF16)
    core_send(lambda: (d_attn_2.at[pl.ds(0, ROWS)], d_attn_2.at[pl.ds(ROWS, ROWS)]), 3)
    loads[0].wait()
    d_context[...] = dot_nt(d_attn_2[:ROWS, :], w_proj[...]).astype(BF16)

    def core_send_heads(half):
        for at in range(3):
            cols = pl.ds(at * D + half * 512, 512)
            core_send(
                lambda cols=cols: (d_qkv_2.at[pl.ds(0, ROWS), cols], d_qkv_2.at[pl.ds(ROWS, ROWS), cols]),
                4 + 3 * half + at,
            )

    started, passed = [], []
    attend_back_groups(range(4), qkv, probs, d_context, d_qkv_2)
    core_send_heads(0)
    core_wait(1)
    core_wait(3)
    grad_x[..., 0:256] = folded(context_2, d_attn_2, 0)
    grad_z[..., 0:256] = folded(context_2, d_attn_2, 512)
    started.append(ring_start(0))
    sums_pass(0)
    attend_back_groups(range(4, 8), qkv, probs, d_context, d_qkv_2)
    core_send_heads(1)
    core_wait(0)
    for at in range(3):
        core_wait(4 + at)
    grad_x[..., 256:512] = folded(tok_2, d_qkv_2, 0)
    grad_z[..., 256:512] = folded(tok_2, d_qkv_2, D)
    grad_z[..., 512:768] = folded(tok_2, d_qkv_2, 2 * D)
    started.append(ring_start(1))
    passed.append(ring_pass(0, started[0]))
    core_wait(2)
    for at in range(3):
        core_wait(7 + at)
    grad_x[..., 512:768] = folded(tok_2, d_qkv_2, 512)
    grad_x[..., 768:1024] = folded(tok_2, d_qkv_2, D + 512)
    grad_z[..., 768:1024] = folded(tok_2, d_qkv_2, 2 * D + 512)
    grad_z[..., 1024:1152] = (
        (router_own[:, c].astype(F32) + router_other[...].astype(F32)).astype(BF16).reshape(4, 4, 4, 16, 128)
    )
    started.append(ring_start(2))
    passed.append(ring_pass(1, started[1]))
    second = ring_finish(0, started[0], passed[0])
    loads[1].wait()
    d_tok_w = (d_direct[...] + dot_nt(d_qkv_2[:ROWS, :], w_qkv[...])).astype(BF16)
    d_tok_v[...] = dot(from_windows(), d_tok_w).astype(BF16)
    write_tokens = pltpu.make_async_copy(d_tok_v, d_tokens, load_sem.at[4])
    write_tokens.start()
    sums_pass(1)
    passed.append(ring_pass(2, started[2]))
    second += ring_finish(1, started[1], passed[1])
    second += ring_finish(2, started[2], passed[2])
    for copy in second:
        copy.wait()

    @pl.loop(0, 4)
    def _(yi):
        total_x = sum_x[yi, z].astype(F32)
        total_z = sum_z[yi, x].astype(F32)
        for j in range(3):
            total_x = total_x + x_recv[j, yi].astype(F32)
            total_z = total_z + z_recv[j, yi].astype(F32)
        sum_y[yi, :, :1024] = total_x.astype(BF16)
        sum_y[yi, :, 1024:] = total_z.astype(BF16)

    third = [
        send(sum_y.at[lax.rem(y + j, 4)], y_recv.at[j - 1], send_y.at[j - 1], recv_y.at[j - 1], at_y(j))
        for j in (1, 2, 3)
    ]
    def complete(at):
        grad, out = ((g_second, out_second), (g_first, out_first))[at]
        sums_complete(at)
        write = pltpu.make_async_copy(grad.at[y], out, load_sem.at[7 + at])
        write.start()
        return write

    writes = [complete(0)]
    for copy in third:
        copy.wait()
    total = sum_y[y].astype(F32)
    for j in range(3):
        total = total + y_recv[j].astype(F32)

    def unfolded(first):
        return jnp.concatenate([total[:8, first : first + 256], total[8:, first : first + 256]], axis=1)

    out_proj[...] = jnp.concatenate([unfolded(0), unfolded(1024)], axis=1).astype(BF16)
    out_qkv[...] = jnp.concatenate(
        [unfolded(first) for first in (256, 512, 1280, 768, 1536, 1792)], axis=1
    ).astype(BF16)
    out_router[...] = total[:8, 2048:] + total[8:, 2048:]
    writes.append(complete(1))

    @pl.loop(1, EXPERTS)
    def _(j):
        to_source(3, out4, in2, j).wait_send()

    for write in writes + [write_tokens]:
        write.wait()


def main_kernel(
    tokens, w_qkv, w_proj, rel_bias_in, gain_attn_in, shift_attn_in, router_in, gain_moe_in, shift_moe_in, w_in, w_out, ids_in,
    cotangent,
    block_out, d_tokens, out_qkv, out_proj, out_router, out_first, out_second,
    rel_bias, gain_attn, shift_attn, w_router, gain, shift, ids, tok_own, context_own, probs, attn_out, mid, small_sem, select, pick,
    in1, in2, in3, out4, g_first, g_second, d_direct, router_own, router_other,
    tok_2, context_2, d_qkv_2, d_attn_2,
    f_far, f_near, f_done, s_far, s_near, s_done,
    x_far, x_near, x_done, z_far, z_near, z_done, x_recv, z_recv, y_recv,
    load_sem, send_sem, recv_sem, send_core, recv_core, send_one, recv_one, send_two, recv_two,
    send_y, recv_y, send_dp, recv_dp,
):
    y = lax.axis_index("dp")
    g = lax.axis_index("group")
    z = lax.axis_index("node")
    x = g // 2
    c = g % 2
    me = g * 4 + z
    other = {"group": x * 2 + (1 - c)}
    qkv = d_qkv_2

    def peer(e):
        return {"group": e // 4, "node": lax.rem(e, 4)}

    barrier = pltpu.get_barrier_semaphore()

    @pl.loop(1, EXPERTS)
    def _(j):
        pl.semaphore_signal(barrier, inc=1, device_id=peer(lax.rem(me + j, EXPERTS)), device_id_type=MESH)

    for j in (1, 2, 3):
        pl.semaphore_signal(barrier, inc=1, device_id={"dp": lax.rem(y + j, 4)}, device_id_type=MESH)

    sums_start, sums_pass, sums_complete = expert_sums(
        y, ((g_second, s_far, s_near, s_done), (g_first, f_far, f_near, f_done)), send_dp, recv_dp
    )

    def core_copy(src, dst, at):
        return pltpu.make_async_remote_copy(
            src_ref=src, dst_ref=dst, send_sem=send_core.at[at], recv_sem=recv_core.at[at],
            device_id=other, device_id_type=MESH,
        )

    core_ends = {}

    def core_send(ends, at):
        core_ends[at] = ends
        core_copy(*ends(), at).start()

    def core_wait(at):
        core_copy(*core_ends[at](), at).wait()

    theirs = pl.ds(ROWS, ROWS)

    def start_core():
        for at, (source, target) in enumerate(((tok_own, tok_2), (context_own, context_2))):
            core_send(lambda source=source, target=target: (source, target.at[:, :, theirs]), at)

    small = [
        pltpu.make_async_copy(source, target, small_sem.at[at])
        for at, (source, target) in enumerate((
            (rel_bias_in, rel_bias), (gain_attn_in, gain_attn), (shift_attn_in, shift_attn), (router_in, w_router),
            (gain_moe_in, gain), (shift_moe_in, shift), (ids_in, ids),
        ))
    ]
    for copy in small:
        copy.start()

    def small_wait():
        for copy in small:
            copy.wait()

    attend_env = (
        tokens, w_qkv, w_proj, rel_bias, gain_attn, shift_attn, tok_own, context_own, tok_2, context_2,
        qkv, probs, attn_out, mid, load_sem, c, small_wait, lambda: place_choices(ids, select, pick),
    )
    pl.run_scoped(
        lambda *scratch: attend_phase(attend_env, *scratch),
        pltpu.VMEM((ROWS, D), BF16), pltpu.VMEM((D, 3 * D), BF16), pltpu.VMEM((D, D), BF16),
        pltpu.VMEM((ROWS, D), BF16), pltpu.VMEM((ROWS, D), BF16), pltpu.VMEM((HEADS * 64, 128), F32),
    )
    first_env = (
        mid, ids, select, pick, cotangent, w_router, gain, shift, w_in, w_out, block_out, in1, in2, in3, out4,
        g_first, g_second, d_direct, router_own, router_other, load_sem, send_sem, recv_sem,
        me, y, c, peer, barrier, start_core, core_send, sums_start,
    )
    slots = EXPERTS * SLOTS
    box = pltpu.VMEM((EXPERTS, 16, CHUNK), BF16)
    pl.run_scoped(
        lambda *scratch: experts_phase(first_env, *scratch),
        pltpu.VMEM((D, FF), BF16), pltpu.VMEM((FF, D), BF16), box, box,
        pltpu.VMEM((slots, D), BF16), pltpu.VMEM((slots, D), BF16),
        pltpu.VMEM((slots, FF), BF16), pltpu.VMEM((slots, FF), BF16),
        pltpu.VMEM((ROWS, D), BF16),
    )
    last_env = (
        (w_proj, w_qkv), qkv, probs, attn_out,
        gain_attn, d_tokens, out_qkv, out_proj, out_router, out_first, out_second,
        in2, out4, pick, d_direct, router_own, router_other, tok_2, context_2, d_qkv_2, d_attn_2,
        g_first, g_second, sums_pass, sums_complete, x_far, x_near, x_done, z_far, z_near, z_done, x_recv, z_recv, y_recv,
        load_sem, send_sem, recv_sem, send_one, recv_one, send_two, recv_two, send_y, recv_y,
        me, x, y, z, c, peer, core_send, core_wait,
    )
    pl.run_scoped(
        lambda *scratch: finish_phase(last_env, *scratch),
        pltpu.VMEM((D, 3 * D), BF16), pltpu.VMEM((D, D), BF16), pltpu.VMEM((ROWS, D), BF16),
        pltpu.VMEM((slots, D), BF16), pltpu.VMEM((ROWS, D), BF16),
        pltpu.VMEM((4, 4, 4, 16, 1024), BF16), pltpu.VMEM((4, 4, 4, 16, 1152), BF16),
        pltpu.VMEM((4, 4, 16, 1024), BF16), pltpu.VMEM((4, 4, 16, 1152), BF16), pltpu.VMEM((4, 16, 2176), BF16),
    )


def main(
    tokens, w_qkv, w_proj, rel_bias, gain_attn, shift_attn, w_router, gain_moe, shift_moe, w_in, w_out, expert_ids, cotangent
):
    vmem = pl.BlockSpec(memory_space=pltpu.VMEM)
    anywhere = pl.BlockSpec(memory_space=pl.ANY)
    dma = pltpu.SemaphoreType.DMA
    slots = EXPERTS * SLOTS

    def hold(*shape):
        return pltpu.VMEM(shape, BF16)

    box = hold(EXPERTS, 16, CHUNK)
    return pl.pallas_call(
        main_kernel,
        out_shape=(
            jax.ShapeDtypeStruct((ROWS, D), BF16),
            jax.ShapeDtypeStruct((ROWS, D), BF16),
            jax.ShapeDtypeStruct((8, 3 * D), BF16),
            jax.ShapeDtypeStruct((8, D), BF16),
            jax.ShapeDtypeStruct((8, 128), F32),
            jax.ShapeDtypeStruct((D // 4, FF), BF16),
            jax.ShapeDtypeStruct((FF // 4, D), BF16),
        ),
        in_specs=[anywhere] * 13,
        out_specs=[anywhere] * 2 + [vmem] * 3 + [anywhere] * 2,
        scratch_shapes=[
            pltpu.VMEM((HEADS, 225), F32), pltpu.VMEM((1, D), F32), pltpu.VMEM((1, D), F32), pltpu.VMEM((EXPERTS, D), F32),
            pltpu.VMEM((1, D), F32), pltpu.VMEM((1, D), F32), pltpu.VMEM((2, ROWS), jnp.int32),
            hold(16, 32, ROWS), hold(16, 32, ROWS), hold(2, 8, 256, 128),
            pltpu.VMEM((ROWS, D), F32), hold(ROWS, D), dma((7,)),
            hold(slots, 2 * ROWS), hold(ROWS, 2 * slots),
            box, box, box, box,
            hold(4, D // 4, FF), hold(4, FF // 4, D), pltpu.VMEM((ROWS, D), F32),
            hold(16, 2, 4, 16, 128), hold(16, 4, 16, 128),
            hold(16, 32, 2 * ROWS), hold(16, 32, 2 * ROWS), hold(2 * ROWS, 3 * D), hold(2 * ROWS, D),
            *[hold(2, D // 8, FF)] * 3, *[hold(2, FF // 8, D)] * 3,
            *[hold(2, 2, 4, 16, 1024)] * 3, *[hold(2, 2, 4, 16, 1152)] * 3,
            hold(3, 4, 16, 1024), hold(3, 4, 16, 1152), hold(3, 16, 2176),
            dma((11,)), dma((4, EXPERTS)), dma((4, EXPERTS)), dma((10,)), dma((10,)),
            dma((3, 2, 3, 2)), dma((3, 2, 3, 2)), dma((3, 2, 3)), dma((3, 2, 3)), dma((3,)), dma((3,)),
            dma((2, 3, 2)), dma((2, 3, 2)),
        ],
        compiler_params=pltpu.CompilerParams(
            collective_id=0, has_side_effects=True, vmem_limit_bytes=62 * MIB
        ),
    )(
        tokens, w_qkv, w_proj, rel_bias, gain_attn.reshape(1, D), shift_attn.reshape(1, D), w_router.T,
        gain_moe.reshape(1, D), shift_moe.reshape(1, D), w_in, w_out, expert_ids.T, cotangent,
    )


def place_kernel(*refs):
    count = (len(refs) - 2) // 3
    sources, targets, held, (narrow, sems) = refs[:count], refs[count : 2 * count], refs[2 * count : 3 * count], refs[3 * count :]
    reads = [pltpu.make_async_copy(sources[at], held[at], sems.at[0, at]) for at in range(count)]
    for read in reads:
        read.start()
    writes = []
    for at in range(count):
        reads[at].wait()
        source = held[at]
        if at == count - 1:
            narrow[...] = held[at][:, :EXPERTS]
            source = narrow
        writes.append(pltpu.make_async_copy(source, targets[at], sems.at[1, at]))
        writes[at].start()
    for write in writes:
        write.wait()


def place(*values):
    anywhere = pl.BlockSpec(memory_space=pl.ANY)
    count = len(values)
    return pl.pallas_call(
        place_kernel,
        out_shape=tuple(jax.ShapeDtypeStruct(v.shape, v.dtype) for v in values[:-1]) + (jax.ShapeDtypeStruct((8, EXPERTS), F32),),
        in_specs=[anywhere] * count,
        out_specs=[anywhere] * count,
        scratch_shapes=[pltpu.VMEM(v.shape, v.dtype) for v in values]
        + [pltpu.VMEM((8, EXPERTS), F32), pltpu.SemaphoreType.DMA((2, count))],
        compiler_params=pltpu.CompilerParams(vmem_limit_bytes=62 * MIB),
    )(*values)


def per_device(
    tokens, w_qkv, w_proj, rel_bias, gain_attn, shift_attn, w_router, gain_moe, shift_moe, w_in, w_out, expert_ids, cotangent
):
    block_out, d_tokens, sum_qkv, sum_proj, sum_router, first_sum, second_sum = main(
        tokens, w_qkv, w_proj, rel_bias, gain_attn, shift_attn, w_router, gain_moe, shift_moe, w_in[0], w_out[0], expert_ids,
        cotangent,
    )
    block_out, d_tokens, sum_qkv, sum_proj, first_sum, second_sum, sum_router = place(
        block_out, d_tokens, sum_qkv, sum_proj, first_sum, second_sum, sum_router
    )
    return block_out, d_tokens, sum_qkv, sum_proj, sum_router, first_sum[None], second_sum[None]


def solution(mesh):
    split = P(("dp", "group", "node"), None)
    expert = P(("group", "node"), None, None)
    owned = P(("group", "node"), "dp", None)
    return jax.shard_map(
        per_device,
        mesh=mesh,
        in_specs=(split, P(), P(), P(), P(), P(), P(), P(), P(), expert, expert, split, split),
        out_specs=(split, split, split, split, split, owned, owned),
        check_vma=False,
    )
```
